32 devices in a mesh: branch: 2 (over core), dp: 8 (over z, x), tensor: 2 (over y).
Axes of the slice: x: 2, y: 2, z: 4, core: 2. Of those that a mesh axis runs over, the one named last changes fastest.
Arguments:
- crops: bfloat16 [2, 64, 256, 384], P('branch', 'dp'), may hold values from -6 to 6
- segment_ids: int32 [2, 64, 256], P(None, 'dp'), may hold values from 0 to 6, as said below
- cotangent: bfloat16 [64, 256, 384], P('dp'), may hold values from -6 to 6
- qkv_weight: float32 [2, 384, 3, 384], P('branch', 'dp', None, 'tensor'), may hold values from -0.4375 to 0.4375
- out_weight: float32 [2, 384, 384], P('branch', 'tensor', 'dp'), may hold values from -2 to 2
- up_weight: float32 [2, 384, 1536], P('branch', 'dp', 'tensor'), may hold values from -0.3125 to 0.3125
- down_weight: float32 [2, 1536, 384], P('branch', 'tensor', 'dp'), may hold values from -0.21875 to 0.21875
- gain_rows: float32 [2, 2, 384], P('branch', None, 'dp'), may hold values from 0.5 to 1.5
- biases: float32 [2, 4, 384], P('branch', None, 'dp'), may hold values from -1.8 to 1.8
Outputs:
- encoded: bfloat16 [2, 64, 256, 384], P('branch', 'dp')
- crop_grad: float32 [64, 256, 384], P('dp', None, 'branch')
- qkv_weight_grad: float32 [384, 3, 384], P(('branch', 'dp'), None, 'tensor')
- out_weight_grad: float32 [384, 384], P('tensor', ('branch', 'dp'))
- up_weight_grad: float32 [384, 1536], P(('branch', 'dp'), 'tensor')
- down_weight_grad: float32 [1536, 384], P('tensor', ('branch', 'dp'))
- gain_grad: float32 [2, 384], P(None, ('branch', 'dp'))
- bias_grad: float32 [4, 384], P(None, ('branch', 'dp'))
The draws below stay inside these ranges and needn't reach their ends.
Inputs may be any that keep to these rules, and one draw needn't show every extreme that they name: `segment_ids`: each sequence holds 6 crops of exactly 37 consecutive slots, numbered 1 to 6 in order; every other slot is padding with id 0, in gaps before, between and after the crops.
All inputs are finite; a program needn't handle non-finite values.
Results may differ from the reference program's by a relative error of at most 0.02.
Values may be sent and summed in bfloat16 or wider, within the bound.
No kernel may reach another device: no remote copies, remote signals or barrier semaphores. Data moves between devices by JAX's collectives and lax.ppermute only.
A program may use at most 128 MiB of HBM per device.

```python
import math
import jax
import jax.numpy as jnp
from jax import lax

D = 384
HEADS = 12
HD = 32
FF = 1536
L = 256
CROP = 37
CROPS_SEQ = 6
SEQS = 64
N_TENSOR = 2


def draw_segment_ids(key, part):
    key = jax.random.fold_in(key, 7)
    pad_slots = L - CROPS_SEQ * CROP
    gap_cuts = jnp.sort(jax.random.randint(key, (2, SEQS, CROPS_SEQ), 0, pad_slots + 1), axis=-1)
    starts = gap_cuts + jnp.arange(CROPS_SEQ, dtype=jnp.int32) * CROP
    positions = jnp.arange(L, dtype=jnp.int32)
    inside = (positions[None, None, None, :] >= starts[..., None]) & (positions[None, None, None, :] < starts[..., None] + CROP)
    labels = jnp.arange(1, CROPS_SEQ + 1, dtype=jnp.int32)
    return jnp.sum(jnp.where(inside, labels[None, None, :, None], 0), axis=2).astype(jnp.int32)


def block_levels(key, shape, shards, low, high):
    factor_of = 1.0
    for position, shards_of in shards:
        steps = jax.random.uniform(jax.random.fold_in(jax.random.fold_in(key, 6), position), (shards_of,), jnp.float32, low / len(shards), high / len(shards))
        factor_of = factor_of * jnp.repeat(jnp.exp(steps), shape[position] // shards_of).reshape((-1,) + (1,) * (len(shape) - 1 - position))
    return factor_of


def noise(stream_key, shape, deviation, reach, shards=(), held_as=jnp.bfloat16):
    result = jax.random.normal(stream_key, shape, jnp.float32) * deviation
    if len(shards) > 0:
        result = block_levels(stream_key, shape, shards, -0.22, 0.18) * result
    return jnp.clip(result, min=-reach, max=reach).astype(held_as)


def setup_inputs(seed: int = 0) -> dict:
    streams_of = jax.random.split(jax.random.key(seed), 10)
    crops = noise(streams_of[0], (2, SEQS, L, D), 1.0, 6.0, ((0, 2), (1, 8)))
    segment_ids = draw_segment_ids(jax.random.fold_in(streams_of[9], 71), 0)
    cotangent = noise(streams_of[2], (SEQS, L, D), 1.0, 6.0, ((0, 8),))
    qkv_weight = noise(streams_of[3], (2, D, 3, D), (D // 2) ** -0.5, 0.4375, ((0, 2), (1, 8), (3, 2)), jnp.float32)
    out_weight = noise(streams_of[4], (2, D, D), (D // CROP) ** -0.5, 2.0, ((0, 2), (1, 2), (2, 8)), jnp.float32)
    up_weight = noise(streams_of[5], (2, D, FF), D ** -0.5, 0.3125, ((0, 2), (1, 8), (2, 2)), jnp.float32)
    down_weight = noise(streams_of[6], (2, FF, D), (FF // 2) ** -0.5, 0.21875, ((0, 2), (1, 2), (2, 8)), jnp.float32)
    gain_rows = jnp.clip(1.0 + 0.1 * jax.random.normal(streams_of[7], (2, 2, D), jnp.float32), 0.5, 1.5)
    biases = noise(streams_of[8], (2, 4, D), 0.3, 1.8, ((0, 2), (2, 8)), jnp.float32)
    return dict(crops=crops, segment_ids=segment_ids, cotangent=cotangent, qkv_weight=qkv_weight, out_weight=out_weight, up_weight=up_weight, down_weight=down_weight, gain_rows=gain_rows, biases=biases)


@jax.custom_vjp
def low(v):
    return lax.optimization_barrier(v.astype(jnp.bfloat16)).astype(jnp.float32)

@jax.custom_vjp
def low_back(v):
    return v

def low_keep(v):
    return (low(v), None)

def low_pass(kept, grad):
    return (grad,)

def back_keep(v):
    return (v, None)

def back_low(kept, grad):
    return (low(grad),)
low.defvjp(low_keep, low_pass)
low_back.defvjp(back_keep, back_low)
EPSILON = 1e-06
MASKED_SCORE = -1e+30

def matmul(left, right):
    return jnp.dot(left, right, precision=lax.Precision.HIGHEST, preferred_element_type=jnp.float32)

def layer_norm(values, gain_row, bias_row):
    centred = values - lax.optimization_barrier(jnp.mean(values, axis=-1, keepdims=True))
    spread = lax.optimization_barrier(jnp.mean(centred * centred, axis=-1, keepdims=True))
    return centred * lax.rsqrt(spread + EPSILON) * gain_row + bias_row

def encode(params, inputs, seg_block):
    qkv_full, out_full, up_full, down_full, gain_full, bias_full = params
    block_seqs = inputs.shape[0]
    flat_rows = inputs.reshape(block_seqs * L, D)
    head_width = D // N_TENSOR
    unit_width = FF // N_TENSOR
    local_heads = HEADS // N_TENSOR
    same_doc = (seg_block[:, :, None] == seg_block[:, None, :])[:, None]
    normed = low(layer_norm(flat_rows, gain_full[0], bias_full[0]))
    attn_total = jnp.zeros_like(flat_rows)
    for group in range(N_TENSOR):
        lower_col = group * head_width
        normed_part = low_back(normed)
        projected = jnp.einsum('nd,dce->nce', normed_part, qkv_full[:, :, lower_col:lower_col + head_width], precision=lax.Precision.HIGHEST)
        projected = low_back(low(projected))
        queries = projected[:, 0].reshape(block_seqs, L, local_heads, HD)
        keys_part = projected[:, 1].reshape(block_seqs, L, local_heads, HD)
        values_part = projected[:, 2].reshape(block_seqs, L, local_heads, HD)
        scores = jnp.einsum('bqhe,bkhe->bhqk', queries, keys_part, precision=lax.Precision.HIGHEST) * HD ** (-0.5)
        scores = low_back(scores)
        scores = jnp.where(same_doc, scores, MASKED_SCORE)
        row_max = lax.optimization_barrier(jnp.max(scores, axis=-1, keepdims=True))
        weights = jnp.exp(scores - row_max)
        probs = weights / lax.optimization_barrier(jnp.sum(weights, axis=-1, keepdims=True))
        probs_low = low(probs)
        context = jnp.einsum('bhqk,bkhe->bqhe', probs_low, values_part, precision=lax.Precision.HIGHEST)
        context = low_back(low(context.reshape(block_seqs * L, head_width)))
        attn_total = attn_total + low(matmul(context, out_full[lower_col:lower_col + head_width, :]))
    residual = flat_rows + low_back(attn_total) + bias_full[1]
    normed_two = low(layer_norm(residual, gain_full[1], bias_full[2]))
    mlp_total = jnp.zeros_like(flat_rows)
    for group in range(N_TENSOR):
        lower_unit = group * unit_width
        pre_act = low_back(matmul(low_back(normed_two), up_full[:, lower_unit:lower_unit + unit_width]))
        hidden = low(jax.nn.gelu(pre_act, approximate=False))
        mlp_total = mlp_total + low(matmul(hidden, down_full[lower_unit:lower_unit + unit_width, :]))
    output = residual + mlp_total + bias_full[3]
    return low(output).reshape(block_seqs, L, D)

def encode_all(params, inputs, seg_all):
    rounded = tuple((low(member) for member in params))
    block_seqs = math.gcd(SEQS, 16)
    block_count = SEQS // block_seqs

    def step(carried, pair):
        return (carried, encode(rounded, pair[0], pair[1]))
    carried, outputs = lax.scan(jax.checkpoint(step), jnp.zeros((), jnp.float32), (inputs.reshape(block_count, block_seqs, L, D), seg_all.reshape(block_count, block_seqs, L)))
    return outputs.reshape(SEQS, L, D)

def reference(crops, segment_ids, cotangent, qkv_weight, out_weight, up_weight, down_weight, gain_rows, biases):
    masters = (qkv_weight, out_weight, up_weight, down_weight, gain_rows, biases)
    query_masters = tuple((member[0].astype(jnp.float32) for member in masters))
    momentum_masters = tuple((member[1].astype(jnp.float32) for member in masters))
    query_ids = segment_ids[1]

    def query_run(params, inputs):
        return encode_all(params, inputs, query_ids)
    query_out, pullback = jax.vjp(query_run, query_masters, crops[1].astype(jnp.float32))
    weight_grads, crop_grad = pullback(cotangent.astype(jnp.float32))
    momentum_out = encode_all(momentum_masters, crops[0].astype(jnp.float32), segment_ids[0])
    encoded = jnp.stack([momentum_out, query_out]).astype(jnp.bfloat16)
    return (encoded, crop_grad, weight_grads[0], weight_grads[1], weight_grads[2], weight_grads[3], weight_grads[4], weight_grads[5])
```

```python
import functools
import math

import jax
import jax.numpy as jnp
from jax import lax
from jax.experimental import pallas as pl
from jax.experimental.pallas import tpu as pltpu
from jax.sharding import PartitionSpec as P

HD = 32
EPSILON = 1e-06
MASKED_SCORE = -1e30
LOG2E = 1.4426950408889634
BF16 = jnp.bfloat16
F32 = jnp.float32
VMEM_LIMIT = 48 * 1024 * 1024


def nn(left, right):
    return lax.dot_general(left, right, (((1,), (0,)), ((), ())), preferred_element_type=F32)


def nt(left, right):
    return lax.dot_general(left, right, (((1,), (1,)), ((), ())), preferred_element_type=F32)


def tn(left, right):
    return lax.dot_general(left, right, (((0,), (0,)), ((), ())), preferred_element_type=F32)


def gelu_parts(v):
    a = jnp.abs(v)
    t = 1.0 / (1.0 + (0.3275911 / math.sqrt(2.0)) * a)
    bell = jnp.exp2(v * v * (-0.5 * LOG2E))
    poly = t * (
        0.5 * 0.254829592
        + t * (0.5 * -0.284496736 + t * (0.5 * 1.421413741 + t * (0.5 * -1.453152027 + t * (0.5 * 1.061405429))))
    )
    tail = poly * bell
    return jnp.where(v < 0, tail, 1.0 - tail), bell


def norm_cols(values, gain, shift):
    centred = values - jnp.mean(values, axis=0, keepdims=True)
    spread = jnp.mean(centred * centred, axis=0, keepdims=True)
    rstd = lax.rsqrt(spread + EPSILON)
    hat = centred * rstd
    return hat, rstd, hat * gain + shift


def norm_cols_back(upstream, hat, rstd, gain):
    t = upstream * gain
    return rstd * (t - jnp.mean(t, axis=0, keepdims=True) - hat * jnp.mean(t * hat, axis=0, keepdims=True))


def columns_of(vec_ref, scratch):
    scratch[...] = jnp.zeros_like(scratch)
    scratch[0:8, :] = vec_ref[...]
    return scratch[...].T


def attend(x_ref, seg_ref, w1_ref, cols, q_ref, k_ref, v_ref, bias_ref, ctx_ref, pb_ref, inv_ref):
    tensors, width = w1_ref.shape[1], w1_ref.shape[2]
    group = width // tensors
    heads_g = group // HD
    nseq, slots = seg_ref.shape
    x_t = x_ref[...].astype(F32).T
    hat, rstd, normed = norm_cols(x_t, cols[:, 0:1], cols[:, 2:3])
    normed_low = normed.astype(BF16)
    rows = x_t.shape[1]
    for t in range(tensors):
        qk = tn(w1_ref[0, t], normed_low).astype(BF16)
        q_ref[t * heads_g : (t + 1) * heads_g] = qk[:group].reshape(heads_g, HD, rows)
        k_ref[t * heads_g : (t + 1) * heads_g] = qk[group:].reshape(heads_g, HD, rows)
        vo = tn(w1_ref[1, t], normed_low).astype(BF16)
        v_ref[t * heads_g : (t + 1) * heads_g, 0:HD] = vo[:group].reshape(heads_g, HD, rows)
    v_ref[:, HD:, :] = jnp.ones((v_ref.shape[0], v_ref.shape[1] - HD, rows), BF16)
    for s in range(nseq):
        across = jnp.broadcast_to(seg_ref[s : s + 1, :].astype(F32), (slots, slots))
        bias_ref[s] = jnp.where(across == across.T, 0.0, MASKED_SCORE)
    heads = tensors * heads_g

    def one_head(h, carry):
        for s in range(nseq):
            part = slice(s * slots, (s + 1) * slots)
            scores = tn(k_ref[h, :, part], q_ref[h, :, part]) + bias_ref[s]
            top = jnp.max(scores, axis=0, keepdims=True)
            weights = jnp.exp2((scores - top) * (HD**-0.5 * LOG2E)).astype(BF16)
            if pb_ref is not None:
                pb_ref[h, s] = weights
            both = nn(v_ref[h, :, part], weights)
            inv = 1.0 / both[HD : HD + 1]
            if inv_ref is not None:
                inv_ref[h, :, part] = jnp.broadcast_to(inv, (8, slots))
            ctx_ref[h // heads_g, heads_g + h % heads_g, :, part] = (both[:HD] * inv).astype(BF16)
        return carry

    ctx_ref[:, :heads_g] = jnp.zeros((tensors, heads_g, HD, rows), BF16)
    lax.fori_loop(0, heads, one_head, 0)
    attn = sum(nn(w1_ref[1, t], ctx_ref[t].reshape(width, rows)) for t in range(tensors))
    return x_t, hat, rstd, normed_low, attn


def query_attn_kernel(
    x_ref, seg_ref, w1_ref, vec_ref,
    res_ref, hat_ref, rstd_ref, normed_ref, q_ref, k_ref, v_ref, pb_ref, inv_ref, ctx_ref, cols_ref,
    bias_ref, vec_pad,
):
    cols = columns_of(vec_ref, vec_pad)
    cols_ref[...] = cols
    x_t, hat, rstd, normed, attn = attend(
        x_ref, seg_ref, w1_ref, cols, q_ref, k_ref, v_ref, bias_ref, ctx_ref, pb_ref, inv_ref
    )
    hat_ref[...] = hat
    rstd_ref[...] = jnp.broadcast_to(rstd, rstd_ref.shape)
    normed_ref[...] = normed
    res_ref[...] = x_t + attn + cols[:, 3:4]


def momentum_kernel(
    x_ref, seg_ref, w1_ref, w2_ref, vec_ref, out_ref, q_ref, k_ref, v_ref, ctx_ref, bias_ref, vec_pad, acc_ref
):
    cols = columns_of(vec_ref, vec_pad)
    x_t, _, _, _, attn = attend(x_ref, seg_ref, w1_ref, cols, q_ref, k_ref, v_ref, bias_ref, ctx_ref, None, None)
    res = x_t + attn + cols[:, 3:4]
    _, _, normed = norm_cols(res, cols[:, 1:2], cols[:, 4:5])
    rows_low = normed.T.astype(BF16)
    acc_ref[...] = res + cols[:, 5:6]
    tensors, units = w2_ref.shape[1], w2_ref.shape[3]
    chunk = 256
    parts = units // chunk

    def step(i, carry):
        t, c = i // parts, pl.ds(pl.multiple_of((i % parts) * chunk, chunk), chunk)
        pre = nn(rows_low, w2_ref[0, t, :, c])
        half, _ = gelu_parts(pre)
        acc_ref[...] += nt(w2_ref[1, t, :, c], (pre * half).astype(BF16))
        return carry

    lax.fori_loop(0, tensors * parts, step, 0)
    out_ref[...] = acc_ref[...].T.astype(BF16)


def query_mlp_kernel(
    b_ref, res_ref, cot_ref, w2_ref, cols_ref,
    out_ref, keep_ref, send_ref, dres_ref, vgrad_ref,
    acc_ref, dn_ref, n2t_ref, gt_ref,
):
    b = b_ref[0]
    cols = cols_ref[...]
    res = res_ref[...]
    hat, rstd, normed = norm_cols(res, cols[:, 1:2], cols[:, 4:5])
    n2t_ref[...] = normed.astype(BF16)
    rows_low = normed.T.astype(BF16)
    cot = cot_ref[...]
    cot_t = cot.astype(F32).T
    gt_ref[...] = cot_t.astype(BF16)
    acc_ref[...] = res + cols[:, 5:6]
    dn_ref[...] = jnp.zeros_like(dn_ref)
    tensors, width, units = w2_ref.shape[1], w2_ref.shape[2], w2_ref.shape[3]
    chunk = 256
    parts = units // chunk
    half_rows = width // 2

    def step(i, carry):
        t, off = i // parts, pl.multiple_of((i % parts) * chunk, chunk)
        c = pl.ds(off, chunk)
        up, down = w2_ref[0, t, :, c], w2_ref[1, t, :, c]
        pre = nn(rows_low, up)
        d_hidden = nn(cot, down)
        half, bell = gelu_parts(pre)
        hidden = (pre * half).astype(BF16)
        d_pre = (d_hidden * (half + pre * bell * (1.0 / math.sqrt(2.0 * math.pi)))).astype(BF16)
        acc_ref[...] += nt(down, hidden)
        dn_ref[...] += nt(up, d_pre)
        for ref, which in ((keep_ref, b), (send_ref, 1 - b)):
            rows = pl.ds(pl.multiple_of(which * half_rows, 16), half_rows)
            ref[t, :, c] = nn(n2t_ref[rows, :], d_pre).astype(BF16)
            ref[t, :, pl.ds(pl.multiple_of(units + off, chunk), chunk)] = nn(gt_ref[rows, :], hidden).astype(BF16)
        return carry

    lax.fori_loop(0, tensors * parts, step, 0)
    out_ref[...] = acc_ref[...].T.astype(BF16)
    d_n2 = dn_ref[...]
    d_res = cot_t + norm_cols_back(d_n2, hat, rstd, cols[:, 1:2])
    dres_ref[...] = d_res
    lane = lax.broadcasted_iota(jnp.int32, vgrad_ref.shape, 1)
    total = jnp.zeros(vgrad_ref.shape, F32)
    for j, term in ((1, d_n2 * hat), (3, d_res), (4, d_n2), (5, cot_t)):
        total = total + jnp.where(lane == 64 + j, jnp.sum(term, axis=1, keepdims=True), 0.0)
    vgrad_ref[...] = total


def query_back_kernel(
    b_ref, dres_ref, hat_ref, rstd_ref, normed_ref, q_ref, k_ref, v_ref, pb_ref, inv_ref, ctx_ref, cols_ref, w1_ref,
    vgrad_ref,
    crop_keep_ref, crop_send_ref, keep_ref, send_ref,
    dctx_ref, dproj_ref, dattn_ref, vg_ref, crop_ref,
):
    b = b_ref[0]
    tensors, width = w1_ref.shape[1], w1_ref.shape[2]
    group = width // tensors
    heads_g = group // HD
    heads, nseq, slots = pb_ref.shape[0], pb_ref.shape[1], pb_ref.shape[2]
    rows = nseq * slots
    d_attn = dres_ref[...].astype(BF16)
    dattn_ref[...] = d_attn
    for t in range(tensors):
        vo = tn(w1_ref[1, t], d_attn).astype(BF16)
        dctx_ref[t * heads_g : (t + 1) * heads_g] = vo[group:].reshape(heads_g, HD, rows)
    dproj_ref[:, 3 * heads_g :] = jnp.zeros((tensors, heads_g, HD, rows), BF16)

    def one_head(h, carry):
        t, hh = h // heads_g, h % heads_g
        for s in range(nseq):
            part = slice(s * slots, (s + 1) * slots)
            low_ctx = dctx_ref[h, :, part].astype(F32) * inv_ref[h, 0:1, part]
            delta = jnp.sum(low_ctx * ctx_ref[t, heads_g + hh, :, part].astype(F32), axis=0, keepdims=True)
            low_ctx = low_ctx.astype(BF16)
            weights = pb_ref[h, s]
            d_probs = tn(v_ref[h, 0:HD, part], low_ctx)
            d_scores = (weights.astype(F32) * (d_probs - delta)).astype(BF16)
            scale = HD**-0.5
            dproj_ref[t, hh, :, part] = (nn(k_ref[h, :, part], d_scores) * scale).astype(BF16)
            dproj_ref[t, heads_g + hh, :, part] = (nt(q_ref[h, :, part], d_scores) * scale).astype(BF16)
            dproj_ref[t, 2 * heads_g + hh, :, part] = nt(low_ctx, weights).astype(BF16)
        return carry

    lax.fori_loop(0, heads, one_head, 0)
    d_normed = jnp.zeros((width, rows), F32)
    for t in range(tensors):
        d_t = dproj_ref[t].reshape(4 * group, rows)
        d_normed += nn(w1_ref[0, t], d_t[: 2 * group]) + nn(w1_ref[1, t], d_t[2 * group :])
    hat = hat_ref[...]
    cols = cols_ref[...]
    crop_ref[...] = dres_ref[...] + norm_cols_back(d_normed, hat, rstd_ref[0:1, :], cols[:, 0:1])
    lane = lax.broadcasted_iota(jnp.int32, vgrad_ref.shape, 1)
    total = vgrad_ref[...]
    for j, term in ((0, d_normed * hat), (2, d_normed)):
        total = total + jnp.where(lane == 64 + j, jnp.sum(term, axis=1, keepdims=True), 0.0)
    vg_ref[...] = total
    half_rows = width // 2
    for ref, which in ((keep_ref, b), (send_ref, 1 - b)):
        part = pl.ds(pl.multiple_of(which * half_rows, 16), half_rows)
        left, right = normed_ref[part, :], dattn_ref[part, :]
        for t in range(tensors):
            d_t = dproj_ref[t].reshape(4 * group, rows)
            grads = nt(left, d_t[: 3 * group + 64])
            tile = (3 * group) // 128 * 128
            ref[t, :, 0:tile] = grads[:, :tile].astype(BF16)
            ref[t, :, tile : tile + 128] = (grads[:, tile : tile + 128] + vg_ref[part, :]).astype(BF16)
            ref[t, :, tile + 128 : tile + 128 + group] = nt(
                right, ctx_ref[t, heads_g:].reshape(group, rows)
            ).astype(BF16)
            ref[t, :, tile + 128 + group :] = jnp.zeros((half_rows, 64), BF16)
    mine = crop_ref[pl.ds(pl.multiple_of(b * half_rows, 16), half_rows), :]
    other = crop_ref[pl.ds(pl.multiple_of((1 - b) * half_rows, 16), half_rows), :]
    crop_keep_ref[...] = mine.T
    crop_send_ref[...] = other.T.astype(BF16)


def call(kernel, out_shapes, scratch, args, smem=0, flops=0, nbytes=0, trans=0):
    vmem = pl.BlockSpec(memory_space=pltpu.VMEM)
    return pl.pallas_call(
        kernel,
        out_shape=[jax.ShapeDtypeStruct(s, d) for s, d in out_shapes],
        in_specs=[pl.BlockSpec(memory_space=pltpu.SMEM)] * smem + [vmem] * (len(args) - smem),
        out_specs=[vmem] * len(out_shapes),
        scratch_shapes=[pltpu.VMEM(s, d) for s, d in scratch],
        compiler_params=pltpu.CompilerParams(vmem_limit_bytes=VMEM_LIMIT),
        cost_estimate=pl.CostEstimate(flops=flops, bytes_accessed=nbytes, transcendentals=trans),
    )(*args)


SPAN = ("dp", "tensor")


def swap_cores(block):
    return lax.ppermute(block, "branch", [(0, 1), (1, 0)])


def exchange(block, dp_mask, t_mask):
    dp, tensors = lax.axis_size("dp"), lax.axis_size("tensor")
    pairs = [
        (i * tensors + t, (i ^ dp_mask) * tensors + (t ^ t_mask)) for i in range(dp) for t in range(tensors)
    ]
    return lax.ppermute(block, SPAN, pairs)


def after(value, *deps):
    return lax.optimization_barrier((value, *deps))[0]


def dp_groups():
    bits = lax.axis_size("dp").bit_length() - 1
    groups, high = [], bits
    while high >= 2:
        high -= 2
        groups.append((high, 4))
    last = (0, 2) if high == 1 else None
    return groups, last


def put(whole, block, index):
    return lax.dynamic_update_slice(whole, block, index)


def gather(block):
    groups, last = dp_groups()
    me, t = lax.axis_index("dp"), lax.axis_index("tensor")
    tensors = lax.axis_size("tensor")
    for number, (shift, size) in enumerate(groups):
        lead, tail = block.shape[:number], block.shape[number:]
        whole = jnp.zeros(lead + (size,) + tail, block.dtype)
        mine = (me >> shift) & (size - 1)
        pieces = [(0, block)] + [(k, exchange(block, k << shift, 0)) for k in range(1, size)]
        for k, piece in pieces:
            whole = put(whole, jnp.expand_dims(piece, number), (0,) * number + (mine ^ k,) + (0,) * len(tail))
        block = whole
    lead, tail = block.shape[: len(groups)], block.shape[len(groups) :]
    size = last[1] if last else 1
    mine = me & (size - 1)
    whole = jnp.zeros((tensors,) + lead + (size,) + tail, block.dtype)
    for k in range(size):
        for u in range(tensors):
            piece = block if k == u == 0 else exchange(block, k, u)
            piece = jnp.expand_dims(jnp.expand_dims(piece, len(lead)), 0)
            whole = put(whole, piece, (t ^ u,) + (0,) * len(lead) + (mine ^ k,) + (0,) * len(tail))
    return whole.reshape((tensors, lax.axis_size("dp")) + tail)


def scatter_sum(block):
    groups, last = dp_groups()
    me, t = lax.axis_index("dp"), lax.axis_index("tensor")
    tensors = lax.axis_size("tensor")
    tail = block.shape[2:]
    size = last[1] if last else 1
    lead = tuple(g[1] for g in groups)
    block = block.reshape((tensors,) + lead + (size,) + tail)
    mine = me & (size - 1)

    def take(k, u):
        start = (t ^ u,) + (0,) * len(lead) + (mine ^ k,) + (0,) * len(tail)
        piece = lax.dynamic_slice(block, start, (1,) + lead + (1,) + tail)
        return piece.reshape(lead + tail)

    total = take(0, 0).astype(F32)
    for k in range(size):
        for u in range(tensors):
            if k or u:
                total = total + exchange(take(k, u), k, u).astype(F32)
    for number in reversed(range(len(groups))):
        shift, size = groups[number]
        mine = (me >> shift) & (size - 1)
        low = total.astype(BF16)

        def part(k, whole=low, number=number, mine=mine):
            return lax.dynamic_index_in_dim(whole, mine ^ k, number, keepdims=False)

        total = part(0, total).astype(F32)
        for k in range(1, size):
            total = total + exchange(part(k), k << shift, 0).astype(F32)
    return total


def on_device(
    crops, segment_ids, cotangent, qkv_weight, out_weight, up_weight, down_weight, gain_rows, biases
):
    branch, me, t = lax.axis_index("branch"), lax.axis_index("dp"), lax.axis_index("tensor")
    dp, tensors = lax.axis_size("dp"), lax.axis_size("tensor")
    on_query = branch == 0
    _, sequences, slots, width = crops.shape
    nseq = sequences // (2 * tensors)
    rows = nseq * slots
    shard = qkv_weight.shape[1]
    group = out_weight.shape[1]
    units = up_weight.shape[2]
    heads = tensors * group // HD
    heads_g = group // HD

    qkv = qkv_weight[0].astype(BF16)
    small = jnp.concatenate([gain_rows[0], biases[0]], axis=0).astype(BF16)
    vec_rows = put(jnp.zeros((8, width), BF16), small, (0, me * shard))
    half_0 = jnp.concatenate([jnp.concatenate([qkv[:, 0], qkv[:, 1]], axis=1), vec_rows], axis=0)
    half_1 = jnp.concatenate(
        [jnp.concatenate([qkv[:, 2], out_weight[0].T.astype(BF16)], axis=1), vec_rows], axis=0
    )
    mlp_0, mlp_1 = up_weight[0].astype(BF16), down_weight[0].T.astype(BF16)
    keep_1, send_1 = jnp.where(on_query, half_0, half_1), jnp.where(on_query, half_1, half_0)
    keep_2, send_2 = jnp.where(on_query, mlp_0, mlp_1), jnp.where(on_query, mlp_1, mlp_0)
    got_1 = swap_cores(send_1)
    got_2 = swap_cores(send_2)
    q_1, m_1 = jnp.where(on_query, keep_1, got_1), jnp.where(on_query, got_1, keep_1)
    q_2, m_2 = jnp.where(on_query, keep_2, got_2), jnp.where(on_query, got_2, keep_2)

    first = nseq * (2 * t + branch)
    other = nseq * (2 * t + 1 - branch)
    own_crops = lax.dynamic_slice(crops[0], (first, 0, 0), (nseq, slots, width)).reshape(rows, width)
    got_crops = swap_cores(
        lax.dynamic_slice(crops[0], (other, 0, 0), (nseq, slots, width)).reshape(rows, width)
    )
    x_query = jnp.where(on_query, got_crops, own_crops)
    x_momentum = jnp.where(on_query, own_crops, got_crops)
    seg = lax.dynamic_slice(segment_ids, (0, first, 0), (2, nseq, slots))
    cot = lax.dynamic_slice(cotangent, (first, 0, 0), (nseq, slots, width)).reshape(rows, width)

    def finish_1(block):
        whole = gather(block)
        vec = jnp.sum(whole[0, :, shard:].astype(F32), axis=0)
        own = whole[:, :, :shard].reshape(tensors, width, width)
        got = swap_cores(own)
        return jnp.stack([jnp.where(on_query, own, got), jnp.where(on_query, got, own)]), vec

    def finish_2(block):
        own = gather(block).reshape(tensors, width, units)
        got = swap_cores(own)
        return jnp.stack([jnp.where(on_query, own, got), jnp.where(on_query, got, own)])

    wq_1, vec_q = finish_1(q_1)
    wq_2 = finish_2(q_2)
    m_1, m_2 = after((m_1, m_2), wq_2)
    wm_1, vec_m = finish_1(m_1)
    wm_2 = finish_2(m_2)

    flop = 2 * rows * width
    (res, hat, rstd, normed, q_t, k_t, v_t, pb, inv, ctx, cols) = call(
        query_attn_kernel,
        [
            ((width, rows), F32),
            ((width, rows), F32),
            ((8, rows), F32),
            ((width, rows), BF16),
            ((heads, HD, rows), BF16),
            ((heads, HD, rows), BF16),
            ((heads, HD + 16, rows), BF16),
            ((heads, nseq, slots, slots), BF16),
            ((heads, 8, rows), F32),
            ((tensors, 2 * heads_g, HD, rows), BF16),
            ((width, 128), F32),
        ],
        [((nseq, slots, slots), F32), ((128, width), F32)],
        (x_query, seg[1], wq_1, vec_q),
        flops=flop * (4 * width + 4 * slots * 8),
        nbytes=20_000_000,
    )
    b_arr = branch.astype(jnp.int32).reshape(1)
    out_q, keep_g2, send_g2, d_res, vgrad = call(
        query_mlp_kernel,
        [
            ((rows, width), BF16),
            ((tensors, width // 2, 2 * units), BF16),
            ((tensors, width // 2, 2 * units), BF16),
            ((width, rows), F32),
            ((width, 128), F32),
        ],
        [((width, rows), F32), ((width, rows), F32), ((width, rows), BF16), ((width, rows), BF16)],
        (b_arr, res, cot, wq_2, cols),
        smem=1,
        flops=flop * 6 * units * tensors,
        nbytes=20_000_000,
    )
    crop_keep, crop_send, keep_g1, send_g1 = call(
        query_back_kernel,
        [
            ((rows, width // 2), F32),
            ((rows, width // 2), BF16),
            ((tensors, width // 2, 4 * group + 128), BF16),
            ((tensors, width // 2, 4 * group + 128), BF16),
        ],
        [
            ((heads, HD, rows), BF16),
            ((tensors, 4 * heads_g, HD, rows), BF16),
            ((width, rows), BF16),
            ((width, 128), F32),
            ((width, rows), F32),
        ],
        (b_arr, d_res, hat, rstd, normed, q_t, k_t, v_t, pb, inv, ctx, cols, wq_1, vgrad),
        smem=1,
        flops=flop * (8 * width + 10 * slots * 8),
        nbytes=20_000_000,
    )
    (out_m,) = call(
        momentum_kernel,
        [((rows, width), BF16)],
        [
            ((heads, HD, rows), BF16),
            ((heads, HD, rows), BF16),
            ((heads, HD + 16, rows), BF16),
            ((tensors, 2 * heads_g, HD, rows), BF16),
            ((nseq, slots, slots), F32),
            ((128, width), F32),
            ((width, rows), F32),
        ],
        (x_momentum, seg[0], wm_1, wm_2, vec_m),
        flops=flop * (4 * width + 2 * units * tensors + 4 * slots * 8),
        nbytes=20_000_000,
    )

    def shares(keep, send):
        both = (keep.astype(F32) + swap_cores(send).astype(F32)).astype(BF16)
        return scatter_sum(both.reshape(tensors, dp, width // (2 * dp), both.shape[-1]))

    mlp_share = shares(keep_g2, send_g2)
    attn_share = shares(keep_g1, send_g1)
    out_rows = width // (2 * dp)
    qkv_grad = attn_share[:, : 3 * group].reshape(out_rows, 3, group)
    vec_grad = attn_share[:, 3 * group : 3 * group + 6].T
    out_grad = attn_share[:, 3 * group + 64 : 4 * group + 64].T
    up_grad = mlp_share[:, :units]
    down_grad = mlp_share[:, units:].T

    got_half = swap_cores(crop_send)
    mine = (2, nseq, slots, width // 2)
    pair = jnp.zeros(mine, F32)
    pair = put(pair, crop_keep.reshape((1,) + mine[1:]), (branch, 0, 0, 0))
    pair = put(pair, got_half.astype(F32).reshape((1,) + mine[1:]), (1 - branch, 0, 0, 0))
    far = exchange(pair.astype(BF16), 0, 1)
    crop_grad = jnp.zeros((tensors,) + mine, F32)
    crop_grad = put(crop_grad, pair[None], (t, 0, 0, 0, 0))
    crop_grad = put(crop_grad, far.astype(F32)[None], (1 - t, 0, 0, 0, 0))
    crop_grad = crop_grad.reshape(sequences, slots, width // 2)

    def over_tensor(out):
        whole = jnp.zeros((tensors, rows, width), BF16)
        whole = put(whole, out[None], (t, 0, 0))
        return put(whole, exchange(out, 0, 1)[None], (1 - t, 0, 0))

    all_q, all_m = over_tensor(out_q), over_tensor(out_m)
    own = jnp.where(on_query, all_m, all_q)
    got = swap_cores(jnp.where(on_query, all_q, all_m))
    encoded = jnp.zeros((tensors, 2, rows, width), BF16)
    encoded = put(encoded, own[:, None], (0, branch, 0, 0))
    encoded = put(encoded, got[:, None], (0, 1 - branch, 0, 0))
    encoded = encoded.reshape(1, sequences, slots, width)

    return (encoded, crop_grad, qkv_grad, out_grad, up_grad, down_grad, vec_grad[:2], vec_grad[2:])


def solution(mesh):
    placed = (
        P("branch", "dp", None, None),
        P(None, "dp", None),
        P("dp", None, None),
        P("branch", "dp", None, "tensor"),
        P("branch", "tensor", "dp"),
        P("branch", "dp", "tensor"),
        P("branch", "tensor", "dp"),
        P("branch", None, "dp"),
        P("branch", None, "dp"),
    )
    return jax.shard_map(
        on_device,
        mesh=mesh,
        in_specs=placed,
        out_specs=(
            P("branch", "dp", None, None),
            P("dp", None, "branch"),
            P(("branch", "dp"), None, "tensor"),
            P("tensor", ("branch", "dp")),
            P(("branch", "dp"), "tensor"),
            P("tensor", ("branch", "dp")),
            P(None, ("branch", "dp")),
            P(None, ("branch", "dp")),
        ),
        check_vma=False,
    )
```

```python
import functools
import math

import jax
import jax.numpy as jnp
from jax import lax
from jax.experimental import pallas as pl
from jax.experimental.pallas import tpu as pltpu
from jax.sharding import PartitionSpec as P

HD = 32
EPSILON = 1e-06
MASKED_SCORE = -1e30
LOG2E = 1.4426950408889634
BF16 = jnp.bfloat16
F32 = jnp.float32
VMEM_LIMIT = 56 * 1024 * 1024
PACE = 3600000


def nn(left, right):
    return lax.dot_general(left, right, (((1,), (0,)), ((), ())), preferred_element_type=F32)


def nt(left, right):
    return lax.dot_general(left, right, (((1,), (1,)), ((), ())), preferred_element_type=F32)


def tn(left, right):
    return lax.dot_general(left, right, (((0,), (0,)), ((), ())), preferred_element_type=F32)


def gelu_parts(v):
    a = jnp.abs(v)
    t = 1.0 / (1.0 + (0.3275911 / math.sqrt(2.0)) * a)
    bell = jnp.exp2(v * v * (-0.5 * LOG2E))
    poly = t * (
        0.5 * 0.254829592
        + t * (0.5 * -0.284496736 + t * (0.5 * 1.421413741 + t * (0.5 * -1.453152027 + t * (0.5 * 1.061405429))))
    )
    tail = poly * bell
    return jnp.where(v < 0, tail, 1.0 - tail), bell


def norm_cols(values, gain, shift):
    centred = values - jnp.mean(values, axis=0, keepdims=True)
    spread = jnp.mean(centred * centred, axis=0, keepdims=True)
    rstd = lax.rsqrt(spread + EPSILON)
    hat = centred * rstd
    return hat, rstd, hat * gain + shift


def norm_cols_back(upstream, hat, rstd, gain):
    t = upstream * gain
    return rstd * (t - jnp.mean(t, axis=0, keepdims=True) - hat * jnp.mean(t * hat, axis=0, keepdims=True))


def columns_of(vec_ref, scratch):
    scratch[...] = jnp.zeros_like(scratch)
    scratch[0:8, :] = vec_ref[...]
    return scratch[...].T


def place_columns(plan, chunk_refs, shard, width, me, cols_ref):
    for ref, spots in zip(chunk_refs, plan):
        for index, (mask, u) in spots:
            if u == 0:
                rows = pl.ds(pl.multiple_of((me ^ mask) * shard, 16), shard)
                cols_ref[rows, :] = ref[index + (slice(None), slice(width, width + 128))].astype(F32)


def place_weights(plan, own_refs, got_refs, shard, ids, targets):
    b, me, t = ids
    for half, refs in ((b, own_refs), (1 - b, got_refs)):
        for ref, spots in zip(refs, plan):
            for index, (mask, u) in spots:
                rows = pl.ds(pl.multiple_of((me ^ mask) * shard, 16), shard)
                for target, start, wide in targets:
                    target[half, t ^ u, rows, :] = ref[index + (slice(0, shard), slice(start, start + wide))]


def attend(x_ref, seg_ref, w1_ref, cols, q_ref, k_ref, v_ref, bias_ref, ctx_ref, pb_refs, inv_ref, score_refs, ready):
    tensors, width = w1_ref.shape[1], w1_ref.shape[2]
    group = width // tensors
    heads_g = group // HD
    nseq, slots = seg_ref.shape
    x_t = x_ref[...].astype(F32).T
    hat, rstd, normed = norm_cols(x_t, cols[:, 0:1], cols[:, 2:3])
    normed_low = normed.astype(BF16)
    ready("normed", hat, rstd, normed_low)
    rows = x_t.shape[1]
    for t in range(tensors):
        qk = tn(w1_ref[0, t], normed_low).astype(BF16)
        q_ref[t * heads_g : (t + 1) * heads_g] = qk[:group].reshape(heads_g, HD, rows)
        k_ref[t * heads_g : (t + 1) * heads_g] = qk[group:].reshape(heads_g, HD, rows)
        vo = tn(w1_ref[1, t], normed_low).astype(BF16)
        v_ref[t * heads_g : (t + 1) * heads_g, 0:HD] = vo[:group].reshape(heads_g, HD, rows)
    v_ref[:, HD:, :] = jnp.ones((v_ref.shape[0], v_ref.shape[1] - HD, rows), BF16)
    ready("projected")
    for s in range(nseq):
        across = jnp.broadcast_to(seg_ref[s : s + 1, :].astype(F32), (slots, slots))
        bias_ref[s] = jnp.where(across == across.T, 0.0, MASKED_SCORE)
    heads = tensors * heads_g
    parts = [slice(s * slots, (s + 1) * slots) for s in range(nseq)]
    ctx_ref[:, :heads_g] = jnp.zeros((tensors, heads_g, HD, rows), BF16)

    def score(h, s):
        score_refs[s][...] = tn(k_ref[h, :, parts[s]], q_ref[h, :, parts[s]])

    def soften(h, s):
        scores = score_refs[s][...] + bias_ref[s]
        top = jnp.max(scores, axis=0, keepdims=True)
        pb_refs[s][h] = jnp.exp2((scores - top) * (HD**-0.5 * LOG2E)).astype(BF16)

    def blend(h, s):
        both = nn(v_ref[h, :, parts[s]], pb_refs[s][h])
        inv = 1.0 / both[HD : HD + 1]
        if inv_ref is not None:
            inv_ref[h, :, parts[s]] = jnp.broadcast_to(inv, (8, slots))
        ctx_ref[h // heads_g, heads_g + h % heads_g, :, parts[s]] = (both[:HD] * inv).astype(BF16)

    def one_head(h, carry):
        for s in range(nseq):
            if s + 1 < nseq:
                score(h, s + 1)
            else:
                score(jnp.minimum(h + 1, heads - 1), 0)
            if s:
                blend(h, s - 1)
            else:
                blend(jnp.maximum(h - 1, 0), nseq - 1)
            soften(h, s)
        return carry

    score(0, 0)
    lax.fori_loop(0, heads, one_head, 0, unroll=4)
    ready("weights")
    blend(heads - 1, nseq - 1)
    ready("context")
    attn = sum(nn(w1_ref[1, t], ctx_ref[t].reshape(width, rows)) for t in range(tensors))
    return x_t, attn


def pack_kernel(b_ref, qkv_ref, out_ref, up_ref, down_ref, gain_ref, bias_ref, keep_ref, send_ref):
    first = b_ref[0] == 0
    shard, width = up_ref.shape[0], 2 * out_ref.shape[1]
    vec = jnp.concatenate([gain_ref[...], bias_ref[...], jnp.zeros((2, shard), F32)], axis=0)
    vec = jnp.concatenate([vec, jnp.zeros((8, 128 - shard), F32)], axis=1)
    none = jnp.zeros((8, 128), F32)
    vec = jnp.concatenate([jnp.where(first, vec, none), jnp.where(first, none, vec), jnp.zeros((112, 128), F32)], axis=0)
    vec = vec.T[:shard, :].astype(BF16)
    half_0 = jnp.concatenate([qkv_ref[0], qkv_ref[1]], axis=1).astype(BF16)
    half_1 = jnp.concatenate([qkv_ref[2], out_ref[...]], axis=1).astype(BF16)
    up, down = up_ref[...].astype(BF16), down_ref[...].astype(BF16)
    for ref, is_first in ((keep_ref, first), (send_ref, jnp.logical_not(first))):
        ref[:, :width] = jnp.where(is_first, half_0, half_1)
        ref[:, width : width + 128] = vec
        ref[:, width + 128 :] = jnp.where(is_first, up, down)


def split_kernel(width, b_ref, keep_ref, got_ref, q_ref, m_ref):
    first = b_ref[0] == 0
    keep, got = keep_ref[...], got_ref[...]
    q_ref[...] = jnp.where(first, keep, got)
    q_ref[:, width : width + 128] = keep[:, width : width + 128] + got[:, width : width + 128]
    m_ref[:, :width] = jnp.where(first, got[:, :width], keep[:, :width])
    m_ref[:, width:] = jnp.where(first, got[:, width + 128 :], keep[:, width + 128 :])


def query_attn_kernel(plan, shard, *refs):
    ids_ref, x_ref, seg_ref = refs[:3]
    nseq, refs = seg_ref.shape[0], refs[3:]
    if plan is None:
        given_ref, vec_ref = refs[:2]
        refs = refs[2:]
    else:
        own, got = refs[: len(plan)], refs[len(plan) : 2 * len(plan)]
        refs = refs[2 * len(plan) :]
    res_ref, cols_ref, refs = refs[0], refs[1], refs[2:]
    count = 9 + nseq
    far, kept, refs = refs[:count], refs[count : 2 * count], refs[2 * count :]
    w1_ref, hat_ref, rstd_ref, normed_ref, q_ref, k_ref, v_ref, inv_ref, ctx_ref, *pb_refs = kept
    score_refs, bias_ref, sems = refs[:nseq], refs[nseq], refs[-1]
    copies = [pltpu.make_async_copy(here, there, sems.at[i]) for i, (here, there) in enumerate(zip(kept, far))]
    if plan is None:
        w1_ref[...] = given_ref[...]
        cols_ref[...] = columns_of(vec_ref, refs[nseq + 1])
    else:
        ids = ids_ref[0], ids_ref[1], ids_ref[2]
        place_columns(plan, own, shard, w1_ref.shape[3], ids[1], cols_ref)
        place_weights(plan, own, got, shard, ids, [(w1_ref, 0, w1_ref.shape[3])])
    copies[0].start()
    cols = cols_ref[...]

    def ready(what, *values):
        if what == "normed":
            hat, rstd, normed = values
            hat_ref[...] = hat
            rstd_ref[...] = jnp.broadcast_to(rstd, rstd_ref.shape)
            normed_ref[...] = normed
        spots = {"normed": (1, 2, 3), "projected": (4, 5, 6), "weights": range(9, count), "context": (7, 8)}
        for i in spots[what]:
            copies[i].start()

    x_t, attn = attend(
        x_ref, seg_ref, w1_ref, cols, q_ref, k_ref, v_ref, bias_ref, ctx_ref, pb_refs, inv_ref, score_refs, ready
    )
    res_ref[...] = x_t + attn + cols[:, 3:4]
    for copy in copies:
        copy.wait()


def momentum_kernel(plan, shard, *refs):
    ids_ref, x_ref, seg_ref = refs[:3]
    nseq = seg_ref.shape[0]
    pb_refs, score_refs, refs = refs[-2 * nseq : -nseq], refs[-nseq:], refs[3 : -2 * nseq]
    if plan is None:
        w1_ref, w2_ref, vec_ref, out_ref = refs[:4]
        q_ref, k_ref, v_ref, ctx_ref, bias_ref, acc_ref, vec_pad = refs[4:]
        cols = columns_of(vec_ref, vec_pad)
    else:
        cols_ref, refs = refs[0], refs[1:]
        own, got = refs[: len(plan)], refs[len(plan) : 2 * len(plan)]
        out_ref, q_ref, k_ref, v_ref, ctx_ref, bias_ref, acc_ref, w1_ref, w2_ref = refs[2 * len(plan) :]
        cols = cols_ref[...][:, 8:]
        ids = ids_ref[0], ids_ref[1], ids_ref[2]
        wide = w1_ref.shape[3]
        place_weights(plan, own, got, shard, ids, [(w1_ref, 0, wide), (w2_ref, wide, w2_ref.shape[3])])
    x_t, attn = attend(
        x_ref, seg_ref, w1_ref, cols, q_ref, k_ref, v_ref, bias_ref, ctx_ref, pb_refs, None, score_refs, lambda *what: None
    )
    res = x_t + attn + cols[:, 3:4]
    _, _, normed = norm_cols(res, cols[:, 1:2], cols[:, 4:5])
    rows_low = normed.T.astype(BF16)
    acc_ref[...] = res + cols[:, 5:6]
    tensors, units = w2_ref.shape[1], w2_ref.shape[3]
    chunk = 256
    parts = units // chunk

    def step(i, carry):
        t, c = i // parts, pl.ds(pl.multiple_of((i % parts) * chunk, chunk), chunk)
        pre = nn(rows_low, w2_ref[0, t, :, c])
        half, _ = gelu_parts(pre)
        acc_ref[...] += nt(w2_ref[1, t, :, c], (pre * half).astype(BF16))
        return carry

    lax.fori_loop(0, tensors * parts, step, 0)
    out_ref[...] = acc_ref[...].T.astype(BF16)


def store_grads(plan, ids, ref, t, cols, values):
    if plan is None:
        ref[t, :, cols] = values
        return
    dp, final = plan
    me, mine = ids[1], ids[2]
    share = values.shape[0] // dp
    size = final.bit_length()
    for i in range(dp):
        mask = me ^ i
        ref[(mask & final) * 2 + (mine ^ t), mask >> (size), :, cols] = values[i * share : (i + 1) * share]


def query_mlp_kernel(plan, chunks, shard, *refs):
    ids_ref, res_ref, cot_ref, cols_ref = refs[:4]
    refs = refs[4:]
    ids = ids_ref[0], ids_ref[1], ids_ref[2]
    b = ids[0]
    if chunks is None:
        w2_ref, refs = refs[0], refs[1:]
    else:
        own, got = refs[: len(chunks)], refs[len(chunks) : 2 * len(chunks)]
        w2_ref, refs = refs[-1], refs[2 * len(chunks) : -1]
        place_weights(chunks, own, got, shard, ids, [(w2_ref, 0, w2_ref.shape[3])])
    out_ref, keep_ref, send_ref, dres_ref, vgrad_ref, acc_ref, dn_ref, n2t_ref, gt_ref = refs
    cols = cols_ref[...]
    res = res_ref[...]
    hat, rstd, normed = norm_cols(res, cols[:, 1:2], cols[:, 4:5])
    n2t_ref[...] = normed.astype(BF16)
    rows_low = normed.T.astype(BF16)
    cot = cot_ref[...]
    cot_t = cot.astype(F32).T
    gt_ref[...] = cot_t.astype(BF16)
    acc_ref[...] = res + cols[:, 5:6]
    dn_ref[...] = jnp.zeros_like(dn_ref)
    tensors, width, units = w2_ref.shape[1], w2_ref.shape[2], w2_ref.shape[3]
    chunk = 256
    parts = units // chunk
    half_rows = width // 2

    def step(i, carry):
        t, off = i // parts, pl.multiple_of((i % parts) * chunk, chunk)
        c = pl.ds(off, chunk)
        up, down = w2_ref[0, t, :, c], w2_ref[1, t, :, c]
        pre = nn(rows_low, up)
        d_hidden = nn(cot, down)
        half, bell = gelu_parts(pre)
        hidden = (pre * half).astype(BF16)
        d_pre = (d_hidden * (half + pre * bell * (1.0 / math.sqrt(2.0 * math.pi)))).astype(BF16)
        acc_ref[...] += nt(down, hidden)
        dn_ref[...] += nt(up, d_pre)
        for ref, which in ((keep_ref, b), (send_ref, 1 - b)):
            rows = pl.ds(pl.multiple_of(which * half_rows, 16), half_rows)
            store_grads(plan, ids, ref, t, c, nn(n2t_ref[rows, :], d_pre).astype(BF16))
            later = pl.ds(pl.multiple_of(units + off, chunk), chunk)
            store_grads(plan, ids, ref, t, later, nn(gt_ref[rows, :], hidden).astype(BF16))
        return carry

    lax.fori_loop(0, tensors * parts, step, 0)
    out_ref[...] = acc_ref[...].T.astype(BF16)
    d_n2 = dn_ref[...]
    d_res = cot_t + norm_cols_back(d_n2, hat, rstd, cols[:, 1:2])
    dres_ref[...] = d_res
    lane = lax.broadcasted_iota(jnp.int32, vgrad_ref.shape, 1)
    total = jnp.zeros(vgrad_ref.shape, F32)
    for j, term in ((1, d_n2 * hat), (3, d_res), (4, d_n2), (5, cot_t)):
        total = total + jnp.where(lane == 64 + j, jnp.sum(term, axis=1, keepdims=True), 0.0)
    vgrad_ref[...] = total


def query_back_kernel(plan, nseq, *refs):
    ids_ref, dres_ref, vgrad_ref, cols_ref = refs[:4]
    count = 9 + nseq
    far, refs = refs[4 : 4 + count], refs[4 + count :]
    crop_keep_ref, crop_send_ref, keep_ref, send_ref, dctx_ref, dproj_ref, dattn_ref, vg_ref, crop_ref = refs[:9]
    dp_refs, ds_refs, delta_refs = (refs[9 + i * nseq : 9 + (i + 1) * nseq] for i in range(3))
    kept, sems = refs[9 + 3 * nseq : -1], refs[-1]
    w1_ref, hat_ref, rstd_ref, normed_ref, q_ref, k_ref, v_ref, inv_ref, ctx_ref, *pb_refs = kept
    copies = [pltpu.make_async_copy(there, here, sems.at[i]) for i, (here, there) in enumerate(zip(kept, far))]
    late = (1, 2, 3)
    for i in [i for i in range(count) if i not in late] + list(late):
        copies[i].start()
    ids = ids_ref[0], ids_ref[1], ids_ref[2]
    b = ids[0]
    tensors, width = w1_ref.shape[1], w1_ref.shape[2]
    group = width // tensors
    heads_g = group // HD
    heads, slots = pb_refs[0].shape[0], pb_refs[0].shape[1]
    rows = nseq * slots
    d_attn = dres_ref[...].astype(BF16)
    dattn_ref[...] = d_attn
    copies[0].wait()
    for t in range(tensors):
        vo = tn(w1_ref[1, t], d_attn).astype(BF16)
        dctx_ref[t * heads_g : (t + 1) * heads_g] = vo[group:].reshape(heads_g, HD, rows)
    dproj_ref[:, 3 * heads_g :] = jnp.zeros((tensors, heads_g, HD, rows), BF16)
    parts = [slice(s * slots, (s + 1) * slots) for s in range(nseq)]
    scale = HD**-0.5

    def d_weights(h, s):
        t, hh = h // heads_g, h % heads_g
        low_ctx = dctx_ref[h, :, parts[s]].astype(F32) * inv_ref[h, 0:1, parts[s]]
        delta = jnp.sum(low_ctx * ctx_ref[t, heads_g + hh, :, parts[s]].astype(F32), axis=0, keepdims=True)
        delta_refs[s][...] = jnp.broadcast_to(delta, (8, slots))
        low_ctx = low_ctx.astype(BF16)
        dp_refs[s][...] = tn(v_ref[h, 0:HD, parts[s]], low_ctx)
        dproj_ref[t, 2 * heads_g + hh, :, parts[s]] = nt(low_ctx, pb_refs[s][h]).astype(BF16)

    def harden(h, s):
        ds_refs[s][...] = (pb_refs[s][h].astype(F32) * (dp_refs[s][...] - delta_refs[s][0:1, :])).astype(BF16)

    def d_inputs(h, s):
        t, hh = h // heads_g, h % heads_g
        d_scores = ds_refs[s][...]
        dproj_ref[t, hh, :, parts[s]] = (nn(k_ref[h, :, parts[s]], d_scores) * scale).astype(BF16)
        dproj_ref[t, heads_g + hh, :, parts[s]] = (nt(q_ref[h, :, parts[s]], d_scores) * scale).astype(BF16)

    def one_head(h, carry):
        for s in range(nseq):
            if s + 1 < nseq:
                d_weights(h, s + 1)
            else:
                d_weights(jnp.minimum(h + 1, heads - 1), 0)
            if s:
                d_inputs(h, s - 1)
            else:
                d_inputs(jnp.maximum(h - 1, 0), nseq - 1)
            harden(h, s)
        return carry

    for i in range(1, count):
        if i not in late:
            copies[i].wait()
    d_weights(0, 0)
    lax.fori_loop(0, heads, one_head, 0, unroll=4)
    d_inputs(heads - 1, nseq - 1)
    d_normed = jnp.zeros((width, rows), F32)
    for t in range(tensors):
        d_t = dproj_ref[t].reshape(4 * group, rows)
        d_normed += nn(w1_ref[0, t], d_t[: 2 * group]) + nn(w1_ref[1, t], d_t[2 * group :])
    for i in late:
        copies[i].wait()
    hat = hat_ref[...]
    cols = cols_ref[...]
    crop_ref[...] = dres_ref[...] + norm_cols_back(d_normed, hat, rstd_ref[0:1, :], cols[:, 0:1])
    lane = lax.broadcasted_iota(jnp.int32, vgrad_ref.shape, 1)
    total = vgrad_ref[...]
    for j, term in ((0, d_normed * hat), (2, d_normed)):
        total = total + jnp.where(lane == 64 + j, jnp.sum(term, axis=1, keepdims=True), 0.0)
    vg_ref[...] = total
    half_rows = width // 2
    tile = (3 * group) // 128 * 128
    for ref, which in ((keep_ref, b), (send_ref, 1 - b)):
        part = pl.ds(pl.multiple_of(which * half_rows, 16), half_rows)
        left, right = normed_ref[part, :], dattn_ref[part, :]
        for t in range(tensors):
            d_t = dproj_ref[t].reshape(4 * group, rows)
            grads = nt(left, d_t[: 3 * group + 64])
            outs = nt(right, ctx_ref[t, heads_g:].reshape(group, rows))
            outs = jnp.concatenate([outs, jnp.zeros((half_rows, 64), F32)], axis=1)
            grads = jnp.concatenate([grads[:, :tile], grads[:, tile:] + vg_ref[part, :], outs], axis=1)
            store_grads(plan, ids, ref, t, slice(None), grads.astype(BF16))
    for s in range(nseq):
        part = slice(s * slots, (s + 1) * slots)
        crop_keep_ref[s] = crop_ref[pl.ds(pl.multiple_of(b * half_rows, 16), half_rows), part]
        crop_send_ref[s] = crop_ref[pl.ds(pl.multiple_of((1 - b) * half_rows, 16), half_rows), part].astype(BF16)


def encoded_kernel(ids_ref, q_ref, q_far, m_ref, m_far, got_ref, got_far, out_ref):
    b, t = ids_ref[0], ids_ref[2]
    first = b == 0
    out_ref[t, b] = jnp.where(first, m_ref[...], q_ref[...])
    out_ref[1 - t, b] = jnp.where(first, m_far[...], q_far[...])
    out_ref[t, 1 - b] = got_ref[...]
    out_ref[1 - t, 1 - b] = got_far[...]


def call(kernel, out_shapes, scratch, args, smem=0, hbm=0, hbm_outs=0, copies=0, stream=False):
    place, hold = pl.BlockSpec(memory_space=pltpu.VMEM), pl.BlockSpec(memory_space=pltpu.HBM)
    inner = args[smem : len(args) - hbm]
    if stream:
        specs = [pl.BlockSpec(x.shape, lambda i, n=x.ndim: (0,) * n) for x in inner]
    else:
        specs = [place] * len(inner)
    return pl.pallas_call(
        kernel,
        grid=(1,) if stream else (),
        out_shape=[jax.ShapeDtypeStruct(s, d) for s, d in out_shapes],
        in_specs=[pl.BlockSpec(memory_space=pltpu.SMEM)] * smem + specs + [hold] * hbm,
        out_specs=[place] * (len(out_shapes) - hbm_outs) + [hold] * hbm_outs,
        scratch_shapes=[pltpu.VMEM(s, d) for s, d in scratch]
        + ([pltpu.SemaphoreType.DMA((copies,))] if copies else []),
        compiler_params=pltpu.CompilerParams(vmem_limit_bytes=VMEM_LIMIT),
    )(*args)


SPAN = ("dp", "tensor")


def swap_cores(block):
    return lax.ppermute(block, "branch", [(0, 1), (1, 0)])


def exchange(block, dp_mask, t_mask):
    dp, tensors = lax.axis_size("dp"), lax.axis_size("tensor")
    pairs = [
        (i * tensors + t, (i ^ dp_mask) * tensors + (t ^ t_mask)) for i in range(dp) for t in range(tensors)
    ]
    return lax.ppermute(block, SPAN, pairs)


def after(value, *deps):
    return lax.optimization_barrier((value, *deps))[0]


def near_pieces(both):
    return [exchange(both[j], j // 2, j % 2) for j in range(1, both.shape[0])]


def far_pieces(low, final):
    return [exchange(low[k], k << final.bit_length(), 0) for k in range(1, low.shape[0])]


def add_all(total, pieces):
    for piece in pieces:
        total = total + piece.astype(F32)
    return total


def dp_groups():
    bits = lax.axis_size("dp").bit_length() - 1
    groups, high = [], bits
    while high >= 2:
        high -= 2
        groups.append((high, 4))
    last = (0, 2) if high == 1 else None
    return groups, last


def put(whole, block, index):
    return lax.dynamic_update_slice(whole, block, index)


def gather(block):
    groups, last = dp_groups()
    me, t = lax.axis_index("dp"), lax.axis_index("tensor")
    tensors = lax.axis_size("tensor")
    for number, (shift, size) in enumerate(groups):
        lead, tail = block.shape[:number], block.shape[number:]
        whole = jnp.zeros(lead + (size,) + tail, block.dtype)
        mine = (me >> shift) & (size - 1)
        pieces = [(0, block)] + [(k, exchange(block, k << shift, 0)) for k in range(1, size)]
        for k, piece in pieces:
            whole = put(whole, jnp.expand_dims(piece, number), (0,) * number + (mine ^ k,) + (0,) * len(tail))
        block = whole
    lead, tail = block.shape[: len(groups)], block.shape[len(groups) :]
    size = last[1] if last else 1
    mine = me & (size - 1)
    whole = jnp.zeros((tensors,) + lead + (size,) + tail, block.dtype)
    for k in range(size):
        for u in range(tensors):
            piece = block if k == u == 0 else exchange(block, k, u)
            piece = jnp.expand_dims(jnp.expand_dims(piece, len(lead)), 0)
            whole = put(whole, piece, (t ^ u,) + (0,) * len(lead) + (mine ^ k,) + (0,) * len(tail))
    return whole.reshape((tensors, lax.axis_size("dp")) + tail)


def scatter_sum(block):
    groups, last = dp_groups()
    me, t = lax.axis_index("dp"), lax.axis_index("tensor")
    tensors = lax.axis_size("tensor")
    tail = block.shape[2:]
    size = last[1] if last else 1
    lead = tuple(g[1] for g in groups)
    block = block.reshape((tensors,) + lead + (size,) + tail)
    mine = me & (size - 1)

    def take(k, u):
        start = (t ^ u,) + (0,) * len(lead) + (mine ^ k,) + (0,) * len(tail)
        piece = lax.dynamic_slice(block, start, (1,) + lead + (1,) + tail)
        return piece.reshape(lead + tail)

    total = take(0, 0).astype(F32)
    for k in range(size):
        for u in range(tensors):
            if k or u:
                total = total + exchange(take(k, u), k, u).astype(F32)
    for number in reversed(range(len(groups))):
        shift, size = groups[number]
        mine = (me >> shift) & (size - 1)
        low = total.astype(BF16)

        def part(k, whole=low, number=number, mine=mine):
            return lax.dynamic_index_in_dim(whole, mine ^ k, number, keepdims=False)

        total = part(0, total).astype(F32)
        for k in range(1, size):
            total = total + exchange(part(k), k << shift, 0).astype(F32)
    return total


def stack_peers(block, stage):
    return jnp.stack([block] + [exchange(block, *peer) for peer in stage]), [(0, 0)] + stage


def chunks_of(block, masks, stage):
    pieces = [((0, 0), block)] + [(peer, exchange(block, *peer)) for peer in stage]
    return [
        (piece, [((j,), (m ^ peer[0], u ^ peer[1])) for j, (m, u) in enumerate(masks)]) for peer, piece in pieces
    ]


def chip_sum(keep, send):
    return (keep.astype(F32) + swap_cores(send).astype(F32)).astype(BF16)


def on_device(
    crops, segment_ids, cotangent, qkv_weight, out_weight, up_weight, down_weight, gain_rows, biases
):
    branch, me, t = lax.axis_index("branch"), lax.axis_index("dp"), lax.axis_index("tensor")
    dp, tensors = lax.axis_size("dp"), lax.axis_size("tensor")
    on_query = branch == 0
    _, sequences, slots, width = crops.shape
    nseq = sequences // (2 * tensors)
    rows = nseq * slots
    shard = qkv_weight.shape[1]
    group = out_weight.shape[1]
    units = up_weight.shape[2]
    heads = tensors * group // HD
    heads_g = group // HD
    ids = jnp.stack([branch, me, t]).astype(jnp.int32)
    fine = tensors == 2 and dp == 8 and shard % 16 == 0
    near = [(k << 1, 0) for k in range(1, 4)]

    qkv, out_t = qkv_weight[0].transpose(1, 0, 2), out_weight[0].T
    up, down_t = up_weight[0], down_weight[0].T
    if fine:
        block = ((shard, width + 128 + units), BF16)
        keep, send = call(
            pack_kernel,
            [block] * 2,
            [],
            (ids, qkv, out_t, up, down_t, gain_rows[0], biases[0]),
            smem=1,
            stream=True,
        )
        got = swap_cores(send)
        q_all, m_all = call(
            functools.partial(split_kernel, width),
            [block, ((shard, width + units), BF16)],
            [],
            (ids, keep, got),
            smem=1,
        )
    else:
        small = jnp.concatenate([gain_rows[0], biases[0]], axis=0).astype(BF16)
        vec_rows = put(jnp.zeros((8, width), BF16), small, (0, me * shard))
        half_0 = jnp.concatenate([qkv[0], qkv[1]], axis=1).astype(BF16)
        half_1 = jnp.concatenate([qkv[2], out_t], axis=1).astype(BF16)
        half_0, half_1 = (jnp.concatenate([half, vec_rows], axis=0) for half in (half_0, half_1))
        mlp_0, mlp_1 = up.astype(BF16), down_t.astype(BF16)
        keep_1, send_1 = jnp.where(on_query, half_0, half_1), jnp.where(on_query, half_1, half_0)
        keep_2, send_2 = jnp.where(on_query, mlp_0, mlp_1), jnp.where(on_query, mlp_1, mlp_0)
        got_1, got_2 = swap_cores(send_1), swap_cores(send_2)
        q_2, m_2 = jnp.where(on_query, keep_2, got_2), jnp.where(on_query, got_2, keep_2)

    first = nseq * (2 * t + branch)
    other = nseq * (2 * t + 1 - branch)
    own_crops = lax.dynamic_slice(crops[0], (first, 0, 0), (nseq, slots, width)).reshape(rows, width)
    got_crops = swap_cores(
        lax.dynamic_slice(crops[0], (other, 0, 0), (nseq, slots, width)).reshape(rows, width)
    )
    x_query = jnp.where(on_query, got_crops, own_crops)
    x_momentum = jnp.where(on_query, own_crops, got_crops)
    seg = lax.dynamic_slice(segment_ids, (0, first, 0), (2, nseq, slots))
    cot = lax.dynamic_slice(cotangent, (first, 0, 0), (nseq, slots, width)).reshape(rows, width)

    w1_shape, w2_shape = (2, tensors, width, width), (2, tensors, width, units)
    share = width // (2 * dp)
    if fine:
        both_ways = [(1, 0), (0, 1), (1, 1)]
        stack_q, masks = stack_peers(q_all, near)
        stack_1, stack_2 = stack_q[..., : width + 128], stack_q[..., width + 128 :]
        chunks = chunks_of(stack_1, masks, both_ways)
        plan = [spots for _, spots in chunks]
        args_1 = [block for block, _ in chunks]
        args_1 = args_1 + [swap_cores(block) for block in args_1]
        stack_2 = after(stack_2, args_1[1])
        m_all = after(m_all, stack_1)
        stack_m, _ = stack_peers(m_all, near)
        x_query = after(x_query, stack_2)
        own_2 = [block for block, _ in chunks_of(stack_2, masks, both_ways)]
        plan_1 = plan_2 = plan_m = plan
        extra_1, extra_2, extra_m = [], [(w2_shape, BF16)], [(w1_shape, BF16), (w2_shape, BF16)]
        scatter = (dp, 1)
        grads_1, grads_2 = (4, dp // 2, share, 4 * group + 128), (4, dp // 2, share, 2 * units)
    else:

        def finish(block):
            own = gather(block)
            got = swap_cores(own)
            return jnp.stack([jnp.where(on_query, own, got), jnp.where(on_query, got, own)])

        def finish_1(block):
            whole = finish(block)
            vec = jnp.sum(whole[0, 0, :, shard:].astype(F32), axis=0)
            return whole[:, :, :, :shard].reshape(w1_shape), vec

        wq_1, vec_q = finish_1(jnp.where(on_query, keep_1, got_1))
        wm_1, vec_m = finish_1(jnp.where(on_query, got_1, keep_1))
        wq_2, wm_2 = (finish(block).reshape(w2_shape) for block in (q_2, m_2))
        plan_1 = plan_2 = plan_m = scatter = None
        args_1, args_2, args_m = [wq_1, vec_q], [wq_2], [wm_1, wm_2, vec_m]
        extra_1 = extra_m = [((128, width), F32)]
        extra_2 = []
        grads_1, grads_2 = (tensors, width // 2, 4 * group + 128), (tensors, width // 2, 2 * units)

    head_block = ((heads, HD, rows), BF16)
    v_block = ((heads, HD + 16, rows), BF16)
    ctx_block = ((tensors, 2 * heads_g, HD, rows), BF16)
    bias_block = ((nseq, slots, slots), F32)
    score_block, pb_block = ((slots, slots), F32), ((heads, slots, slots), BF16)
    col_block = ((width, 128), F32)
    wide_f, wide_b = ((width, rows), F32), ((width, rows), BF16)
    kept = [(w1_shape, BF16), wide_f, ((8, rows), F32), wide_b, head_block, head_block, v_block]
    kept = kept + [((heads, 8, rows), F32), ctx_block] + [pb_block] * nseq
    attn_outs = call(
        functools.partial(query_attn_kernel, plan_1, shard),
        [wide_f, col_block] + kept,
        kept + [score_block] * nseq + [bias_block] + extra_1,
        (ids, x_query, seg[1], *args_1),
        smem=1,
        hbm_outs=len(kept),
        copies=len(kept),
    )
    if fine:
        own_2, attn_outs = after((own_2, attn_outs))
        args_2 = own_2 + [swap_cores(block) for block in own_2]
        cot = after(cot, stack_m)
        own_m = [block for block, _ in chunks_of(stack_m, masks, both_ways)]
    res, cols, *saved = attn_outs
    out_q, keep_g2, send_g2, d_res, vgrad = call(
        functools.partial(query_mlp_kernel, scatter, plan_2, shard),
        [((rows, width), BF16), (grads_2, BF16), (grads_2, BF16), wide_f, col_block],
        [wide_f, wide_f, wide_b, wide_b] + extra_2,
        (ids, res, cot, cols, *args_2),
        smem=1,
    )
    if fine:
        own_m, (out_q, keep_g2, send_g2, d_res, vgrad) = after((own_m, (out_q, keep_g2, send_g2, d_res, vgrad)))
        args_m = own_m + [swap_cores(block) for block in own_m]
        mlp_chip = chip_sum(keep_g2, send_g2)
        d_res = after(d_res, mlp_chip)
        pieces_2 = near_pieces(mlp_chip)
    crop_keep, crop_send, keep_g1, send_g1 = call(
        functools.partial(query_back_kernel, scatter, nseq),
        [((nseq, width // 2, slots), F32), ((nseq, width // 2, slots), BF16), (grads_1, BF16), (grads_1, BF16)],
        [head_block, ((tensors, 4 * heads_g, HD, rows), BF16), wide_b, col_block, wide_f]
        + [score_block] * nseq
        + [((slots, slots), BF16)] * nseq
        + [((8, slots), F32)] * nseq
        + kept,
        (ids, d_res, vgrad, cols, *saved),
        smem=1,
        hbm=len(kept),
        copies=len(kept),
    )
    if fine:
        pieces_2, (crop_keep, crop_send, keep_g1, send_g1) = after((pieces_2, (crop_keep, crop_send, keep_g1, send_g1)))
        mlp_near = add_all(mlp_chip[0].astype(F32), pieces_2)
        mlp_low = mlp_near.astype(BF16)
    got_half = swap_cores(crop_send)
    mine = (2, nseq, width // 2, slots)
    pair = jnp.zeros(mine, F32)
    pair = put(pair, crop_keep[None], (branch, 0, 0, 0))
    pair = put(pair, got_half.astype(F32)[None], (1 - branch, 0, 0, 0))
    if fine:
        attn_chip = chip_sum(keep_g1, send_g1)
        x_momentum = after(x_momentum, attn_chip, pair, mlp_low)
        pieces_1, far_2, far = near_pieces(attn_chip), far_pieces(mlp_low, 1), exchange(pair.astype(BF16), 0, 1)
    (out_m,) = call(
        functools.partial(momentum_kernel, plan_m, shard),
        [((rows, width), BF16)],
        [head_block, head_block, v_block, ctx_block, bias_block, wide_f] + extra_m + [pb_block] * nseq + [score_block] * nseq,
        (ids, x_momentum, seg[0], *([cols] if fine else []), *args_m),
        smem=1,
    )

    if fine:
        pieces_1, far_2, far, out_m = after((pieces_1, far_2, far, out_m))
        mlp_share = add_all(mlp_near[0], far_2)
        attn_near = add_all(attn_chip[0].astype(F32), pieces_1)
        attn_share = add_all(attn_near[0], far_pieces(attn_near.astype(BF16), 1))
    else:

        def shares(keep, send):
            both = chip_sum(keep, send)
            return scatter_sum(both.reshape(tensors, dp, share, both.shape[-1]))

        mlp_share, attn_share = shares(keep_g2, send_g2), shares(keep_g1, send_g1)
    qkv_grad = attn_share[:, : 3 * group].reshape(share, 3, group)
    vec_grad = attn_share[:, 3 * group : 3 * group + 6].T
    out_grad = attn_share[:, 3 * group + 64 : 4 * group + 64].T
    up_grad = mlp_share[:, :units]
    down_grad = mlp_share[:, units:].T

    if not fine:
        far = exchange(pair.astype(BF16), 0, 1)
    crop_grad = jnp.zeros((tensors,) + mine, F32)
    crop_grad = put(crop_grad, pair[None], (t, 0, 0, 0, 0))
    crop_grad = put(crop_grad, far.astype(F32)[None], (1 - t, 0, 0, 0, 0))
    crop_grad = crop_grad.reshape(sequences, width // 2, slots).transpose(0, 2, 1)

    far_q, far_m = exchange(out_q, 0, 1), exchange(out_m, 0, 1)
    got = swap_cores(jnp.where(on_query, out_q, out_m))
    got_far = swap_cores(jnp.where(on_query, far_q, far_m))
    (encoded,) = call(
        encoded_kernel,
        [((tensors, 2, rows, width), BF16)],
        [],
        (ids, out_q, far_q, out_m, far_m, got, got_far),
        smem=1,
    )
    encoded = encoded.reshape(1, sequences, slots, width)

    return (encoded, crop_grad, qkv_grad, out_grad, up_grad, down_grad, vec_grad[:2], vec_grad[2:])


def solution(mesh):
    placed = (
        P("branch", "dp", None, None),
        P(None, "dp", None),
        P("dp", None, None),
        P("branch", "dp", None, "tensor"),
        P("branch", "tensor", "dp"),
        P("branch", "dp", "tensor"),
        P("branch", "tensor", "dp"),
        P("branch", None, "dp"),
        P("branch", None, "dp"),
    )
    return jax.shard_map(
        on_device,
        mesh=mesh,
        in_specs=placed,
        out_specs=(
            P("branch", "dp", None, None),
            P("dp", None, "branch"),
            P(("branch", "dp"), None, "tensor"),
            P("tensor", ("branch", "dp")),
            P(("branch", "dp"), "tensor"),
            P("tensor", ("branch", "dp")),
            P(None, ("branch", "dp")),
            P(None, ("branch", "dp")),
        ),
        check_vma=False,
    )
```

```python
import functools
import math

import jax
import jax.numpy as jnp
from jax import lax
from jax.experimental import pallas as pl
from jax.experimental.pallas import tpu as pltpu
from jax.sharding import PartitionSpec as P

HD = 32
HEADS_STEP = 4
EPSILON = 1e-06
MASKED_SCORE = -1e30
LOG2E = 1.4426950408889634
BF16 = jnp.bfloat16
F32 = jnp.float32
PACE = 3600000


def nn(left, right):
    return lax.dot_general(left, right, (((1,), (0,)), ((), ())), preferred_element_type=F32)


def nt(left, right):
    return lax.dot_general(left, right, (((1,), (1,)), ((), ())), preferred_element_type=F32)


def tn(left, right):
    return lax.dot_general(left, right, (((0,), (0,)), ((), ())), preferred_element_type=F32)


def gelu_parts(v):
    a = jnp.abs(v)
    t = 1.0 / (1.0 + (0.3275911 / math.sqrt(2.0)) * a)
    bell = jnp.exp2(v * v * (-0.5 * LOG2E))
    poly = t * (
        0.5 * 0.254829592
        + t * (0.5 * -0.284496736 + t * (0.5 * 1.421413741 + t * (0.5 * -1.453152027 + t * (0.5 * 1.061405429))))
    )
    tail = poly * bell
    return jnp.where(v < 0, tail, 1.0 - tail), bell


def norm_cols(values, gain, shift):
    centred = values - jnp.mean(values, axis=0, keepdims=True)
    spread = jnp.mean(centred * centred, axis=0, keepdims=True)
    rstd = lax.rsqrt(spread + EPSILON)
    hat = centred * rstd
    return hat, rstd, hat * gain + shift


def norm_cols_back(upstream, hat, rstd, gain):
    t = upstream * gain
    return rstd * (t - jnp.mean(t, axis=0, keepdims=True) - hat * jnp.mean(t * hat, axis=0, keepdims=True))


def columns_of(query_ref, momentum_ref, scratch):
    scratch[...] = jnp.zeros_like(scratch)
    scratch[0:8, :] = query_ref[...]
    scratch[8:16, :] = momentum_ref[...]
    return scratch[...].T


def place_columns(plan, chunk_refs, shard, width, me, cols_ref):
    for ref, spots in zip(chunk_refs, plan):
        for index, (mask, u) in spots:
            if u == 0:
                rows = pl.ds(pl.multiple_of((me ^ mask) * shard, 16), shard)
                cols_ref[rows, :] = ref[index + (slice(None), slice(width, width + 128))].astype(F32)


def place_weights(plan, own_refs, got_refs, shard, ids, targets):
    b, me, t = ids
    for half, refs in ((b, own_refs), (1 - b, got_refs)):
        for ref, spots in zip(refs, plan):
            for index, (mask, u) in spots:
                rows = pl.ds(pl.multiple_of((me ^ mask) * shard, 16), shard)
                for target, to, start, wide in targets:
                    block = ref[index + (slice(0, shard), slice(start, start + wide))]
                    target[half, t ^ u, rows, to : to + wide] = block


def attend(x, segs, w1_ref, cols, q_ref, k_ref, v_ref, bias_ref, ctx_ref, pb_refs, inv_ref, score_refs, keep=None):
    tensors, width = w1_ref.shape[1], w1_ref.shape[2]
    group = width // tensors
    heads_g = group // HD
    nseq, slots = len(segs), segs[0].shape[1]
    x_t = x.astype(F32).T
    hat, rstd, normed = norm_cols(x_t, cols[:, 0:1], cols[:, 2:3])
    normed_low = normed.astype(BF16)
    if keep is not None:
        keep(hat, rstd, normed_low)
    rows = x_t.shape[1]
    for t in range(tensors):
        qk = tn(w1_ref[0, t], normed_low).astype(BF16)
        q_ref[t * heads_g : (t + 1) * heads_g] = qk[:group].reshape(heads_g, HD, rows)
        k_ref[t * heads_g : (t + 1) * heads_g] = qk[group:].reshape(heads_g, HD, rows)
        vo = tn(w1_ref[1, t], normed_low).astype(BF16)
        v_ref[t * heads_g : (t + 1) * heads_g, 0:HD] = vo[:group].reshape(heads_g, HD, rows)
    v_ref[:, HD:, :] = jnp.ones((v_ref.shape[0], v_ref.shape[1] - HD, rows), BF16)
    for s in range(nseq):
        across = jnp.broadcast_to(segs[s].astype(F32), (slots, slots))
        bias_ref[s] = jnp.where(across == across.T, 0.0, MASKED_SCORE)
    heads = tensors * heads_g
    parts = [slice(s * slots, (s + 1) * slots) for s in range(nseq)]
    ctx_ref[:, :heads_g] = jnp.zeros((tensors, heads_g, HD, rows), BF16)

    def score(h, s):
        score_refs[s][...] = tn(k_ref[h, :, parts[s]], q_ref[h, :, parts[s]])

    def soften(h, s):
        scores = score_refs[s][...] + bias_ref[s]
        top = jnp.max(scores, axis=0, keepdims=True)
        pb_refs[s][h] = jnp.exp2((scores - top) * (HD**-0.5 * LOG2E)).astype(BF16)

    def blend(h, s):
        both = nn(v_ref[h, :, parts[s]], pb_refs[s][h])
        inv = 1.0 / both[HD : HD + 1]
        if inv_ref is not None:
            inv_ref[h, :, parts[s]] = jnp.broadcast_to(inv, (8, slots))
        ctx_ref[h // heads_g, heads_g + h % heads_g, :, parts[s]] = (both[:HD] * inv).astype(BF16)

    def one_head(h, carry):
        for s in range(nseq):
            if s + 1 < nseq:
                score(h, s + 1)
            else:
                score(jnp.minimum(h + 1, heads - 1), 0)
            if s:
                blend(h, s - 1)
            else:
                blend(jnp.maximum(h - 1, 0), nseq - 1)
            soften(h, s)
        return carry

    score(0, 0)

    def some_heads(g, carry):
        for h in range(HEADS_STEP):
            one_head(g * HEADS_STEP + h, carry)
        return carry

    lax.fori_loop(0, heads // HEADS_STEP, some_heads, 0)
    blend(heads - 1, nseq - 1)
    attn = sum(nn(w1_ref[1, t], ctx_ref[t].reshape(width, rows)) for t in range(tensors))
    return x_t, attn


def pack_kernel(b_ref, *refs):
    far, keep_ref, send_ref, near, sems = refs[:6], refs[6], refs[7], refs[8:14], refs[14]
    copies = [pltpu.make_async_copy(there, here, sems.at[i]) for i, (there, here) in enumerate(zip(far, near))]
    for copy in copies:
        copy.start()
    qkv_ref, out_ref, up_ref, down_ref, gain_ref, bias_ref = near
    first = b_ref[0] == 0
    shard, width = up_ref.shape[0], 2 * out_ref.shape[1]
    for copy in copies:
        copy.wait()
    vec = jnp.concatenate([gain_ref[...], bias_ref[...], jnp.zeros((2, shard), F32)], axis=0)
    vec = jnp.concatenate([vec, jnp.zeros((8, 128 - shard), F32)], axis=1)
    none = jnp.zeros((8, 128), F32)
    vec = jnp.concatenate([jnp.where(first, vec, none), jnp.where(first, none, vec), jnp.zeros((112, 128), F32)], axis=0)
    vec = vec.T[:shard, :].astype(BF16)
    half_0 = jnp.concatenate([qkv_ref[0], qkv_ref[1]], axis=1).astype(BF16)
    half_1 = jnp.concatenate([qkv_ref[2], out_ref[...]], axis=1).astype(BF16)
    up, down = up_ref[...].astype(BF16), down_ref[...].astype(BF16)
    for ref, is_first in ((keep_ref, first), (send_ref, jnp.logical_not(first))):
        ref[:, :width] = jnp.where(is_first, half_0, half_1)
        ref[:, width : width + 128] = vec
        ref[:, width + 128 :] = jnp.where(is_first, up, down)


def split_kernel(width, b_ref, got_ref, far_ref, first_ref, second_ref, keep_ref, sems):
    copy = pltpu.make_async_copy(far_ref, keep_ref, sems.at[0])
    copy.start()
    first = b_ref[0] == 0
    got = got_ref[...]
    copy.wait()
    keep = keep_ref[...]
    query, momentum = jnp.where(first, keep, got), jnp.where(first, got, keep)
    units = second_ref.shape[1] // 2
    first_ref[:, :width] = query[:, :width]
    first_ref[:, width : width + 128] = keep[:, width : width + 128] + got[:, width : width + 128]
    first_ref[:, width + 128 :] = momentum[:, :width]
    second_ref[:, :units] = query[:, width + 128 :]
    second_ref[:, units:] = momentum[:, width + 128 :]


def attention_kernel(plan, shard, *refs):
    ids_ref, got_crops, seg_ref, refs = refs[0], refs[1], refs[2], refs[3:]
    ids = ids_ref[0], ids_ref[1], ids_ref[2]
    slots = seg_ref.shape[2]
    nseq = got_crops.shape[0] // slots
    if plan is None:
        w1_given, vec_q, w1_m, vec_m = refs[:4]
        refs = refs[4:]
    else:
        own, got = refs[: len(plan)], refs[len(plan) : 2 * len(plan)]
        refs = refs[2 * len(plan) :]
    crops_ref, res_ref, res_m_ref, cols_ref, refs = refs[0], refs[1], refs[2], refs[3], refs[4:]
    w1_ref, hat_ref, rstd_ref, normed_ref, q_ref, k_ref, v_ref, inv_ref, ctx_ref, *pb_refs = refs[: 9 + nseq]
    refs = refs[9 + nseq :]
    score_refs, pb_m, refs = refs[:nseq], refs[nseq : 2 * nseq], refs[2 * nseq :]
    q_m, k_m, v_m, ctx_m, bias_ref, mine_ref, spare, sems = refs
    first = nseq * (2 * ids[2] + ids[0])
    copy = pltpu.make_async_copy(crops_ref.at[pl.ds(first, nseq)], mine_ref, sems.at[0])
    copy.start()
    if plan is None:
        w1_ref[...] = w1_given[...]
        cols_ref[...] = columns_of(vec_q, vec_m, spare)
    else:
        wide, w1_m = w1_ref.shape[3], spare
        place_columns(plan, own, shard, wide, ids[1], cols_ref)
        place_weights(plan, own, got, shard, ids, [(w1_ref, 0, 0, wide), (w1_m, 0, wide + 128, wide)])
    cols = cols_ref[...]

    def keep(hat, rstd, normed):
        hat_ref[...] = hat
        rstd_ref[...] = jnp.broadcast_to(rstd, rstd_ref.shape)
        normed_ref[...] = normed

    copy.wait()

    def rows_of(encoder):
        mine = mine_ref[...].reshape(got_crops.shape)
        segs = [seg_ref[1 - encoder, pl.ds(first + s, 1), :] for s in range(nseq)]
        return jnp.where(ids[0] == encoder, got_crops[...], mine), segs

    x_t, attn = attend(
        *rows_of(0), w1_ref, cols, q_ref, k_ref, v_ref, bias_ref, ctx_ref, pb_refs, inv_ref, score_refs, keep
    )
    res_ref[...] = x_t + attn + cols[:, 3:4]
    cols = cols[:, 8:]
    x_t, attn = attend(*rows_of(1), w1_m, cols, q_m, k_m, v_m, bias_ref, ctx_m, pb_m, None, score_refs)
    res_m_ref[...] = x_t + attn + cols[:, 3:4]


def momentum_mlp_kernel(plan, shard, *refs):
    ids_ref, res_ref, cols_ref, query_ref, refs = refs[0], refs[1], refs[2], refs[3], refs[4:]
    ids = ids_ref[0], ids_ref[1], ids_ref[2]
    cols = cols_ref[...][:, 8:]
    if plan is None:
        w2_ref, out_ref, own_ref, send_ref, acc_ref = refs
    else:
        own, got = refs[: len(plan)], refs[len(plan) : 2 * len(plan)]
        out_ref, own_ref, send_ref, acc_ref, w2_ref = refs[2 * len(plan) :]
        place_weights(plan, own, got, shard, ids, [(w2_ref, 0, 0, w2_ref.shape[3])])
    res = res_ref[...]
    _, _, normed = norm_cols(res, cols[:, 1:2], cols[:, 4:5])
    rows_low = normed.T.astype(BF16)
    acc_ref[...] = res + cols[:, 5:6]
    tensors, units = w2_ref.shape[1], w2_ref.shape[3]
    chunk = 256
    parts = units // chunk

    def step(i, carry):
        t, c = i // parts, pl.ds(pl.multiple_of((i % parts) * chunk, chunk), chunk)
        pre = nn(rows_low, w2_ref[0, t, :, c])
        half, _ = gelu_parts(pre)
        acc_ref[...] += nt(w2_ref[1, t, :, c], (pre * half).astype(BF16))
        return carry

    lax.fori_loop(0, tensors * parts, step, 0)
    momentum, query = acc_ref[...].T.astype(BF16), query_ref[...]
    first = ids[0] == 0
    out_ref[...] = momentum
    own_ref[...] = jnp.where(first, momentum, query)
    send_ref[...] = jnp.where(first, query, momentum)


def store_grads(plan, ids, ref, t, cols, values):
    if plan is None:
        ref[t, :, cols] = values
        return
    dp, final = plan
    me, mine = ids[1], ids[2]
    share = values.shape[0] // dp
    size = final.bit_length()
    for i in range(dp):
        mask = me ^ i
        ref[(mask & final) * 2 + (mine ^ t), mask >> (size), :, cols] = values[i * share : (i + 1) * share]


def query_mlp_kernel(plan, chunks, shard, *refs):
    ids_ref, res_ref, cols_ref = refs[:3]
    cot_here, sems, refs = refs[-2], refs[-1], refs[3:-2]
    ids = ids_ref[0], ids_ref[1], ids_ref[2]
    b = ids[0]
    if chunks is None:
        w2_ref, cot_ref, refs = refs[0], refs[1], refs[2:]
    else:
        own, got = refs[: len(chunks)], refs[len(chunks) : 2 * len(chunks)]
        cot_ref, w2_ref, refs = refs[2 * len(chunks)], refs[-1], refs[2 * len(chunks) + 1 : -1]
    nseq = cot_here.shape[0]
    copy = pltpu.make_async_copy(cot_ref.at[pl.ds(nseq * (2 * ids[2] + b), nseq)], cot_here, sems.at[0])
    copy.start()
    if chunks is not None:
        place_weights(chunks, own, got, shard, ids, [(w2_ref, 0, 0, w2_ref.shape[3])])
    out_ref, keep_ref, send_ref, dres_ref, vgrad_ref, acc_ref, dn_ref, n2t_ref, gt_ref = refs
    cols = cols_ref[...]
    res = res_ref[...]
    hat, rstd, normed = norm_cols(res, cols[:, 1:2], cols[:, 4:5])
    n2t_ref[...] = normed.astype(BF16)
    rows_low = normed.T.astype(BF16)
    copy.wait()
    cot = cot_here[...].reshape(-1, cot_here.shape[2])
    cot_t = cot.astype(F32).T
    gt_ref[...] = cot_t.astype(BF16)
    acc_ref[...] = res + cols[:, 5:6]
    dn_ref[...] = jnp.zeros_like(dn_ref)
    tensors, width, units = w2_ref.shape[1], w2_ref.shape[2], w2_ref.shape[3]
    chunk = 256
    parts = units // chunk
    half_rows = width // 2

    def step(i, carry):
        t, off = i // parts, pl.multiple_of((i % parts) * chunk, chunk)
        c = pl.ds(off, chunk)
        up, down = w2_ref[0, t, :, c], w2_ref[1, t, :, c]
        pre = nn(rows_low, up)
        d_hidden = nn(cot, down)
        half, bell = gelu_parts(pre)
        hidden = (pre * half).astype(BF16)
        d_pre = (d_hidden * (half + pre * bell * (1.0 / math.sqrt(2.0 * math.pi)))).astype(BF16)
        acc_ref[...] += nt(down, hidden)
        dn_ref[...] += nt(up, d_pre)
        for ref, which in ((keep_ref, b), (send_ref, 1 - b)):
            rows = pl.ds(pl.multiple_of(which * half_rows, 16), half_rows)
            store_grads(plan, ids, ref, t, c, nn(n2t_ref[rows, :], d_pre).astype(BF16))
            later = pl.ds(pl.multiple_of(units + off, chunk), chunk)
            store_grads(plan, ids, ref, t, later, nn(gt_ref[rows, :], hidden).astype(BF16))
        return carry

    lax.fori_loop(0, tensors * parts, step, 0)
    out_ref[...] = acc_ref[...].T.astype(BF16)
    d_n2 = dn_ref[...]
    d_res = cot_t + norm_cols_back(d_n2, hat, rstd, cols[:, 1:2])
    dres_ref[...] = d_res
    lane = lax.broadcasted_iota(jnp.int32, vgrad_ref.shape, 1)
    total = jnp.zeros(vgrad_ref.shape, F32)
    for j, term in ((1, d_n2 * hat), (3, d_res), (4, d_n2), (5, cot_t)):
        total = total + jnp.where(lane == 64 + j, jnp.sum(term, axis=1, keepdims=True), 0.0)
    vgrad_ref[...] = total


def query_back_kernel(plan, nseq, *refs):
    ids_ref, dres_ref, vgrad_ref, cols_ref = refs[:4]
    w1_ref, hat_ref, rstd_ref, normed_ref, q_ref, k_ref, v_ref, inv_ref, ctx_ref, *pb_refs = refs[4 : 13 + nseq]
    refs = refs[13 + nseq :]
    crop_keep_ref, crop_send_ref, keep_ref, send_ref, dctx_ref, dproj_ref, dattn_ref, vg_ref, crop_ref = refs[:9]
    dp_refs, ds_refs, delta_refs = (refs[9 + i * nseq : 9 + (i + 1) * nseq] for i in range(3))
    ids = ids_ref[0], ids_ref[1], ids_ref[2]
    b = ids[0]
    tensors, width = w1_ref.shape[1], w1_ref.shape[2]
    group = width // tensors
    heads_g = group // HD
    heads, slots = pb_refs[0].shape[0], pb_refs[0].shape[1]
    rows = nseq * slots
    d_attn = dres_ref[...].astype(BF16)
    dattn_ref[...] = d_attn
    for t in range(tensors):
        vo = tn(w1_ref[1, t], d_attn).astype(BF16)
        dctx_ref[t * heads_g : (t + 1) * heads_g] = vo[group:].reshape(heads_g, HD, rows)
    dproj_ref[:, 3 * heads_g :] = jnp.zeros((tensors, heads_g, HD, rows), BF16)
    parts = [slice(s * slots, (s + 1) * slots) for s in range(nseq)]
    scale = HD**-0.5

    def d_weights(h, s):
        t, hh = h // heads_g, h % heads_g
        low_ctx = dctx_ref[h, :, parts[s]].astype(F32) * inv_ref[h, 0:1, parts[s]]
        delta = jnp.sum(low_ctx * ctx_ref[t, heads_g + hh, :, parts[s]].astype(F32), axis=0, keepdims=True)
        delta_refs[s][...] = jnp.broadcast_to(delta, (8, slots))
        low_ctx = low_ctx.astype(BF16)
        dp_refs[s][...] = tn(v_ref[h, 0:HD, parts[s]], low_ctx)
        dproj_ref[t, 2 * heads_g + hh, :, parts[s]] = nt(low_ctx, pb_refs[s][h]).astype(BF16)

    def harden(h, s):
        ds_refs[s][...] = (pb_refs[s][h].astype(F32) * (dp_refs[s][...] - delta_refs[s][0:1, :])).astype(BF16)

    def d_inputs(h, s):
        t, hh = h // heads_g, h % heads_g
        d_scores = ds_refs[s][...]
        dproj_ref[t, hh, :, parts[s]] = (nn(k_ref[h, :, parts[s]], d_scores) * scale).astype(BF16)
        dproj_ref[t, heads_g + hh, :, parts[s]] = (nt(q_ref[h, :, parts[s]], d_scores) * scale).astype(BF16)

    def one_head(h, carry):
        for s in range(nseq):
            if s + 1 < nseq:
                d_weights(h, s + 1)
            else:
                d_weights(jnp.minimum(h + 1, heads - 1), 0)
            if s:
                d_inputs(h, s - 1)
            else:
                d_inputs(jnp.maximum(h - 1, 0), nseq - 1)
            harden(h, s)
        return carry

    def some_heads(g, carry):
        for h in range(HEADS_STEP):
            one_head(g * HEADS_STEP + h, carry)
        return carry

    d_weights(0, 0)
    lax.fori_loop(0, heads // HEADS_STEP, some_heads, 0)
    d_inputs(heads - 1, nseq - 1)
    d_normed = jnp.zeros((width, rows), F32)
    for t in range(tensors):
        d_t = dproj_ref[t].reshape(4 * group, rows)
        d_normed += nn(w1_ref[0, t], d_t[: 2 * group]) + nn(w1_ref[1, t], d_t[2 * group :])
    hat = hat_ref[...]
    cols = cols_ref[...]
    crop_ref[...] = dres_ref[...] + norm_cols_back(d_normed, hat, rstd_ref[0:1, :], cols[:, 0:1])
    lane = lax.broadcasted_iota(jnp.int32, vgrad_ref.shape, 1)
    total = vgrad_ref[...]
    for j, term in ((0, d_normed * hat), (2, d_normed)):
        total = total + jnp.where(lane == 64 + j, jnp.sum(term, axis=1, keepdims=True), 0.0)
    vg_ref[...] = total
    half_rows = width // 2
    tile = (3 * group) // 128 * 128
    for ref, which in ((keep_ref, b), (send_ref, 1 - b)):
        part = pl.ds(pl.multiple_of(which * half_rows, 16), half_rows)
        left, right = normed_ref[part, :], dattn_ref[part, :]
        for t in range(tensors):
            d_t = dproj_ref[t].reshape(4 * group, rows)
            grads = nt(left, d_t[: 3 * group + 64])
            outs = nt(right, ctx_ref[t, heads_g:].reshape(group, rows))
            outs = jnp.concatenate([outs, jnp.zeros((half_rows, 64), F32)], axis=1)
            grads = jnp.concatenate([grads[:, :tile], grads[:, tile:] + vg_ref[part, :], outs], axis=1)
            store_grads(plan, ids, ref, t, slice(None), grads.astype(BF16))
    for s in range(nseq):
        part = slice(s * slots, (s + 1) * slots)
        crop_keep_ref[s] = crop_ref[pl.ds(pl.multiple_of(b * half_rows, 16), half_rows), part]
        crop_send_ref[s] = crop_ref[pl.ds(pl.multiple_of((1 - b) * half_rows, 16), half_rows), part].astype(BF16)


def chip_sum_kernel(keep_ref, got_ref, own_ref, *sends):
    total = keep_ref[...].astype(F32) + got_ref[...].astype(F32)
    own_ref[...] = total[0]
    for j, ref in enumerate(sends):
        ref[...] = total[1 + j].astype(BF16)


def half_sum_kernel(keep_ref, got_ref, own_ref, send_ref):
    half = own_ref.shape[0]
    own_ref[...] = keep_ref[:half].astype(F32) + got_ref[:half].astype(F32)
    send_ref[...] = (keep_ref[half:].astype(F32) + got_ref[half:].astype(F32)).astype(BF16)


def x_sum_kernel(own_ref, got_ref, keep_ref, send_ref):
    total = own_ref[...] + got_ref[...].astype(F32)
    keep_ref[...] = total[0]
    send_ref[...] = total[1].astype(BF16)


def near_sum_kernel(*refs):
    mlp, attn, own_ref, sends = refs[:2], refs[2:6], refs[6], refs[7:]
    wide = mlp[0].shape[2]
    for part, cols in ((mlp, slice(0, wide)), (attn, slice(wide, None))):
        total = part[0][...]
        for ref in part[1:]:
            total = total + ref[...].astype(F32)
        own_ref[:, cols] = total[0]
        for k, ref in enumerate(sends):
            ref[:, cols] = total[1 + k].astype(BF16)


def shares_kernel(units, group, *refs):
    own_ref, got, (qkv_ref, out_ref, up_ref, down_ref, gain_ref, bias_ref) = refs[0], refs[1:-6], refs[-6:]
    total = own_ref[...]
    for ref in got:
        total = total + ref[...].astype(F32)
    up_ref[...] = total[:, :units]
    down_ref[...] = total[:, units : 2 * units]
    attn = total[:, 2 * units :]
    for j in range(3):
        qkv_ref[j] = attn[:, j * group : (j + 1) * group]
    tile = 3 * group // 128 * 128
    vec = attn[:, tile : tile + 128]
    share = vec.shape[0]
    vec = jnp.concatenate([vec, jnp.zeros((128 - share, 128), F32)], axis=0).T
    gain_ref[...] = vec[64:66, :share]
    bias_ref[...] = vec[66:70, :share]
    out_ref[...] = attn[:, tile + 128 : tile + 128 + group]


def crop_pair_kernel(ids_ref, keep_ref, got_ref, pair_ref):
    b = ids_ref[0]
    pair_ref[b] = keep_ref[...].astype(BF16)
    pair_ref[1 - b] = got_ref[...]


def crop_kernel(ids_ref, keep_ref, got_ref, far_ref, out_ref):
    b, t = ids_ref[0], ids_ref[2]
    out_ref[t, b] = keep_ref[...]
    out_ref[t, 1 - b] = got_ref[...].astype(F32)
    out_ref[1 - t] = far_ref[...].astype(F32)


def pick_kernel(ids_ref, query_ref, momentum_ref, own_ref, send_ref):
    first = ids_ref[0] == 0
    own_ref[...] = jnp.where(first, momentum_ref[...], query_ref[...])
    send_ref[...] = jnp.where(first, query_ref[...], momentum_ref[...])


def encoded_kernel(ids_ref, own_ref, own_far, got_ref, got_far, out_ref, sems):
    b, t = ids_ref[0], ids_ref[2]
    places = ((own_ref, t, b), (own_far, 1 - t, b), (got_ref, t, 1 - b), (got_far, 1 - t, 1 - b))
    copies = [pltpu.make_async_copy(part, out_ref.at[i, j], sems.at[n]) for n, (part, i, j) in enumerate(places)]
    for copy in copies:
        copy.start()
    for copy in copies:
        copy.wait()


def call(kernel, out_shapes, scratch, args, smem=0, hbm=0, hbm_outs=0, copies=0, stream=False, limit=24):
    place, hold = pl.BlockSpec(memory_space=pltpu.VMEM), pl.BlockSpec(memory_space=pltpu.HBM)
    inner = args[smem : len(args) - hbm]
    if stream:
        specs = [pl.BlockSpec(x.shape, lambda i, n=x.ndim: (0,) * n) for x in inner]
    else:
        specs = [place] * len(inner)
    return pl.pallas_call(
        kernel,
        grid=(1,) if stream else (),
        out_shape=[jax.ShapeDtypeStruct(s, d) for s, d in out_shapes],
        in_specs=[pl.BlockSpec(memory_space=pltpu.SMEM)] * smem + specs + [hold] * hbm,
        out_specs=[place] * (len(out_shapes) - hbm_outs) + [hold] * hbm_outs,
        scratch_shapes=[pltpu.VMEM(s, d) for s, d in scratch]
        + ([pltpu.SemaphoreType.DMA((copies,))] if copies else []),
        compiler_params=pltpu.CompilerParams(vmem_limit_bytes=limit * 1024 * 1024),
    )(*args)


SPAN = ("dp", "tensor")


def swap_cores(block):
    return lax.ppermute(block, "branch", [(0, 1), (1, 0)])


def exchange(block, dp_mask, t_mask):
    dp, tensors = lax.axis_size("dp"), lax.axis_size("tensor")
    pairs = [
        (i * tensors + t, (i ^ dp_mask) * tensors + (t ^ t_mask)) for i in range(dp) for t in range(tensors)
    ]
    return lax.ppermute(block, SPAN, pairs)


def after(value, *deps):
    return lax.optimization_barrier((value, *deps))[0]


def dp_groups():
    bits = lax.axis_size("dp").bit_length() - 1
    groups, high = [], bits
    while high >= 2:
        high -= 2
        groups.append((high, 4))
    last = (0, 2) if high == 1 else None
    return groups, last


def put(whole, block, index):
    return lax.dynamic_update_slice(whole, block, index)


def gather(block):
    groups, last = dp_groups()
    me, t = lax.axis_index("dp"), lax.axis_index("tensor")
    tensors = lax.axis_size("tensor")
    for number, (shift, size) in enumerate(groups):
        lead, tail = block.shape[:number], block.shape[number:]
        whole = jnp.zeros(lead + (size,) + tail, block.dtype)
        mine = (me >> shift) & (size - 1)
        pieces = [(0, block)] + [(k, exchange(block, k << shift, 0)) for k in range(1, size)]
        for k, piece in pieces:
            whole = put(whole, jnp.expand_dims(piece, number), (0,) * number + (mine ^ k,) + (0,) * len(tail))
        block = whole
    lead, tail = block.shape[: len(groups)], block.shape[len(groups) :]
    size = last[1] if last else 1
    mine = me & (size - 1)
    whole = jnp.zeros((tensors,) + lead + (size,) + tail, block.dtype)
    for k in range(size):
        for u in range(tensors):
            piece = block if k == u == 0 else exchange(block, k, u)
            piece = jnp.expand_dims(jnp.expand_dims(piece, len(lead)), 0)
            whole = put(whole, piece, (t ^ u,) + (0,) * len(lead) + (mine ^ k,) + (0,) * len(tail))
    return whole.reshape((tensors, lax.axis_size("dp")) + tail)


def scatter_sum(block):
    groups, last = dp_groups()
    me, t = lax.axis_index("dp"), lax.axis_index("tensor")
    tensors = lax.axis_size("tensor")
    tail = block.shape[2:]
    size = last[1] if last else 1
    lead = tuple(g[1] for g in groups)
    block = block.reshape((tensors,) + lead + (size,) + tail)
    mine = me & (size - 1)

    def take(k, u):
        start = (t ^ u,) + (0,) * len(lead) + (mine ^ k,) + (0,) * len(tail)
        piece = lax.dynamic_slice(block, start, (1,) + lead + (1,) + tail)
        return piece.reshape(lead + tail)

    total = take(0, 0).astype(F32)
    for k in range(size):
        for u in range(tensors):
            if k or u:
                total = total + exchange(take(k, u), k, u).astype(F32)
    for number in reversed(range(len(groups))):
        shift, size = groups[number]
        mine = (me >> shift) & (size - 1)
        low = total.astype(BF16)

        def part(k, whole=low, number=number, mine=mine):
            return lax.dynamic_index_in_dim(whole, mine ^ k, number, keepdims=False)

        total = part(0, total).astype(F32)
        for k in range(1, size):
            total = total + exchange(part(k), k << shift, 0).astype(F32)
    return total


def stack_peers(block, stage):
    return jnp.stack([block] + [exchange(block, *peer) for peer in stage]), [(0, 0)] + stage


def chunks_of(block, masks, stage):
    pieces = [((0, 0), block)] + [(peer, exchange(block, *peer)) for peer in stage]
    return [
        (piece, [((j,), (m ^ peer[0], u ^ peer[1])) for j, (m, u) in enumerate(masks)]) for peer, piece in pieces
    ]


def gathered(shards, on_query, me, tensors, width, units):
    qkv, out_t, up, down_t, gains, biases = shards
    shard = up.shape[0]
    small = jnp.concatenate([gains, biases], axis=0).astype(BF16)
    vec_rows = put(jnp.zeros((8, width), BF16), small, (0, me * shard))
    half_0 = jnp.concatenate([qkv[0], qkv[1]], axis=1).astype(BF16)
    half_1 = jnp.concatenate([qkv[2], out_t], axis=1).astype(BF16)
    half_0, half_1 = (jnp.concatenate([half, vec_rows], axis=0) for half in (half_0, half_1))
    mlp_0, mlp_1 = up.astype(BF16), down_t.astype(BF16)

    def finish(first, second):
        keep, got = jnp.where(on_query, first, second), swap_cores(jnp.where(on_query, second, first))
        both = []
        for block in (jnp.where(on_query, keep, got), jnp.where(on_query, got, keep)):
            own = gather(block)
            other = swap_cores(own)
            both.append(jnp.stack([jnp.where(on_query, own, other), jnp.where(on_query, other, own)]))
        return both

    def parts_of(whole):
        vec = jnp.sum(whole[0, 0, :, shard:].astype(F32), axis=0)
        return whole[:, :, :, :shard].reshape(2, tensors, width, width), vec

    (wq_1, vec_q), (wm_1, vec_m) = (parts_of(whole) for whole in finish(half_0, half_1))
    wq_2, wm_2 = (whole.reshape(2, tensors, width, units) for whole in finish(mlp_0, mlp_1))
    return [wq_1, vec_q, wm_1, vec_m], [wq_2], [wm_2]


def on_device(
    crops, segment_ids, cotangent, qkv_weight, out_weight, up_weight, down_weight, gain_rows, biases
):
    branch, me, t = lax.axis_index("branch"), lax.axis_index("dp"), lax.axis_index("tensor")
    dp, tensors = lax.axis_size("dp"), lax.axis_size("tensor")
    on_query = branch == 0
    _, sequences, slots, width = crops.shape
    nseq = sequences // (2 * tensors)
    rows = nseq * slots
    shard = qkv_weight.shape[1]
    group = out_weight.shape[1]
    units = up_weight.shape[2]
    heads = tensors * group // HD
    heads_g = group // HD
    share = width // (2 * dp)
    ids = jnp.stack([branch, me, t]).astype(jnp.int32)
    fine = tensors == 2 and dp == 8 and shard % 16 == 0
    near = [(k << 1, 0) for k in range(1, 4)]
    both_ways = [(1, 0), (0, 1), (1, 1)]

    w1_shape, w2_shape = (2, tensors, width, width), (2, tensors, width, units)
    head_block = ((heads, HD, rows), BF16)
    v_block = ((heads, HD + 16, rows), BF16)
    ctx_block = ((tensors, 2 * heads_g, HD, rows), BF16)
    bias_block = ((nseq, slots, slots), F32)
    score_block, pb_block = ((slots, slots), F32), ((heads, slots, slots), BF16)
    col_block, vec_block = ((width, 128), F32), ((128, width), F32)
    crop_block = ((nseq, slots, width), BF16)
    wide_f, wide_b = ((width, rows), F32), ((width, rows), BF16)
    kept = [(w1_shape, BF16), wide_f, ((8, rows), F32), wide_b, head_block, head_block, v_block]
    kept = kept + [((heads, 8, rows), F32), ctx_block] + [pb_block] * nseq
    grads_1, grads_2 = (tensors, width // 2, 4 * group + 128), (tensors, width // 2, 2 * units)
    scatter = None
    if fine:
        grads_1, grads_2 = (4, dp // 2, share, grads_1[2]), (4, dp // 2, share, grads_2[2])
        scatter = (dp, 1)

    def attention(plan, weights, got_crops):
        return call(
            functools.partial(attention_kernel, plan, shard),
            [wide_f, wide_f, col_block] + kept,
            [score_block] * nseq
            + [pb_block] * nseq
            + [head_block, head_block, v_block, ctx_block, bias_block, crop_block]
            + [(w1_shape, BF16) if plan else vec_block],
            (ids, got_crops, segment_ids, *weights, crops[0]),
            smem=1,
            hbm=1,
            copies=1,
        )

    def query_mlp(plan, weights, res, cols):
        return call(
            functools.partial(query_mlp_kernel, scatter, plan, shard),
            [((rows, width), BF16), (grads_2, BF16), (grads_2, BF16), wide_f, col_block],
            [wide_f, wide_f, wide_b, wide_b] + ([(w2_shape, BF16)] if plan else []) + [crop_block],
            (ids, res, cols, *weights, cotangent),
            smem=1,
            hbm=1,
            copies=1,
        )

    def query_back(d_res, vgrad, cols, saved):
        return call(
            functools.partial(query_back_kernel, scatter, nseq),
            [((nseq, width // 2, slots), F32), ((nseq, width // 2, slots), BF16), (grads_1, BF16), (grads_1, BF16)],
            [head_block, ((tensors, 4 * heads_g, HD, rows), BF16), wide_b, col_block, wide_f]
            + [score_block] * nseq
            + [((slots, slots), BF16)] * nseq
            + [((8, slots), F32)] * nseq,
            (ids, d_res, vgrad, cols, *saved),
            smem=1,
        )

    def momentum_mlp(plan, weights, res_m, cols, out_q):
        return call(
            functools.partial(momentum_mlp_kernel, plan, shard),
            [((rows, width), BF16)] * 3,
            [wide_f] + ([(w2_shape, BF16)] if plan else []),
            (ids, res_m, cols, out_q, *weights),
            smem=1,
        )

    shards = (
        qkv_weight[0].transpose(1, 0, 2),
        out_weight[0].T,
        up_weight[0],
        down_weight[0].T,
        gain_rows[0],
        biases[0],
    )
    other = nseq * (2 * t + 1 - branch)
    send_crops = lax.dynamic_slice(crops[0], (other, 0, 0), (nseq, slots, width)).reshape(rows, width)

    if fine:
        block = ((shard, width + 128 + units), BF16)
        keep, send = call(
            pack_kernel, [block] * 2, [(x.shape, F32) for x in shards], (ids, *shards), smem=1, hbm=6, copies=6, limit=56
        )
        block_1, block_2 = call(
            functools.partial(split_kernel, width),
            [((shard, 2 * width + 128), BF16), ((shard, 2 * units), BF16)],
            [block],
            (ids, swap_cores(send), keep),
            smem=1,
            hbm=1,
            copies=1,
        )
        masks = [(0, 0)] + near
        plan = [[((j,), (m ^ n, u)) for j, (m, _) in enumerate(masks)] for n, u in [(0, 0)] + both_ways]
        got_crops = swap_cores(send_crops)
        far_1 = [exchange(block_1, *peer) for peer in near]
        stack_1, got_crops = after((jnp.stack([block_1, *far_1]), got_crops))
        own_1 = [stack_1] + [exchange(stack_1, *peer) for peer in both_ways]
        got_1 = [swap_cores(x) for x in own_1]
        parts = [block_2] + [exchange(block_2, *peer) for peer in near]
        stack_q, stack_m = (jnp.stack([x[..., cols] for x in parts]) for cols in (slice(0, units), slice(units, None)))
        own_q = [stack_q] + [exchange(stack_q, *peer) for peer in both_ways]
        res, res_m, cols, *saved = attention(plan, own_1 + got_1, after(got_crops, stack_q, stack_m))
        own_q, res, res_m, stack_m = after((own_q, res, res_m, stack_m))
        got_q = [swap_cores(x) for x in own_q]
        own_m = [stack_m] + [exchange(stack_m, *peer) for peer in both_ways]
        out_q, keep_g2, send_g2, d_res, vgrad = query_mlp(plan, own_q + got_q, res, cols)
        own_m, out_q, keep_g2, send_g2, d_res, vgrad = after((own_m, out_q, keep_g2, send_g2, d_res, vgrad))
        got_m = [swap_cores(x) for x in own_m]

        part = (2, dp // 2, share, 2 * units)
        mlp_own, mlp_send = call(half_sum_kernel, [(part, F32), (part, BF16)], [], (keep_g2, swap_cores(send_g2)))
        mlp_got = exchange(mlp_send, 1, 0)
        far_q = exchange(out_q, 0, 1)
        res_m = after(res_m, mlp_own)
        out_m, out_own, out_send = momentum_mlp(plan, own_m + got_m, res_m, cols, out_q)
        far_q, out_m, out_send = after((far_q, out_m, out_send))
        far_m = exchange(out_m, 0, 1)
        crop_keep, crop_send, keep_g1, send_g1 = query_back(after(d_res, out_m), vgrad, cols, saved)
        mlp_got, far_m, crop_send, send_g1 = after((mlp_got, far_m, crop_send, send_g1))
        part = (dp // 2, share, 2 * units)
        mlp_own, mlp_send = call(x_sum_kernel, [(part, F32), (part, BF16)], [], (mlp_own, mlp_got))
        mlp_got = exchange(mlp_send, 0, 1)
        part = (dp // 2, share, grads_1[3])
        attn_own, *attn_sends = call(
            chip_sum_kernel, [(part, F32)] + [(part, BF16)] * 3, [], (keep_g1, swap_cores(send_g1))
        )
        attn_got = [exchange(x, *peer) for x, peer in zip(attn_sends, [(0, 1), (1, 0), (1, 1)])]
        half = (nseq, width // 2, slots)
        crop_got = swap_cores(crop_send)
        (pair,) = call(crop_pair_kernel, [((2, *half), BF16)], [], (ids, crop_keep, crop_got), smem=1)
        attn_got, mlp_got, pair = after((attn_got, mlp_got, pair))
        crop_far = exchange(pair, 0, 1)
        wide = 2 * units + grads_1[3]
        own, *sends = call(
            near_sum_kernel,
            [((share, wide), F32)] + [((share, wide), BF16)] * 3,
            [],
            (mlp_own, mlp_got, attn_own, *attn_got),
        )
        got = [exchange(x, *peer) for x, peer in zip(sends, near)]
        qkv_grad, out_grad, up_grad, down_grad, gain_grad, bias_grad = call(
            functools.partial(shares_kernel, units, group),
            [
                ((3, share, group), F32),
                ((share, group), F32),
                ((share, units), F32),
                ((share, units), F32),
                ((2, share), F32),
                ((4, share), F32),
            ],
            [],
            (own, *got),
        )
        qkv_grad, out_grad, down_grad = qkv_grad.transpose(1, 0, 2), out_grad.T, down_grad.T
        (crop_grad,) = call(
            crop_kernel, [((tensors, 2, *half), F32)], [], (ids, crop_keep, crop_got, crop_far), smem=1
        )
        crop_grad = crop_grad.reshape(sequences, width // 2, slots).transpose(0, 2, 1)
        far_own, far_send = call(pick_kernel, [((rows, width), BF16)] * 2, [], (ids, far_q, far_m), smem=1)
        (encoded,) = call(
            encoded_kernel,
            [((tensors, 2, rows, width), BF16)],
            [],
            (ids, out_own, far_own, swap_cores(out_send), swap_cores(far_send)),
            smem=1,
            hbm=4,
            hbm_outs=1,
            copies=4,
        )
        encoded = encoded.reshape(1, sequences, slots, width)
        return (encoded, crop_grad, qkv_grad, out_grad, up_grad, down_grad, gain_grad, bias_grad)

    weights_1, weights_2, weights_4 = gathered(shards, on_query, me, tensors, width, units)
    got_crops = swap_cores(send_crops)
    res, res_m, cols, *saved = attention(None, weights_1, got_crops)
    out_q, keep_g2, send_g2, d_res, vgrad = query_mlp(None, weights_2, res, cols)
    crop_keep, crop_send, keep_g1, send_g1 = query_back(d_res, vgrad, cols, saved)
    _, out_own, out_send = momentum_mlp(None, weights_4, res_m, cols, out_q)

    def shares(keep, send):
        both = (keep.astype(F32) + swap_cores(send).astype(F32)).astype(BF16)
        return scatter_sum(both.reshape(tensors, dp, share, both.shape[-1]))

    mlp_share, attn_share = shares(keep_g2, send_g2), shares(keep_g1, send_g1)
    qkv_grad = attn_share[:, : 3 * group].reshape(share, 3, group)
    vec_grad = attn_share[:, 3 * group : 3 * group + 6].T
    out_grad = attn_share[:, 3 * group + 64 : 4 * group + 64].T
    up_grad, down_grad = mlp_share[:, :units], mlp_share[:, units:].T

    mine = (2, nseq, width // 2, slots)
    pair = jnp.zeros(mine, F32)
    pair = put(pair, crop_keep[None], (branch, 0, 0, 0))
    pair = put(pair, swap_cores(crop_send).astype(F32)[None], (1 - branch, 0, 0, 0))
    far = exchange(pair.astype(BF16), 0, 1)
    crop_grad = jnp.zeros((tensors,) + mine, F32)
    crop_grad = put(crop_grad, pair[None], (t, 0, 0, 0, 0))
    crop_grad = put(crop_grad, far.astype(F32)[None], (1 - t, 0, 0, 0, 0))
    crop_grad = crop_grad.reshape(sequences, width // 2, slots).transpose(0, 2, 1)

    pair = jnp.zeros((2, rows, width), BF16)
    pair = put(put(pair, out_own[None], (branch, 0, 0)), swap_cores(out_send)[None], (1 - branch, 0, 0))
    encoded = jnp.zeros((tensors, 2, rows, width), BF16)
    encoded = put(encoded, pair[None], (t, 0, 0, 0))
    encoded = put(encoded, exchange(pair, 0, 1)[None], (1 - t, 0, 0, 0))
    encoded = encoded.reshape(1, sequences, slots, width)

    return (encoded, crop_grad, qkv_grad, out_grad, up_grad, down_grad, vec_grad[:2], vec_grad[2:])


def solution(mesh):
    placed = (
        P("branch", "dp", None, None),
        P(None, "dp", None),
        P("dp", None, None),
        P("branch", "dp", None, "tensor"),
        P("branch", "tensor", "dp"),
        P("branch", "dp", "tensor"),
        P("branch", "tensor", "dp"),
        P("branch", None, "dp"),
        P("branch", None, "dp"),
    )
    return jax.shard_map(
        on_device,
        mesh=mesh,
        in_specs=placed,
        out_specs=(
            P("branch", "dp", None, None),
            P("dp", None, "branch"),
            P(("branch", "dp"), None, "tensor"),
            P("tensor", ("branch", "dp")),
            P(("branch", "dp"), "tensor"),
            P("tensor", ("branch", "dp")),
            P(None, ("branch", "dp")),
            P(None, ("branch", "dp")),
        ),
        check_vma=False,
    )
```

```python
import functools
import math

import jax
import jax.numpy as jnp
from jax import lax
from jax.experimental import pallas as pl
from jax.experimental.pallas import tpu as pltpu
from jax.sharding import PartitionSpec as P

HD = 32
HEADS_STEP = 4
EPSILON = 1e-06
MASKED_SCORE = -1e30
LOG2E = 1.4426950408889634
BF16 = jnp.bfloat16
F32 = jnp.float32
PACE = 3600000


def nn(left, right):
    return lax.dot_general(left, right, (((1,), (0,)), ((), ())), preferred_element_type=F32)


def nt(left, right):
    return lax.dot_general(left, right, (((1,), (1,)), ((), ())), preferred_element_type=F32)


def tn(left, right):
    return lax.dot_general(left, right, (((0,), (0,)), ((), ())), preferred_element_type=F32)


def place():
    return lax.axis_index("branch"), lax.axis_index("dp"), lax.axis_index("tensor")


def gelu_parts(v):
    a = jnp.abs(v)
    t = 1.0 / (1.0 + (0.3275911 / math.sqrt(2.0)) * a)
    bell = jnp.exp2(v * v * (-0.5 * LOG2E))
    poly = t * (
        0.5 * 0.254829592
        + t * (0.5 * -0.284496736 + t * (0.5 * 1.421413741 + t * (0.5 * -1.453152027 + t * (0.5 * 1.061405429))))
    )
    tail = poly * bell
    return jnp.where(v < 0, tail, 1.0 - tail), bell


def norm_cols(values, gain, shift):
    centred = values - jnp.mean(values, axis=0, keepdims=True)
    spread = jnp.mean(centred * centred, axis=0, keepdims=True)
    rstd = lax.rsqrt(spread + EPSILON)
    hat = centred * rstd
    return hat, rstd, hat * gain + shift


def norm_cols_back(upstream, hat, rstd, gain):
    t = upstream * gain
    return rstd * (t - jnp.mean(t, axis=0, keepdims=True) - hat * jnp.mean(t * hat, axis=0, keepdims=True))


def columns_of(query_ref, momentum_ref, scratch):
    scratch[...] = jnp.zeros_like(scratch)
    scratch[0:8, :] = query_ref[...]
    scratch[8:16, :] = momentum_ref[...]
    return scratch[...].T


def place_columns(plan, chunk_refs, shard, width, me, cols_ref):
    for ref, spots in zip(chunk_refs, plan):
        for index, (mask, u) in spots:
            if u == 0:
                rows = pl.ds(pl.multiple_of((me ^ mask) * shard, 16), shard)
                cols_ref[rows, :] = ref[index + (slice(None), slice(width, width + 128))].astype(F32)


def place_weights(plan, own_refs, got_refs, shard, ids, targets):
    b, me, t = ids
    for half, refs in ((b, own_refs), (1 - b, got_refs)):
        for ref, spots in zip(refs, plan):
            for index, (mask, u) in spots:
                rows = pl.ds(pl.multiple_of((me ^ mask) * shard, 16), shard)
                for target, to, start, wide in targets:
                    block = ref[index + (slice(0, shard), slice(start, start + wide))]
                    target[half, t ^ u, rows, to : to + wide] = block


def attend(x, segs, w1_ref, cols, q_ref, k_ref, v_ref, bias_ref, ctx_ref, pb_refs, inv_ref, score_refs, keep=None):
    tensors, width = w1_ref.shape[1], w1_ref.shape[2]
    group = width // tensors
    heads_g = group // HD
    nseq, slots = len(segs), segs[0].shape[1]
    x_t = x.astype(F32).T
    hat, rstd, normed = norm_cols(x_t, cols[:, 0:1], cols[:, 2:3])
    normed_low = normed.astype(BF16)
    if keep is not None:
        keep(hat, rstd, normed_low)
    rows = x_t.shape[1]
    for t in range(tensors):
        qk = tn(w1_ref[0, t], normed_low).astype(BF16)
        q_ref[t * heads_g : (t + 1) * heads_g] = qk[:group].reshape(heads_g, HD, rows)
        k_ref[t * heads_g : (t + 1) * heads_g] = qk[group:].reshape(heads_g, HD, rows)
        vo = tn(w1_ref[1, t], normed_low).astype(BF16)
        v_ref[t * heads_g : (t + 1) * heads_g, 0:HD] = vo[:group].reshape(heads_g, HD, rows)
    v_ref[:, HD:, :] = jnp.ones((v_ref.shape[0], v_ref.shape[1] - HD, rows), BF16)
    for s in range(nseq):
        across = jnp.broadcast_to(segs[s].astype(F32), (slots, slots))
        bias_ref[s] = jnp.where(across == across.T, 0.0, MASKED_SCORE)
    heads = tensors * heads_g
    parts = [slice(s * slots, (s + 1) * slots) for s in range(nseq)]
    ctx_ref[:, :heads_g] = jnp.zeros((tensors, heads_g, HD, rows), BF16)

    def score(h, s):
        score_refs[s][...] = tn(k_ref[h, :, parts[s]], q_ref[h, :, parts[s]])

    def soften(h, s):
        scores = score_refs[s][...] + bias_ref[s]
        top = jnp.max(scores, axis=0, keepdims=True)
        pb_refs[s][h] = jnp.exp2((scores - top) * (HD**-0.5 * LOG2E)).astype(BF16)

    def blend(h, s):
        both = nn(v_ref[h, :, parts[s]], pb_refs[s][h])
        inv = 1.0 / both[HD : HD + 1]
        if inv_ref is not None:
            inv_ref[h, :, parts[s]] = jnp.broadcast_to(inv, (8, slots))
        ctx_ref[h // heads_g, heads_g + h % heads_g, :, parts[s]] = (both[:HD] * inv).astype(BF16)

    def one_head(h, carry):
        for s in range(nseq):
            if s + 1 < nseq:
                score(h, s + 1)
            else:
                score(jnp.minimum(h + 1, heads - 1), 0)
            if s:
                blend(h, s - 1)
            else:
                blend(jnp.maximum(h - 1, 0), nseq - 1)
            soften(h, s)
        return carry

    score(0, 0)

    def some_heads(g, carry):
        for h in range(HEADS_STEP):
            one_head(g * HEADS_STEP + h, carry)
        return carry

    lax.fori_loop(0, heads // HEADS_STEP, some_heads, 0)
    blend(heads - 1, nseq - 1)
    attn = sum(nn(w1_ref[1, t], ctx_ref[t].reshape(width, rows)) for t in range(tensors))
    return x_t, attn


def pack_kernel(*refs):
    far, keep_ref, send_ref, near, sems = refs[:6], refs[6], refs[7], refs[8:14], refs[14]
    copies = [pltpu.make_async_copy(there, here, sems.at[i]) for i, (there, here) in enumerate(zip(far, near))]
    for copy in copies:
        copy.start()
    qkv_ref, out_ref, up_ref, down_ref, gain_ref, bias_ref = near
    first = lax.axis_index("branch") == 0
    shard, width = up_ref.shape[0], 2 * out_ref.shape[1]
    for copy in copies:
        copy.wait()
    vec = jnp.concatenate([gain_ref[...], bias_ref[...], jnp.zeros((2, shard), F32)], axis=0)
    vec = jnp.concatenate([vec, jnp.zeros((8, 128 - shard), F32)], axis=1)
    none = jnp.zeros((8, 128), F32)
    vec = jnp.concatenate([jnp.where(first, vec, none), jnp.where(first, none, vec), jnp.zeros((112, 128), F32)], axis=0)
    vec = vec.T[:shard, :].astype(BF16)
    half_0 = jnp.concatenate([qkv_ref[0], qkv_ref[1]], axis=1).astype(BF16)
    half_1 = jnp.concatenate([qkv_ref[2], out_ref[...]], axis=1).astype(BF16)
    up, down = up_ref[...].astype(BF16), down_ref[...].astype(BF16)
    for ref, is_first in ((keep_ref, first), (send_ref, jnp.logical_not(first))):
        ref[:, :width] = jnp.where(is_first, half_0, half_1)
        ref[:, width : width + 128] = vec
        ref[:, width + 128 :] = jnp.where(is_first, up, down)


def split_kernel(width, got_ref, far_ref, first_ref, second_ref, keep_ref, sems):
    copy = pltpu.make_async_copy(far_ref, keep_ref, sems.at[0])
    copy.start()
    first = lax.axis_index("branch") == 0
    got = got_ref[...]
    copy.wait()
    keep = keep_ref[...]
    query, momentum = jnp.where(first, keep, got), jnp.where(first, got, keep)
    units = second_ref.shape[1] // 2
    first_ref[:, :width] = query[:, :width]
    first_ref[:, width : width + 128] = keep[:, width : width + 128] + got[:, width : width + 128]
    first_ref[:, width + 128 :] = momentum[:, :width]
    second_ref[:, :units] = query[:, width + 128 :]
    second_ref[:, units:] = momentum[:, width + 128 :]


def attention_kernel(plan, shard, *refs):
    got_crops, seg_ref, refs = refs[0], refs[1], refs[2:]
    ids = place()
    slots = seg_ref.shape[2]
    nseq = got_crops.shape[0] // slots
    if plan is None:
        w1_given, vec_q, w1_m, vec_m = refs[:4]
        refs = refs[4:]
    else:
        own, got = refs[: len(plan)], refs[len(plan) : 2 * len(plan)]
        refs = refs[2 * len(plan) :]
    crops_ref, res_ref, res_m_ref, cols_ref, refs = refs[0], refs[1], refs[2], refs[3], refs[4:]
    w1_ref, hat_ref, rstd_ref, normed_ref, q_ref, k_ref, v_ref, inv_ref, ctx_ref, *pb_refs = refs[: 9 + nseq]
    refs = refs[9 + nseq :]
    score_refs, pb_m, refs = refs[:nseq], refs[nseq : 2 * nseq], refs[2 * nseq :]
    q_m, k_m, v_m, ctx_m, bias_ref, mine_ref, spare, sems = refs
    first = nseq * (2 * ids[2] + ids[0])
    copy = pltpu.make_async_copy(crops_ref.at[pl.ds(first, nseq)], mine_ref, sems.at[0])
    copy.start()
    if plan is None:
        w1_ref[...] = w1_given[...]
        cols_ref[...] = columns_of(vec_q, vec_m, spare)
    else:
        wide, w1_m = w1_ref.shape[3], spare
        place_columns(plan, own, shard, wide, ids[1], cols_ref)
        place_weights(plan, own, got, shard, ids, [(w1_ref, 0, 0, wide), (w1_m, 0, wide + 128, wide)])
    cols = cols_ref[...]

    def keep(hat, rstd, normed):
        hat_ref[...] = hat
        rstd_ref[...] = jnp.broadcast_to(rstd, rstd_ref.shape)
        normed_ref[...] = normed

    copy.wait()

    def rows_of(encoder):
        mine = mine_ref[...].reshape(got_crops.shape)
        segs = [seg_ref[1 - encoder, pl.ds(first + s, 1), :] for s in range(nseq)]
        return jnp.where(ids[0] == encoder, got_crops[...], mine), segs

    x_t, attn = attend(
        *rows_of(0), w1_ref, cols, q_ref, k_ref, v_ref, bias_ref, ctx_ref, pb_refs, inv_ref, score_refs, keep
    )
    res_ref[...] = x_t + attn + cols[:, 3:4]
    cols = cols[:, 8:]
    x_t, attn = attend(*rows_of(1), w1_m, cols, q_m, k_m, v_m, bias_ref, ctx_m, pb_m, None, score_refs)
    res_m_ref[...] = x_t + attn + cols[:, 3:4]


def momentum_mlp_kernel(plan, shard, *refs):
    res_ref, cols_ref, query_ref, refs = refs[0], refs[1], refs[2], refs[3:]
    ids = place()
    cols = cols_ref[...][:, 8:]
    if plan is None:
        w2_ref, out_ref, own_ref, send_ref, acc_ref = refs
    else:
        count = sum(len(part) for part in plan)
        own, got = refs[:count], refs[count : 2 * count]
        out_ref, own_ref, send_ref, acc_ref, w2_ref = refs[2 * count :]
        at, wide = 0, own[0].shape[-1]
        for i, part in enumerate(plan):
            targets = [(w2_ref, i * wide, 0, wide)]
            place_weights(part, own[at : at + len(part)], got[at : at + len(part)], shard, ids, targets)
            at += len(part)
    res = res_ref[...]
    _, _, normed = norm_cols(res, cols[:, 1:2], cols[:, 4:5])
    rows_low = normed.T.astype(BF16)
    acc_ref[...] = res + cols[:, 5:6]
    tensors, units = w2_ref.shape[1], w2_ref.shape[3]
    chunk = 256
    parts = units // chunk

    def step(i, carry):
        t, c = i // parts, pl.ds(pl.multiple_of((i % parts) * chunk, chunk), chunk)
        pre = nn(rows_low, w2_ref[0, t, :, c])
        half, _ = gelu_parts(pre)
        acc_ref[...] += nt(w2_ref[1, t, :, c], (pre * half).astype(BF16))
        return carry

    lax.fori_loop(0, tensors * parts, step, 0, unroll=6)
    momentum, query = acc_ref[...].T.astype(BF16), query_ref[...]
    first = ids[0] == 0
    out_ref[...] = momentum
    own_ref[...] = jnp.where(first, momentum, query)
    send_ref[...] = jnp.where(first, query, momentum)


def store_grads(plan, ids, ref, t, cols, values):
    if plan is None:
        ref[t, :, cols] = values
        return
    dp, final = plan
    me, mine = ids[1], ids[2]
    share = values.shape[0] // dp
    size = final.bit_length()
    for i in range(dp):
        mask = me ^ i
        ref[(mask & final) * 2 + (mine ^ t), mask >> (size), :, cols] = values[i * share : (i + 1) * share]


def query_mlp_kernel(plan, chunks, shard, *refs):
    res_ref, cols_ref = refs[:2]
    cot_here, sems, refs = refs[-2], refs[-1], refs[2:-2]
    ids = place()
    b = ids[0]
    if chunks is None:
        w2_ref, cot_ref, refs = refs[0], refs[1], refs[2:]
    else:
        own, got = refs[: len(chunks)], refs[len(chunks) : 2 * len(chunks)]
        cot_ref, w2_ref, refs = refs[2 * len(chunks)], refs[-1], refs[2 * len(chunks) + 1 : -1]
    nseq = cot_here.shape[0]
    copy = pltpu.make_async_copy(cot_ref.at[pl.ds(nseq * (2 * ids[2] + b), nseq)], cot_here, sems.at[0])
    copy.start()
    if chunks is not None:
        place_weights(chunks, own, got, shard, ids, [(w2_ref, 0, 0, w2_ref.shape[3])])
    out_ref, keep_ref, send_ref, dres_ref, vgrad_ref, acc_ref, dn_ref, n2t_ref, gt_ref = refs
    cols = cols_ref[...]
    res = res_ref[...]
    hat, rstd, normed = norm_cols(res, cols[:, 1:2], cols[:, 4:5])
    n2t_ref[...] = normed.astype(BF16)
    rows_low = normed.T.astype(BF16)
    copy.wait()
    cot = cot_here[...].reshape(-1, cot_here.shape[2])
    cot_t = cot.astype(F32).T
    gt_ref[...] = cot_t.astype(BF16)
    acc_ref[...] = res + cols[:, 5:6]
    dn_ref[...] = jnp.zeros_like(dn_ref)
    tensors, width, units = w2_ref.shape[1], w2_ref.shape[2], w2_ref.shape[3]
    chunk = 256
    parts = units // chunk
    half_rows = width // 2

    def step(i, carry):
        t, off = i // parts, pl.multiple_of((i % parts) * chunk, chunk)
        c = pl.ds(off, chunk)
        up, down = w2_ref[0, t, :, c], w2_ref[1, t, :, c]
        pre = nn(rows_low, up)
        d_hidden = nn(cot, down)
        half, bell = gelu_parts(pre)
        hidden = (pre * half).astype(BF16)
        d_pre = (d_hidden * (half + pre * bell * (1.0 / math.sqrt(2.0 * math.pi)))).astype(BF16)
        acc_ref[...] += nt(down, hidden)
        dn_ref[...] += nt(up, d_pre)
        for ref, which in ((keep_ref, b), (send_ref, 1 - b)):
            rows = pl.ds(pl.multiple_of(which * half_rows, 16), half_rows)
            store_grads(plan, ids, ref, t, c, nn(n2t_ref[rows, :], d_pre).astype(BF16))
            later = pl.ds(pl.multiple_of(units + off, chunk), chunk)
            store_grads(plan, ids, ref, t, later, nn(gt_ref[rows, :], hidden).astype(BF16))
        return carry

    lax.fori_loop(0, tensors * parts, step, 0, unroll=6)
    out_ref[...] = acc_ref[...].T.astype(BF16)
    d_n2 = dn_ref[...]
    d_res = cot_t + norm_cols_back(d_n2, hat, rstd, cols[:, 1:2])
    dres_ref[...] = d_res
    lane = lax.broadcasted_iota(jnp.int32, vgrad_ref.shape, 1)
    total = jnp.zeros(vgrad_ref.shape, F32)
    for j, term in ((1, d_n2 * hat), (3, d_res), (4, d_n2), (5, cot_t)):
        total = total + jnp.where(lane == 64 + j, jnp.sum(term, axis=1, keepdims=True), 0.0)
    vgrad_ref[...] = total


def query_back_kernel(plan, nseq, *refs):
    dres_ref, vgrad_ref, cols_ref = refs[:3]
    w1_ref, hat_ref, rstd_ref, normed_ref, q_ref, k_ref, v_ref, inv_ref, ctx_ref, *pb_refs = refs[3 : 12 + nseq]
    refs = refs[12 + nseq :]
    crop_keep_ref, crop_send_ref, keep_ref, send_ref, dctx_ref, dproj_ref, dattn_ref, vg_ref, crop_ref = refs[:9]
    dp_refs, ds_refs, delta_refs = (refs[9 + i * nseq : 9 + (i + 1) * nseq] for i in range(3))
    ids = place()
    b = ids[0]
    tensors, width = w1_ref.shape[1], w1_ref.shape[2]
    group = width // tensors
    heads_g = group // HD
    heads, slots = pb_refs[0].shape[0], pb_refs[0].shape[1]
    rows = nseq * slots
    d_attn = dres_ref[...].astype(BF16)
    dattn_ref[...] = d_attn
    for t in range(tensors):
        vo = tn(w1_ref[1, t], d_attn).astype(BF16)
        dctx_ref[t * heads_g : (t + 1) * heads_g] = vo[group:].reshape(heads_g, HD, rows)
    dproj_ref[:, 3 * heads_g :] = jnp.zeros((tensors, heads_g, HD, rows), BF16)
    parts = [slice(s * slots, (s + 1) * slots) for s in range(nseq)]
    scale = HD**-0.5

    def d_weights(h, s):
        t, hh = h // heads_g, h % heads_g
        low_ctx = dctx_ref[h, :, parts[s]].astype(F32) * inv_ref[h, 0:1, parts[s]]
        delta = jnp.sum(low_ctx * ctx_ref[t, heads_g + hh, :, parts[s]].astype(F32), axis=0, keepdims=True)
        delta_refs[s][...] = jnp.broadcast_to(delta, (8, slots))
        low_ctx = low_ctx.astype(BF16)
        dp_refs[s][...] = tn(v_ref[h, 0:HD, parts[s]], low_ctx)
        dproj_ref[t, 2 * heads_g + hh, :, parts[s]] = nt(low_ctx, pb_refs[s][h]).astype(BF16)

    def harden(h, s):
        ds_refs[s][...] = (pb_refs[s][h].astype(F32) * (dp_refs[s][...] - delta_refs[s][0:1, :])).astype(BF16)

    def d_inputs(h, s):
        t, hh = h // heads_g, h % heads_g
        d_scores = ds_refs[s][...]
        dproj_ref[t, hh, :, parts[s]] = (nn(k_ref[h, :, parts[s]], d_scores) * scale).astype(BF16)
        dproj_ref[t, heads_g + hh, :, parts[s]] = (nt(q_ref[h, :, parts[s]], d_scores) * scale).astype(BF16)

    def one_head(h, carry):
        for s in range(nseq):
            if s + 1 < nseq:
                d_weights(h, s + 1)
            else:
                d_weights(jnp.minimum(h + 1, heads - 1), 0)
            if s:
                d_inputs(h, s - 1)
            else:
                d_inputs(jnp.maximum(h - 1, 0), nseq - 1)
            harden(h, s)
        return carry

    def some_heads(g, carry):
        for h in range(HEADS_STEP):
            one_head(g * HEADS_STEP + h, carry)
        return carry

    d_weights(0, 0)
    lax.fori_loop(0, heads // HEADS_STEP, some_heads, 0)
    d_inputs(heads - 1, nseq - 1)
    d_normed = jnp.zeros((width, rows), F32)
    for t in range(tensors):
        d_t = dproj_ref[t].reshape(4 * group, rows)
        d_normed += nn(w1_ref[0, t], d_t[: 2 * group]) + nn(w1_ref[1, t], d_t[2 * group :])
    hat = hat_ref[...]
    cols = cols_ref[...]
    crop_ref[...] = dres_ref[...] + norm_cols_back(d_normed, hat, rstd_ref[0:1, :], cols[:, 0:1])
    lane = lax.broadcasted_iota(jnp.int32, vgrad_ref.shape, 1)
    total = vgrad_ref[...]
    for j, term in ((0, d_normed * hat), (2, d_normed)):
        total = total + jnp.where(lane == 64 + j, jnp.sum(term, axis=1, keepdims=True), 0.0)
    vg_ref[...] = total
    half_rows = width // 2
    tile = (3 * group) // 128 * 128
    for ref, which in ((keep_ref, b), (send_ref, 1 - b)):
        part = pl.ds(pl.multiple_of(which * half_rows, 16), half_rows)
        left, right = normed_ref[part, :], dattn_ref[part, :]
        for t in range(tensors):
            d_t = dproj_ref[t].reshape(4 * group, rows)
            grads = nt(left, d_t[: 3 * group + 64])
            outs = nt(right, ctx_ref[t, heads_g:].reshape(group, rows))
            outs = jnp.concatenate([outs, jnp.zeros((half_rows, 64), F32)], axis=1)
            grads = jnp.concatenate([grads[:, :tile], grads[:, tile:] + vg_ref[part, :], outs], axis=1)
            store_grads(plan, ids, ref, t, slice(None), grads.astype(BF16))
    for s in range(nseq):
        part = slice(s * slots, (s + 1) * slots)
        crop_keep_ref[s] = crop_ref[pl.ds(pl.multiple_of(b * half_rows, 16), half_rows), part]
        crop_send_ref[s] = crop_ref[pl.ds(pl.multiple_of((1 - b) * half_rows, 16), half_rows), part].astype(BF16)


def chip_sum_kernel(keep_ref, got_ref, own_ref, *sends):
    total = keep_ref[...].astype(F32) + got_ref[...].astype(F32)
    own_ref[...] = total[0]
    for j, ref in enumerate(sends):
        ref[...] = total[1 + j].astype(BF16)


def half_sum_kernel(keep_ref, got_ref, own_ref, send_ref):
    half = own_ref.shape[0]
    own_ref[...] = keep_ref[:half].astype(F32) + got_ref[:half].astype(F32)
    send_ref[...] = (keep_ref[half:].astype(F32) + got_ref[half:].astype(F32)).astype(BF16)


def x_sum_kernel(own_ref, got_ref, keep_ref, send_ref):
    total = own_ref[...] + got_ref[...].astype(F32)
    keep_ref[...] = total[0]
    send_ref[...] = total[1].astype(BF16)


def near_sum_kernel(*refs):
    mlp, attn, own_ref, sends = refs[:2], refs[2:6], refs[6], refs[7:]
    wide = mlp[0].shape[2]
    for part, cols in ((mlp, slice(0, wide)), (attn, slice(wide, None))):
        total = part[0][...]
        for ref in part[1:]:
            total = total + ref[...].astype(F32)
        own_ref[:, cols] = total[0]
        for k, ref in enumerate(sends):
            ref[:, cols] = total[1 + k].astype(BF16)


def shares_kernel(units, group, *refs):
    own_ref, got, (qkv_ref, out_ref, up_ref, down_ref, gain_ref, bias_ref) = refs[0], refs[1:-6], refs[-6:]
    total = own_ref[...]
    for ref in got:
        total = total + ref[...].astype(F32)
    up_ref[...] = total[:, :units]
    down_ref[...] = total[:, units : 2 * units]
    attn = total[:, 2 * units :]
    for j in range(3):
        qkv_ref[j] = attn[:, j * group : (j + 1) * group]
    tile = 3 * group // 128 * 128
    vec = attn[:, tile : tile + 128]
    share = vec.shape[0]
    vec = jnp.concatenate([vec, jnp.zeros((128 - share, 128), F32)], axis=0).T
    gain_ref[...] = vec[64:66, :share]
    bias_ref[...] = vec[66:70, :share]
    out_ref[...] = attn[:, tile + 128 : tile + 128 + group]


def crop_pair_kernel(keep_ref, got_ref, pair_ref):
    b = lax.axis_index("branch")
    pair_ref[b] = keep_ref[...].astype(BF16)
    pair_ref[1 - b] = got_ref[...]


def crop_kernel(keep_ref, got_ref, far_ref, out_ref):
    b, _, t = place()
    out_ref[t, b] = keep_ref[...]
    out_ref[t, 1 - b] = got_ref[...].astype(F32)
    out_ref[1 - t] = far_ref[...].astype(F32)


def pick_kernel(query_ref, momentum_ref, own_ref, send_ref):
    first = lax.axis_index("branch") == 0
    own_ref[...] = jnp.where(first, momentum_ref[...], query_ref[...])
    send_ref[...] = jnp.where(first, query_ref[...], momentum_ref[...])


def encoded_kernel(own_ref, own_far, got_ref, got_far, out_ref, sems):
    b, _, t = place()
    places = ((own_ref, t, b), (own_far, 1 - t, b), (got_ref, t, 1 - b), (got_far, 1 - t, 1 - b))
    copies = [pltpu.make_async_copy(part, out_ref.at[i, j], sems.at[n]) for n, (part, i, j) in enumerate(places)]
    for copy in copies:
        copy.start()
    for copy in copies:
        copy.wait()


def call(kernel, out_shapes, scratch, args, hbm=0, hbm_outs=0, copies=0, stream=False, limit=24):
    place, hold = pl.BlockSpec(memory_space=pltpu.VMEM), pl.BlockSpec(memory_space=pltpu.HBM)
    inner = args[: len(args) - hbm]
    if stream:
        specs = [pl.BlockSpec(x.shape, lambda i, n=x.ndim: (0,) * n) for x in inner]
    else:
        specs = [place] * len(inner)
    return pl.pallas_call(
        kernel,
        grid=(1,) if stream else (),
        out_shape=[jax.ShapeDtypeStruct(s, d) for s, d in out_shapes],
        in_specs=specs + [hold] * hbm,
        out_specs=[place] * (len(out_shapes) - hbm_outs) + [hold] * hbm_outs,
        scratch_shapes=[pltpu.VMEM(s, d) for s, d in scratch]
        + ([pltpu.SemaphoreType.DMA((copies,))] if copies else []),
        compiler_params=pltpu.CompilerParams(vmem_limit_bytes=limit * 1024 * 1024),
    )(*args)


SPAN = ("dp", "tensor")


def swap_cores(block):
    return lax.ppermute(block, "branch", [(0, 1), (1, 0)])


def exchange(block, dp_mask, t_mask):
    dp, tensors = lax.axis_size("dp"), lax.axis_size("tensor")
    pairs = [
        (i * tensors + t, (i ^ dp_mask) * tensors + (t ^ t_mask)) for i in range(dp) for t in range(tensors)
    ]
    return lax.ppermute(block, SPAN, pairs)


def after(value, *deps):
    return lax.optimization_barrier((value, *deps))[0]


def dp_groups():
    bits = lax.axis_size("dp").bit_length() - 1
    groups, high = [], bits
    while high >= 2:
        high -= 2
        groups.append((high, 4))
    last = (0, 2) if high == 1 else None
    return groups, last


def put(whole, block, index):
    return lax.dynamic_update_slice(whole, block, index)


def gather(block):
    groups, last = dp_groups()
    me, t = lax.axis_index("dp"), lax.axis_index("tensor")
    tensors = lax.axis_size("tensor")
    for number, (shift, size) in enumerate(groups):
        lead, tail = block.shape[:number], block.shape[number:]
        whole = jnp.zeros(lead + (size,) + tail, block.dtype)
        mine = (me >> shift) & (size - 1)
        pieces = [(0, block)] + [(k, exchange(block, k << shift, 0)) for k in range(1, size)]
        for k, piece in pieces:
            whole = put(whole, jnp.expand_dims(piece, number), (0,) * number + (mine ^ k,) + (0,) * len(tail))
        block = whole
    lead, tail = block.shape[: len(groups)], block.shape[len(groups) :]
    size = last[1] if last else 1
    mine = me & (size - 1)
    whole = jnp.zeros((tensors,) + lead + (size,) + tail, block.dtype)
    for k in range(size):
        for u in range(tensors):
            piece = block if k == u == 0 else exchange(block, k, u)
            piece = jnp.expand_dims(jnp.expand_dims(piece, len(lead)), 0)
            whole = put(whole, piece, (t ^ u,) + (0,) * len(lead) + (mine ^ k,) + (0,) * len(tail))
    return whole.reshape((tensors, lax.axis_size("dp")) + tail)


def scatter_sum(block):
    groups, last = dp_groups()
    me, t = lax.axis_index("dp"), lax.axis_index("tensor")
    tensors = lax.axis_size("tensor")
    tail = block.shape[2:]
    size = last[1] if last else 1
    lead = tuple(g[1] for g in groups)
    block = block.reshape((tensors,) + lead + (size,) + tail)
    mine = me & (size - 1)

    def take(k, u):
        start = (t ^ u,) + (0,) * len(lead) + (mine ^ k,) + (0,) * len(tail)
        piece = lax.dynamic_slice(block, start, (1,) + lead + (1,) + tail)
        return piece.reshape(lead + tail)

    total = take(0, 0).astype(F32)
    for k in range(size):
        for u in range(tensors):
            if k or u:
                total = total + exchange(take(k, u), k, u).astype(F32)
    for number in reversed(range(len(groups))):
        shift, size = groups[number]
        mine = (me >> shift) & (size - 1)
        low = total.astype(BF16)

        def part(k, whole=low, number=number, mine=mine):
            return lax.dynamic_index_in_dim(whole, mine ^ k, number, keepdims=False)

        total = part(0, total).astype(F32)
        for k in range(1, size):
            total = total + exchange(part(k), k << shift, 0).astype(F32)
    return total


def stack_peers(block, stage):
    return jnp.stack([block] + [exchange(block, *peer) for peer in stage]), [(0, 0)] + stage


def chunks_of(block, masks, stage):
    pieces = [((0, 0), block)] + [(peer, exchange(block, *peer)) for peer in stage]
    return [
        (piece, [((j,), (m ^ peer[0], u ^ peer[1])) for j, (m, u) in enumerate(masks)]) for peer, piece in pieces
    ]


def gathered(shards, on_query, me, tensors, width, units):
    qkv, out_t, up, down_t, gains, biases = shards
    shard = up.shape[0]
    small = jnp.concatenate([gains, biases], axis=0).astype(BF16)
    vec_rows = put(jnp.zeros((8, width), BF16), small, (0, me * shard))
    half_0 = jnp.concatenate([qkv[0], qkv[1]], axis=1).astype(BF16)
    half_1 = jnp.concatenate([qkv[2], out_t], axis=1).astype(BF16)
    half_0, half_1 = (jnp.concatenate([half, vec_rows], axis=0) for half in (half_0, half_1))
    mlp_0, mlp_1 = up.astype(BF16), down_t.astype(BF16)

    def finish(first, second):
        keep, got = jnp.where(on_query, first, second), swap_cores(jnp.where(on_query, second, first))
        both = []
        for block in (jnp.where(on_query, keep, got), jnp.where(on_query, got, keep)):
            own = gather(block)
            other = swap_cores(own)
            both.append(jnp.stack([jnp.where(on_query, own, other), jnp.where(on_query, other, own)]))
        return both

    def parts_of(whole):
        vec = jnp.sum(whole[0, 0, :, shard:].astype(F32), axis=0)
        return whole[:, :, :, :shard].reshape(2, tensors, width, width), vec

    (wq_1, vec_q), (wm_1, vec_m) = (parts_of(whole) for whole in finish(half_0, half_1))
    wq_2, wm_2 = (whole.reshape(2, tensors, width, units) for whole in finish(mlp_0, mlp_1))
    return [wq_1, vec_q, wm_1, vec_m], [wq_2], [wm_2]


def on_device(
    crops, segment_ids, cotangent, qkv_weight, out_weight, up_weight, down_weight, gain_rows, biases
):
    branch, me, t = lax.axis_index("branch"), lax.axis_index("dp"), lax.axis_index("tensor")
    dp, tensors = lax.axis_size("dp"), lax.axis_size("tensor")
    on_query = branch == 0
    _, sequences, slots, width = crops.shape
    nseq = sequences // (2 * tensors)
    rows = nseq * slots
    shard = qkv_weight.shape[1]
    group = out_weight.shape[1]
    units = up_weight.shape[2]
    heads = tensors * group // HD
    heads_g = group // HD
    share = width // (2 * dp)
    fine = tensors == 2 and dp == 8 and shard % 16 == 0
    near = [(k << 1, 0) for k in range(1, 4)]
    both_ways = [(1, 0), (0, 1), (1, 1)]

    w1_shape, w2_shape = (2, tensors, width, width), (2, tensors, width, units)
    head_block = ((heads, HD, rows), BF16)
    v_block = ((heads, HD + 16, rows), BF16)
    ctx_block = ((tensors, 2 * heads_g, HD, rows), BF16)
    bias_block = ((nseq, slots, slots), F32)
    score_block, pb_block = ((slots, slots), F32), ((heads, slots, slots), BF16)
    col_block, vec_block = ((width, 128), F32), ((128, width), F32)
    crop_block = ((nseq, slots, width), BF16)
    wide_f, wide_b = ((width, rows), F32), ((width, rows), BF16)
    kept = [(w1_shape, BF16), wide_f, ((8, rows), F32), wide_b, head_block, head_block, v_block]
    kept = kept + [((heads, 8, rows), F32), ctx_block] + [pb_block] * nseq
    grads_1, grads_2 = (tensors, width // 2, 4 * group + 128), (tensors, width // 2, 2 * units)
    scatter = None
    if fine:
        grads_1, grads_2 = (4, dp // 2, share, grads_1[2]), (4, dp // 2, share, grads_2[2])
        scatter = (dp, 1)

    def attention(plan, weights, got_crops):
        return call(
            functools.partial(attention_kernel, plan, shard),
            [wide_f, wide_f, col_block] + kept,
            [score_block] * nseq
            + [pb_block] * nseq
            + [head_block, head_block, v_block, ctx_block, bias_block, crop_block]
            + [(w1_shape, BF16) if plan else vec_block],
            (got_crops, segment_ids, *weights, crops[0]),
            hbm=1,
            copies=1,
        )

    def query_mlp(plan, weights, res, cols):
        return call(
            functools.partial(query_mlp_kernel, scatter, plan, shard),
            [((rows, width), BF16), (grads_2, BF16), (grads_2, BF16), wide_f, col_block],
            [wide_f, wide_f, wide_b, wide_b] + ([(w2_shape, BF16)] if plan else []) + [crop_block],
            (res, cols, *weights, cotangent),
            hbm=1,
            copies=1,
        )

    def query_back(d_res, vgrad, cols, saved):
        return call(
            functools.partial(query_back_kernel, scatter, nseq),
            [((nseq, width // 2, slots), F32), ((nseq, width // 2, slots), BF16), (grads_1, BF16), (grads_1, BF16)],
            [head_block, ((tensors, 4 * heads_g, HD, rows), BF16), wide_b, col_block, wide_f]
            + [score_block] * nseq
            + [((slots, slots), BF16)] * nseq
            + [((8, slots), F32)] * nseq,
            (d_res, vgrad, cols, *saved),
        )

    def momentum_mlp(plan, weights, res_m, cols, out_q):
        return call(
            functools.partial(momentum_mlp_kernel, plan, shard),
            [((rows, width), BF16)] * 3,
            [wide_f] + ([(w2_shape, BF16)] if plan else []),
            (res_m, cols, out_q, *weights),
        )

    shards = (
        qkv_weight[0].transpose(1, 0, 2),
        out_weight[0].T,
        up_weight[0],
        down_weight[0].T,
        gain_rows[0],
        biases[0],
    )
    other = nseq * (2 * t + 1 - branch)
    send_crops = lax.dynamic_slice(crops[0], (other, 0, 0), (nseq, slots, width)).reshape(rows, width)

    if fine:
        block = ((shard, width + 128 + units), BF16)
        keep, send = call(
            pack_kernel, [block] * 2, [(x.shape, F32) for x in shards], shards, hbm=6, copies=6, limit=56
        )
        block_1, block_2 = call(
            functools.partial(split_kernel, width),
            [((shard, 2 * width + 128), BF16), ((shard, 2 * units), BF16)],
            [block],
            (swap_cores(send), keep),
            hbm=1,
            copies=1,
        )
        masks = [(0, 0)] + near
        plan = [[((j,), (m ^ n, u)) for j, (m, _) in enumerate(masks)] for n, u in [(0, 0)] + both_ways]
        got_crops = swap_cores(send_crops)
        far_1 = [exchange(block_1, *peer) for peer in near]
        stack_1, got_crops = after((jnp.stack([block_1, *far_1]), got_crops))
        own_1 = [stack_1] + [exchange(stack_1, *peer) for peer in both_ways]
        got_1 = [swap_cores(x) for x in own_1]
        parts = after([block_2] + [exchange(block_2, *peer) for peer in near], own_1[1], own_1[2])
        stack_q, stack_a, stack_b = (
            jnp.stack([x[..., start : start + wide] for x in parts])
            for start, wide in ((0, units), (units, units // 2), (units + units // 2, units // 2))
        )
        by_y = [[((v, j), (m ^ n, v)) for v in range(2) for j, (m, _) in enumerate(masks)] for n in range(2)]
        by_x = [[((n, j), (m ^ n, v)) for n in range(2) for j, (m, _) in enumerate(masks)] for v in range(2)]
        own_q = [stack_q] + [exchange(stack_q, *peer) for peer in both_ways]
        got_a, got_b = exchange(stack_a, 0, 1), exchange(stack_b, 1, 0)
        res, res_m, cols, *saved = attention(plan, own_1 + got_1, after(got_crops, stack_q, stack_a, stack_b))
        own_q, got_a, got_b, res, res_m = after((own_q, got_a, got_b, res, res_m))
        got_q = [swap_cores(x) for x in own_q]
        stack_a, stack_b = jnp.stack([stack_a, got_a]), jnp.stack([stack_b, got_b])
        own_m = [stack_a, exchange(stack_a, 1, 0), stack_b, exchange(stack_b, 0, 1)]
        out_q, keep_g2, send_g2, d_res, vgrad = query_mlp(plan, own_q + got_q, res, cols)
        own_m, out_q, keep_g2, send_g2, d_res, vgrad = after((own_m, out_q, keep_g2, send_g2, d_res, vgrad))
        got_m = [swap_cores(x) for x in own_m]

        part = (2, dp // 2, share, 2 * units)
        mlp_own, mlp_send = call(half_sum_kernel, [(part, F32), (part, BF16)], [], (keep_g2, swap_cores(send_g2)))
        mlp_got = exchange(mlp_send, 1, 0)
        far_q = exchange(out_q, 0, 1)
        res_m = after(res_m, mlp_own)
        out_m, out_own, out_send = momentum_mlp((by_y, by_x), own_m + got_m, res_m, cols, out_q)
        far_q, out_m, out_send = after((far_q, out_m, out_send))
        far_m = exchange(out_m, 0, 1)
        crop_keep, crop_send, keep_g1, send_g1 = query_back(after(d_res, out_m), vgrad, cols, saved)
        mlp_got, far_m, crop_send, send_g1 = after((mlp_got, far_m, crop_send, send_g1))
        part = (dp // 2, share, 2 * units)
        mlp_own, mlp_send = call(x_sum_kernel, [(part, F32), (part, BF16)], [], (mlp_own, mlp_got))
        mlp_got = exchange(mlp_send, 0, 1)
        part = (dp // 2, share, grads_1[3])
        attn_own, *attn_sends = call(
            chip_sum_kernel, [(part, F32)] + [(part, BF16)] * 3, [], (keep_g1, swap_cores(send_g1))
        )
        attn_got = [exchange(x, *peer) for x, peer in zip(attn_sends, [(0, 1), (1, 0), (1, 1)])]
        half = (nseq, width // 2, slots)
        crop_got = swap_cores(crop_send)
        (pair,) = call(crop_pair_kernel, [((2, *half), BF16)], [], (crop_keep, crop_got))
        attn_got, mlp_got, pair = after((attn_got, mlp_got, pair))
        crop_far = exchange(pair, 0, 1)
        wide = 2 * units + grads_1[3]
        own, *sends = call(
            near_sum_kernel,
            [((share, wide), F32)] + [((share, wide), BF16)] * 3,
            [],
            (mlp_own, mlp_got, attn_own, *attn_got),
        )
        got = [exchange(x, *peer) for x, peer in zip(sends, near)]
        (crop_grad,) = call(
            crop_kernel, [((tensors, 2, *half), F32)], [], (crop_keep, crop_got, crop_far)
        )
        got, crop_grad = after((got, crop_grad))
        qkv_grad, out_grad, up_grad, down_grad, gain_grad, bias_grad = call(
            functools.partial(shares_kernel, units, group),
            [
                ((3, share, group), F32),
                ((share, group), F32),
                ((share, units), F32),
                ((share, units), F32),
                ((2, share), F32),
                ((4, share), F32),
            ],
            [],
            (own, *got),
        )
        qkv_grad, out_grad, down_grad = qkv_grad.transpose(1, 0, 2), out_grad.T, down_grad.T
        crop_grad = crop_grad.reshape(sequences, width // 2, slots).transpose(0, 2, 1)
        far_own, far_send = call(pick_kernel, [((rows, width), BF16)] * 2, [], (far_q, far_m))
        (encoded,) = call(
            encoded_kernel,
            [((tensors, 2, rows, width), BF16)],
            [],
            (out_own, far_own, swap_cores(out_send), swap_cores(far_send)),
            hbm=4,
            hbm_outs=1,
            copies=4,
        )
        encoded = encoded.reshape(1, sequences, slots, width)
        return (encoded, crop_grad, qkv_grad, out_grad, up_grad, down_grad, gain_grad, bias_grad)

    weights_1, weights_2, weights_4 = gathered(shards, on_query, me, tensors, width, units)
    got_crops = swap_cores(send_crops)
    res, res_m, cols, *saved = attention(None, weights_1, got_crops)
    out_q, keep_g2, send_g2, d_res, vgrad = query_mlp(None, weights_2, res, cols)
    crop_keep, crop_send, keep_g1, send_g1 = query_back(d_res, vgrad, cols, saved)
    _, out_own, out_send = momentum_mlp(None, weights_4, res_m, cols, out_q)

    def shares(keep, send):
        both = (keep.astype(F32) + swap_cores(send).astype(F32)).astype(BF16)
        return scatter_sum(both.reshape(tensors, dp, share, both.shape[-1]))

    mlp_share, attn_share = shares(keep_g2, send_g2), shares(keep_g1, send_g1)
    qkv_grad = attn_share[:, : 3 * group].reshape(share, 3, group)
    vec_grad = attn_share[:, 3 * group : 3 * group + 6].T
    out_grad = attn_share[:, 3 * group + 64 : 4 * group + 64].T
    up_grad, down_grad = mlp_share[:, :units], mlp_share[:, units:].T

    mine = (2, nseq, width // 2, slots)
    pair = jnp.zeros(mine, F32)
    pair = put(pair, crop_keep[None], (branch, 0, 0, 0))
    pair = put(pair, swap_cores(crop_send).astype(F32)[None], (1 - branch, 0, 0, 0))
    far = exchange(pair.astype(BF16), 0, 1)
    crop_grad = jnp.zeros((tensors,) + mine, F32)
    crop_grad = put(crop_grad, pair[None], (t, 0, 0, 0, 0))
    crop_grad = put(crop_grad, far.astype(F32)[None], (1 - t, 0, 0, 0, 0))
    crop_grad = crop_grad.reshape(sequences, width // 2, slots).transpose(0, 2, 1)

    pair = jnp.zeros((2, rows, width), BF16)
    pair = put(put(pair, out_own[None], (branch, 0, 0)), swap_cores(out_send)[None], (1 - branch, 0, 0))
    encoded = jnp.zeros((tensors, 2, rows, width), BF16)
    encoded = put(encoded, pair[None], (t, 0, 0, 0))
    encoded = put(encoded, exchange(pair, 0, 1)[None], (1 - t, 0, 0, 0))
    encoded = encoded.reshape(1, sequences, slots, width)

    return (encoded, crop_grad, qkv_grad, out_grad, up_grad, down_grad, vec_grad[:2], vec_grad[2:])


def solution(mesh):
    placed = (
        P("branch", "dp", None, None),
        P(None, "dp", None),
        P("dp", None, None),
        P("branch", "dp", None, "tensor"),
        P("branch", "tensor", "dp"),
        P("branch", "dp", "tensor"),
        P("branch", "tensor", "dp"),
        P("branch", None, "dp"),
        P("branch", None, "dp"),
    )
    return jax.shard_map(
        on_device,
        mesh=mesh,
        in_specs=placed,
        out_specs=(
            P("branch", "dp", None, None),
            P("dp", None, "branch"),
            P(("branch", "dp"), None, "tensor"),
            P("tensor", ("branch", "dp")),
            P(("branch", "dp"), "tensor"),
            P("tensor", ("branch", "dp")),
            P(None, ("branch", "dp")),
            P(None, ("branch", "dp")),
        ),
        check_vma=False,
    )
```

```python
import functools
import math

import jax
import jax.numpy as jnp
from jax import lax
from jax.experimental import pallas as pl
from jax.experimental.pallas import tpu as pltpu
from jax.sharding import PartitionSpec as P

HD = 32
HEADS_STEP = 4
EPSILON = 1e-06
MASKED_SCORE = -1e30
LOG2E = 1.4426950408889634
BF16 = jnp.bfloat16
F32 = jnp.float32
PACE = 3600000


def nn(left, right):
    return lax.dot_general(left, right, (((1,), (0,)), ((), ())), preferred_element_type=F32)


def nt(left, right):
    return lax.dot_general(left, right, (((1,), (1,)), ((), ())), preferred_element_type=F32)


def tn(left, right):
    return lax.dot_general(left, right, (((0,), (0,)), ((), ())), preferred_element_type=F32)


def place():
    return lax.axis_index("branch"), lax.axis_index("dp"), lax.axis_index("tensor")


def gelu_parts(v):
    a = jnp.abs(v)
    t = 1.0 / (1.0 + (0.3275911 / math.sqrt(2.0)) * a)
    bell = jnp.exp2(v * v * (-0.5 * LOG2E))
    poly = t * (
        0.5 * 0.254829592
        + t * (0.5 * -0.284496736 + t * (0.5 * 1.421413741 + t * (0.5 * -1.453152027 + t * (0.5 * 1.061405429))))
    )
    tail = poly * bell
    return jnp.where(v < 0, tail, 1.0 - tail), bell


def norm_cols(values, gain, shift):
    centred = values - jnp.mean(values, axis=0, keepdims=True)
    spread = jnp.mean(centred * centred, axis=0, keepdims=True)
    rstd = lax.rsqrt(spread + EPSILON)
    hat = centred * rstd
    return hat, rstd, hat * gain + shift


def norm_cols_back(upstream, hat, rstd, gain):
    t = upstream * gain
    return rstd * (t - jnp.mean(t, axis=0, keepdims=True) - hat * jnp.mean(t * hat, axis=0, keepdims=True))


def columns_of(query_ref, momentum_ref, scratch):
    scratch[...] = jnp.zeros_like(scratch)
    scratch[0:8, :] = query_ref[...]
    scratch[8:16, :] = momentum_ref[...]
    return scratch[...].T


def place_columns(plan, chunk_refs, shard, me, cols_ref):
    for ref, spots in zip(chunk_refs, plan):
        for index, (mask, u) in spots:
            if u == 0:
                rows = pl.ds(pl.multiple_of((me ^ mask) * shard, 16), shard)
                vec = ref[index + (slice(ref.shape[-2] - 16, None), slice(None))].astype(F32)
                cols_ref[rows, :] = jnp.concatenate([vec, jnp.zeros((112, 128), F32)], axis=0).T[:shard, :]


def place_tiles(plan, own_refs, got_refs, shard, ids, targets):
    b, me, t = ids
    for half, refs in ((b, own_refs), (1 - b, got_refs)):
        for ref, spots in zip(refs, plan):
            for index, (mask, u) in spots:
                rows = pl.ds(pl.multiple_of((me ^ mask) * shard, 16), shard)
                for i, target in enumerate(targets):
                    tiles = target.shape[3] // 128
                    for j in range(tiles):
                        start = (i * tiles + j) * shard
                        tile = ref[index + (slice(start, start + shard), slice(None))]
                        target[half, t ^ u, rows, j * 128 : (j + 1) * 128] = tile


def place_weights(plan, own_refs, got_refs, shard, ids, targets):
    b, me, t = ids
    for half, refs in ((b, own_refs), (1 - b, got_refs)):
        for ref, spots in zip(refs, plan):
            for index, (mask, u) in spots:
                rows = pl.ds(pl.multiple_of((me ^ mask) * shard, 16), shard)
                for target, to, start, wide in targets:
                    block = ref[index + (slice(0, shard), slice(start, start + wide))]
                    target[half, t ^ u, rows, to : to + wide] = block


def attend(x, segs, w1_ref, cols, q_ref, k_ref, v_ref, bias_ref, ctx_ref, pb_refs, inv_ref, score_refs, keep=None):
    tensors, width = w1_ref.shape[1], w1_ref.shape[2]
    group = width // tensors
    heads_g = group // HD
    nseq, slots = len(segs), segs[0].shape[1]
    x_t = x.astype(F32).T
    hat, rstd, normed = norm_cols(x_t, cols[:, 0:1], cols[:, 2:3])
    normed_low = normed.astype(BF16)
    if keep is not None:
        keep(hat, rstd, normed_low)
    rows = x_t.shape[1]
    for t in range(tensors):
        qk = tn(w1_ref[0, t], normed_low).astype(BF16)
        q_ref[t * heads_g : (t + 1) * heads_g] = qk[:group].reshape(heads_g, HD, rows)
        k_ref[t * heads_g : (t + 1) * heads_g] = qk[group:].reshape(heads_g, HD, rows)
        vo = tn(w1_ref[1, t], normed_low).astype(BF16)
        v_ref[t * heads_g : (t + 1) * heads_g, 0:HD] = vo[:group].reshape(heads_g, HD, rows)
    v_ref[:, HD:, :] = jnp.ones((v_ref.shape[0], v_ref.shape[1] - HD, rows), BF16)
    for s in range(nseq):
        across = jnp.broadcast_to(segs[s].astype(F32), (slots, slots))
        bias_ref[s] = jnp.where(across == across.T, 0.0, MASKED_SCORE)
    heads = tensors * heads_g
    parts = [slice(s * slots, (s + 1) * slots) for s in range(nseq)]
    ctx_ref[:, :heads_g] = jnp.zeros((tensors, heads_g, HD, rows), BF16)

    def score(h, s):
        score_refs[s][...] = tn(k_ref[h, :, parts[s]], q_ref[h, :, parts[s]])

    def soften(h, s):
        scores = score_refs[s][...] + bias_ref[s]
        top = jnp.max(scores, axis=0, keepdims=True)
        pb_refs[s][h] = jnp.exp2((scores - top) * (HD**-0.5 * LOG2E)).astype(BF16)

    def blend(h, s):
        both = nn(v_ref[h, :, parts[s]], pb_refs[s][h])
        inv = 1.0 / both[HD : HD + 1]
        if inv_ref is not None:
            inv_ref[h, :, parts[s]] = jnp.broadcast_to(inv, (8, slots))
        ctx_ref[h // heads_g, heads_g + h % heads_g, :, parts[s]] = (both[:HD] * inv).astype(BF16)

    def one_head(h, carry):
        for s in range(nseq):
            if s + 1 < nseq:
                score(h, s + 1)
            else:
                score(jnp.minimum(h + 1, heads - 1), 0)
            if s:
                blend(h, s - 1)
            else:
                blend(jnp.maximum(h - 1, 0), nseq - 1)
            soften(h, s)
        return carry

    score(0, 0)

    def some_heads(g, carry):
        for h in range(HEADS_STEP):
            one_head(g * HEADS_STEP + h, carry)
        return carry

    lax.fori_loop(0, heads // HEADS_STEP, some_heads, 0)
    blend(heads - 1, nseq - 1)
    attn = sum(nn(w1_ref[1, t], ctx_ref[t].reshape(width, rows)) for t in range(tensors))
    return x_t, attn


def pack_kernel(*refs):
    far, keep_ref, send_ref, near, sems = refs[:6], refs[6], refs[7], refs[8:14], refs[14]
    copies = [pltpu.make_async_copy(there, here, sems.at[i]) for i, (there, here) in enumerate(zip(far, near))]
    for copy in copies:
        copy.start()
    qkv_ref, out_ref, up_ref, down_ref, gain_ref, bias_ref = near
    first = lax.axis_index("branch") == 0
    shard, width = up_ref.shape[0], 2 * out_ref.shape[1]
    for copy in copies:
        copy.wait()
    vec = jnp.concatenate([gain_ref[...], bias_ref[...], jnp.zeros((2, shard), F32)], axis=0)
    vec = jnp.concatenate([vec, jnp.zeros((8, 128 - shard), F32)], axis=1)
    none = jnp.zeros((8, 128), F32)
    vec = [jnp.where(first, vec, none), jnp.where(first, none, vec), jnp.zeros((shard - 16, 128), F32)]
    vec = jnp.concatenate(vec, axis=0).astype(BF16)
    half_0 = jnp.concatenate([qkv_ref[0], qkv_ref[1]], axis=1).astype(BF16)
    half_1 = jnp.concatenate([qkv_ref[2], out_ref[...]], axis=1).astype(BF16)
    up, down = up_ref[...].astype(BF16), down_ref[...].astype(BF16)
    for ref, is_first in ((keep_ref, first), (send_ref, jnp.logical_not(first))):
        ref[:, :width] = jnp.where(is_first, half_0, half_1)
        ref[:, width : width + 128] = vec
        ref[:, width + 128 :] = jnp.where(is_first, up, down)


def split_kernel(width, got_ref, far_ref, first_ref, second_ref, keep_ref, sems):
    copy = pltpu.make_async_copy(far_ref, keep_ref, sems.at[0])
    copy.start()
    first = lax.axis_index("branch") == 0
    got = got_ref[...]
    copy.wait()
    keep = keep_ref[...]
    query, momentum = jnp.where(first, keep, got), jnp.where(first, got, keep)
    units = second_ref.shape[1] // 2
    shard, tiles = query.shape[0], width // 128
    for i, half in enumerate((query, momentum)):
        for j in range(tiles):
            first_ref[pl.ds((i * tiles + j) * shard, shard), :] = half[:, j * 128 : (j + 1) * 128]
    first_ref[2 * tiles * shard :, :] = (keep + got)[:16, width : width + 128]
    second_ref[:, :units] = query[:, width + 128 :]
    second_ref[:, units:] = momentum[:, width + 128 :]


def attention_kernel(plan, shard, *refs):
    got_crops, seg_ref, refs = refs[0], refs[1], refs[2:]
    ids = place()
    slots = seg_ref.shape[2]
    nseq = got_crops.shape[0] // slots
    if plan is None:
        w1_given, vec_q, w1_m, vec_m = refs[:4]
        refs = refs[4:]
    else:
        own, got = refs[: len(plan)], refs[len(plan) : 2 * len(plan)]
        refs = refs[2 * len(plan) :]
    crops_ref, res_ref, res_m_ref, cols_ref, refs = refs[0], refs[1], refs[2], refs[3], refs[4:]
    w1_ref, hat_ref, rstd_ref, normed_ref, q_ref, k_ref, v_ref, inv_ref, ctx_ref, *pb_refs = refs[: 9 + nseq]
    refs = refs[9 + nseq :]
    score_refs, pb_m, refs = refs[:nseq], refs[nseq : 2 * nseq], refs[2 * nseq :]
    q_m, k_m, v_m, ctx_m, bias_ref, mine_ref, spare, sems = refs
    first = nseq * (2 * ids[2] + ids[0])
    copy = pltpu.make_async_copy(crops_ref.at[pl.ds(first, nseq)], mine_ref, sems.at[0])
    copy.start()
    if plan is None:
        w1_ref[...] = w1_given[...]
        cols_ref[...] = columns_of(vec_q, vec_m, spare)
    else:
        w1_m = spare
        place_columns(plan, own, shard, ids[1], cols_ref)
        place_tiles(plan, own, got, shard, ids, (w1_ref, w1_m))
    cols = cols_ref[...]

    def keep(hat, rstd, normed):
        hat_ref[...] = hat
        rstd_ref[...] = jnp.broadcast_to(rstd, rstd_ref.shape)
        normed_ref[...] = normed

    copy.wait()

    def rows_of(encoder):
        mine = mine_ref[...].reshape(got_crops.shape)
        segs = [seg_ref[1 - encoder, pl.ds(first + s, 1), :] for s in range(nseq)]
        return jnp.where(ids[0] == encoder, got_crops[...], mine), segs

    x_t, attn = attend(
        *rows_of(0), w1_ref, cols, q_ref, k_ref, v_ref, bias_ref, ctx_ref, pb_refs, inv_ref, score_refs, keep
    )
    res_ref[...] = x_t + attn + cols[:, 3:4]
    cols = cols[:, 8:]
    x_t, attn = attend(*rows_of(1), w1_m, cols, q_m, k_m, v_m, bias_ref, ctx_m, pb_m, None, score_refs)
    res_m_ref[...] = x_t + attn + cols[:, 3:4]


def momentum_mlp_kernel(plan, shard, *refs):
    res_ref, cols_ref, query_ref, refs = refs[0], refs[1], refs[2], refs[3:]
    ids = place()
    cols = cols_ref[...][:, 8:]
    if plan is None:
        w2_ref, out_ref, own_ref, send_ref, acc_ref = refs
    else:
        count = sum(len(part) for part in plan)
        own, got = refs[:count], refs[count : 2 * count]
        out_ref, own_ref, send_ref, acc_ref, w2_ref = refs[2 * count :]
        at, wide = 0, own[0].shape[-1]
        for i, part in enumerate(plan):
            targets = [(w2_ref, i * wide, 0, wide)]
            place_weights(part, own[at : at + len(part)], got[at : at + len(part)], shard, ids, targets)
            at += len(part)
    res = res_ref[...]
    _, _, normed = norm_cols(res, cols[:, 1:2], cols[:, 4:5])
    rows_low = normed.T.astype(BF16)
    acc_ref[...] = res + cols[:, 5:6]
    tensors, units = w2_ref.shape[1], w2_ref.shape[3]
    chunk = 768
    parts = units // chunk

    def step(i, carry):
        t, c = i // parts, pl.ds(pl.multiple_of((i % parts) * chunk, chunk), chunk)
        pre = nn(rows_low, w2_ref[0, t, :, c])
        half, _ = gelu_parts(pre)
        acc_ref[...] += nt(w2_ref[1, t, :, c], (pre * half).astype(BF16))
        return carry

    lax.fori_loop(0, tensors * parts, step, 0, unroll=2)
    momentum, query = acc_ref[...].T.astype(BF16), query_ref[...]
    first = ids[0] == 0
    out_ref[...] = momentum
    own_ref[...] = jnp.where(first, momentum, query)
    send_ref[...] = jnp.where(first, query, momentum)


def store_grads(plan, ids, ref, t, cols, values):
    if plan is None:
        ref[t, :, cols] = values
        return
    dp, final = plan
    me, mine = ids[1], ids[2]
    share = values.shape[0] // dp
    size = final.bit_length()
    for i in range(dp):
        mask = me ^ i
        ref[(mask & final) * 2 + (mine ^ t), mask >> (size), :, cols] = values[i * share : (i + 1) * share]


def query_mlp_kernel(plan, chunks, shard, *refs):
    res_ref, cols_ref = refs[:2]
    cot_here, sems, refs = refs[-2], refs[-1], refs[2:-2]
    ids = place()
    b = ids[0]
    if chunks is None:
        w2_ref, cot_ref, refs = refs[0], refs[1], refs[2:]
    else:
        own, got = refs[: len(chunks)], refs[len(chunks) : 2 * len(chunks)]
        cot_ref, w2_ref, refs = refs[2 * len(chunks)], refs[-1], refs[2 * len(chunks) + 1 : -1]
    nseq = cot_here.shape[0]
    copy = pltpu.make_async_copy(cot_ref.at[pl.ds(nseq * (2 * ids[2] + b), nseq)], cot_here, sems.at[0])
    copy.start()
    if chunks is not None:
        place_weights(chunks, own, got, shard, ids, [(w2_ref, 0, 0, w2_ref.shape[3])])
    out_ref, keep_ref, send_ref, dres_ref, vgrad_ref, acc_ref, dn_ref, n2t_ref, gt_ref = refs
    cols = cols_ref[...]
    res = res_ref[...]
    hat, rstd, normed = norm_cols(res, cols[:, 1:2], cols[:, 4:5])
    n2t_ref[...] = normed.astype(BF16)
    rows_low = normed.T.astype(BF16)
    copy.wait()
    cot = cot_here[...].reshape(-1, cot_here.shape[2])
    cot_t = cot.astype(F32).T
    gt_ref[...] = cot_t.astype(BF16)
    acc_ref[...] = res + cols[:, 5:6]
    dn_ref[...] = jnp.zeros_like(dn_ref)
    tensors, width, units = w2_ref.shape[1], w2_ref.shape[2], w2_ref.shape[3]
    chunk = 768
    parts = units // chunk
    half_rows = width // 2

    def step(i, carry):
        t, off = i // parts, pl.multiple_of((i % parts) * chunk, chunk)
        c = pl.ds(off, chunk)
        up, down = w2_ref[0, t, :, c], w2_ref[1, t, :, c]
        pre = nn(rows_low, up)
        d_hidden = nn(cot, down)
        half, bell = gelu_parts(pre)
        hidden = (pre * half).astype(BF16)
        d_pre = (d_hidden * (half + pre * bell * (1.0 / math.sqrt(2.0 * math.pi)))).astype(BF16)
        acc_ref[...] += nt(down, hidden)
        dn_ref[...] += nt(up, d_pre)
        for ref, which in ((keep_ref, b), (send_ref, 1 - b)):
            rows = pl.ds(pl.multiple_of(which * half_rows, 16), half_rows)
            store_grads(plan, ids, ref, t, c, nn(n2t_ref[rows, :], d_pre).astype(BF16))
            later = pl.ds(pl.multiple_of(units + off, chunk), chunk)
            store_grads(plan, ids, ref, t, later, nn(gt_ref[rows, :], hidden).astype(BF16))
        return carry

    lax.fori_loop(0, tensors * parts, step, 0, unroll=2)
    out_ref[...] = acc_ref[...].T.astype(BF16)
    d_n2 = dn_ref[...]
    d_res = cot_t + norm_cols_back(d_n2, hat, rstd, cols[:, 1:2])
    dres_ref[...] = d_res
    lane = lax.broadcasted_iota(jnp.int32, vgrad_ref.shape, 1)
    total = jnp.zeros(vgrad_ref.shape, F32)
    for j, term in ((1, d_n2 * hat), (3, d_res), (4, d_n2), (5, cot_t)):
        total = total + jnp.where(lane == 64 + j, jnp.sum(term, axis=1, keepdims=True), 0.0)
    vgrad_ref[...] = total


def query_back_kernel(plan, nseq, *refs):
    dres_ref, vgrad_ref, cols_ref = refs[:3]
    w1_ref, hat_ref, rstd_ref, normed_ref, q_ref, k_ref, v_ref, inv_ref, ctx_ref, *pb_refs = refs[3 : 12 + nseq]
    refs = refs[12 + nseq :]
    crop_keep_ref, crop_send_ref, keep_ref, send_ref, dctx_ref, dproj_ref, dattn_ref, vg_ref, crop_ref = refs[:9]
    dp_refs, ds_refs, delta_refs = (refs[9 + i * nseq : 9 + (i + 1) * nseq] for i in range(3))
    ids = place()
    b = ids[0]
    tensors, width = w1_ref.shape[1], w1_ref.shape[2]
    group = width // tensors
    heads_g = group // HD
    heads, slots = pb_refs[0].shape[0], pb_refs[0].shape[1]
    rows = nseq * slots
    d_attn = dres_ref[...].astype(BF16)
    dattn_ref[...] = d_attn
    for t in range(tensors):
        vo = tn(w1_ref[1, t], d_attn).astype(BF16)
        dctx_ref[t * heads_g : (t + 1) * heads_g] = vo[group:].reshape(heads_g, HD, rows)
    dproj_ref[:, 3 * heads_g :] = jnp.zeros((tensors, heads_g, HD, rows), BF16)
    parts = [slice(s * slots, (s + 1) * slots) for s in range(nseq)]
    scale = HD**-0.5

    def d_weights(h, s):
        t, hh = h // heads_g, h % heads_g
        low_ctx = dctx_ref[h, :, parts[s]].astype(F32) * inv_ref[h, 0:1, parts[s]]
        delta = jnp.sum(low_ctx * ctx_ref[t, heads_g + hh, :, parts[s]].astype(F32), axis=0, keepdims=True)
        delta_refs[s][...] = jnp.broadcast_to(delta, (8, slots))
        low_ctx = low_ctx.astype(BF16)
        dp_refs[s][...] = tn(v_ref[h, 0:HD, parts[s]], low_ctx)
        dproj_ref[t, 2 * heads_g + hh, :, parts[s]] = nt(low_ctx, pb_refs[s][h]).astype(BF16)

    def harden(h, s):
        ds_refs[s][...] = (pb_refs[s][h].astype(F32) * (dp_refs[s][...] - delta_refs[s][0:1, :])).astype(BF16)

    def d_inputs(h, s):
        t, hh = h // heads_g, h % heads_g
        d_scores = ds_refs[s][...]
        dproj_ref[t, hh, :, parts[s]] = (nn(k_ref[h, :, parts[s]], d_scores) * scale).astype(BF16)
        dproj_ref[t, heads_g + hh, :, parts[s]] = (nt(q_ref[h, :, parts[s]], d_scores) * scale).astype(BF16)

    def one_head(h, carry):
        for s in range(nseq):
            if s + 1 < nseq:
                d_weights(h, s + 1)
            else:
                d_weights(jnp.minimum(h + 1, heads - 1), 0)
            if s:
                d_inputs(h, s - 1)
            else:
                d_inputs(jnp.maximum(h - 1, 0), nseq - 1)
            harden(h, s)
        return carry

    def some_heads(g, carry):
        for h in range(HEADS_STEP):
            one_head(g * HEADS_STEP + h, carry)
        return carry

    d_weights(0, 0)
    lax.fori_loop(0, heads // HEADS_STEP, some_heads, 0)
    d_inputs(heads - 1, nseq - 1)
    d_normed = jnp.zeros((width, rows), F32)
    for t in range(tensors):
        d_t = dproj_ref[t].reshape(4 * group, rows)
        d_normed += nn(w1_ref[0, t], d_t[: 2 * group]) + nn(w1_ref[1, t], d_t[2 * group :])
    hat = hat_ref[...]
    cols = cols_ref[...]
    crop_ref[...] = dres_ref[...] + norm_cols_back(d_normed, hat, rstd_ref[0:1, :], cols[:, 0:1])
    lane = lax.broadcasted_iota(jnp.int32, vgrad_ref.shape, 1)
    total = vgrad_ref[...]
    for j, term in ((0, d_normed * hat), (2, d_normed)):
        total = total + jnp.where(lane == 64 + j, jnp.sum(term, axis=1, keepdims=True), 0.0)
    vg_ref[...] = total
    half_rows = width // 2
    tile = (3 * group) // 128 * 128
    for ref, which in ((keep_ref, b), (send_ref, 1 - b)):
        part = pl.ds(pl.multiple_of(which * half_rows, 16), half_rows)
        left, right = normed_ref[part, :], dattn_ref[part, :]
        for t in range(tensors):
            d_t = dproj_ref[t].reshape(4 * group, rows)
            grads = nt(left, d_t[: 3 * group + 64])
            outs = nt(right, ctx_ref[t, heads_g:].reshape(group, rows))
            outs = jnp.concatenate([outs, jnp.zeros((half_rows, 64), F32)], axis=1)
            grads = jnp.concatenate([grads[:, :tile], grads[:, tile:] + vg_ref[part, :], outs], axis=1)
            store_grads(plan, ids, ref, t, slice(None), grads.astype(BF16))
    for s in range(nseq):
        part = slice(s * slots, (s + 1) * slots)
        crop_keep_ref[s] = crop_ref[pl.ds(pl.multiple_of(b * half_rows, 16), half_rows), part]
        crop_send_ref[s] = crop_ref[pl.ds(pl.multiple_of((1 - b) * half_rows, 16), half_rows), part].astype(BF16)


def chip_sum_kernel(keep_ref, got_ref, own_ref, *sends):
    total = keep_ref[...].astype(F32) + got_ref[...].astype(F32)
    own_ref[...] = total[0]
    for j, ref in enumerate(sends):
        ref[...] = total[1 + j].astype(BF16)


def half_sum_kernel(keep_ref, got_ref, own_ref, send_ref):
    half = own_ref.shape[0]
    own_ref[...] = keep_ref[:half].astype(F32) + got_ref[:half].astype(F32)
    send_ref[...] = (keep_ref[half:].astype(F32) + got_ref[half:].astype(F32)).astype(BF16)


def x_sum_kernel(own_ref, got_ref, keep_ref, send_ref):
    total = own_ref[...] + got_ref[...].astype(F32)
    keep_ref[...] = total[0]
    send_ref[...] = total[1].astype(BF16)


def near_sum_kernel(*refs):
    mlp, attn, own_ref, sends = refs[:2], refs[2:6], refs[6], refs[7:]
    wide = mlp[0].shape[2]
    for part, cols in ((mlp, slice(0, wide)), (attn, slice(wide, None))):
        total = part[0][...]
        for ref in part[1:]:
            total = total + ref[...].astype(F32)
        own_ref[:, cols] = total[0]
        for k, ref in enumerate(sends):
            ref[:, cols] = total[1 + k].astype(BF16)


def shares_kernel(units, group, *refs):
    own_ref, got, (qkv_ref, out_ref, up_ref, down_ref, gain_ref, bias_ref) = refs[0], refs[1:-6], refs[-6:]
    total = own_ref[...]
    for ref in got:
        total = total + ref[...].astype(F32)
    up_ref[...] = total[:, :units]
    down_ref[...] = total[:, units : 2 * units]
    attn = total[:, 2 * units :]
    for j in range(3):
        qkv_ref[j] = attn[:, j * group : (j + 1) * group]
    tile = 3 * group // 128 * 128
    vec = attn[:, tile : tile + 128]
    share = vec.shape[0]
    vec = jnp.concatenate([vec, jnp.zeros((128 - share, 128), F32)], axis=0).T
    gain_ref[...] = vec[64:66, :share]
    bias_ref[...] = vec[66:70, :share]
    out_ref[...] = attn[:, tile + 128 : tile + 128 + group]


def crop_pair_kernel(keep_ref, got_ref, pair_ref):
    b = lax.axis_index("branch")
    pair_ref[b] = keep_ref[...].astype(BF16)
    pair_ref[1 - b] = got_ref[...]


def crop_kernel(keep_ref, got_ref, far_ref, out_ref):
    b, _, t = place()
    out_ref[t, b] = keep_ref[...]
    out_ref[t, 1 - b] = got_ref[...].astype(F32)
    out_ref[1 - t] = far_ref[...].astype(F32)


def pick_kernel(query_ref, momentum_ref, own_ref, send_ref):
    first = lax.axis_index("branch") == 0
    own_ref[...] = jnp.where(first, momentum_ref[...], query_ref[...])
    send_ref[...] = jnp.where(first, query_ref[...], momentum_ref[...])


def encoded_kernel(own_ref, own_far, got_ref, got_far, out_ref, sems):
    b, _, t = place()
    places = ((own_ref, t, b), (own_far, 1 - t, b), (got_ref, t, 1 - b), (got_far, 1 - t, 1 - b))
    copies = [pltpu.make_async_copy(part, out_ref.at[i, j], sems.at[n]) for n, (part, i, j) in enumerate(places)]
    for copy in copies:
        copy.start()
    for copy in copies:
        copy.wait()


def call(kernel, out_shapes, scratch, args, hbm=0, hbm_outs=0, copies=0, stream=False, limit=24):
    place, hold = pl.BlockSpec(memory_space=pltpu.VMEM), pl.BlockSpec(memory_space=pltpu.HBM)
    inner = args[: len(args) - hbm]
    if stream:
        specs = [pl.BlockSpec(x.shape, lambda i, n=x.ndim: (0,) * n) for x in inner]
    else:
        specs = [place] * len(inner)
    return pl.pallas_call(
        kernel,
        grid=(1,) if stream else (),
        out_shape=[jax.ShapeDtypeStruct(s, d) for s, d in out_shapes],
        in_specs=specs + [hold] * hbm,
        out_specs=[place] * (len(out_shapes) - hbm_outs) + [hold] * hbm_outs,
        scratch_shapes=[pltpu.VMEM(s, d) for s, d in scratch]
        + ([pltpu.SemaphoreType.DMA((copies,))] if copies else []),
        compiler_params=pltpu.CompilerParams(vmem_limit_bytes=limit * 1024 * 1024),
    )(*args)


SPAN = ("dp", "tensor")


def swap_cores(block):
    return lax.ppermute(block, "branch", [(0, 1), (1, 0)])


def exchange(block, dp_mask, t_mask):
    dp, tensors = lax.axis_size("dp"), lax.axis_size("tensor")
    pairs = [
        (i * tensors + t, (i ^ dp_mask) * tensors + (t ^ t_mask)) for i in range(dp) for t in range(tensors)
    ]
    return lax.ppermute(block, SPAN, pairs)


def after(value, *deps):
    return lax.optimization_barrier((value, *deps))[0]


def dp_groups():
    bits = lax.axis_size("dp").bit_length() - 1
    groups, high = [], bits
    while high >= 2:
        high -= 2
        groups.append((high, 4))
    last = (0, 2) if high == 1 else None
    return groups, last


def put(whole, block, index):
    return lax.dynamic_update_slice(whole, block, index)


def gather(block):
    groups, last = dp_groups()
    me, t = lax.axis_index("dp"), lax.axis_index("tensor")
    tensors = lax.axis_size("tensor")
    for number, (shift, size) in enumerate(groups):
        lead, tail = block.shape[:number], block.shape[number:]
        whole = jnp.zeros(lead + (size,) + tail, block.dtype)
        mine = (me >> shift) & (size - 1)
        pieces = [(0, block)] + [(k, exchange(block, k << shift, 0)) for k in range(1, size)]
        for k, piece in pieces:
            whole = put(whole, jnp.expand_dims(piece, number), (0,) * number + (mine ^ k,) + (0,) * len(tail))
        block = whole
    lead, tail = block.shape[: len(groups)], block.shape[len(groups) :]
    size = last[1] if last else 1
    mine = me & (size - 1)
    whole = jnp.zeros((tensors,) + lead + (size,) + tail, block.dtype)
    for k in range(size):
        for u in range(tensors):
            piece = block if k == u == 0 else exchange(block, k, u)
            piece = jnp.expand_dims(jnp.expand_dims(piece, len(lead)), 0)
            whole = put(whole, piece, (t ^ u,) + (0,) * len(lead) + (mine ^ k,) + (0,) * len(tail))
    return whole.reshape((tensors, lax.axis_size("dp")) + tail)


def scatter_sum(block):
    groups, last = dp_groups()
    me, t = lax.axis_index("dp"), lax.axis_index("tensor")
    tensors = lax.axis_size("tensor")
    tail = block.shape[2:]
    size = last[1] if last else 1
    lead = tuple(g[1] for g in groups)
    block = block.reshape((tensors,) + lead + (size,) + tail)
    mine = me & (size - 1)

    def take(k, u):
        start = (t ^ u,) + (0,) * len(lead) + (mine ^ k,) + (0,) * len(tail)
        piece = lax.dynamic_slice(block, start, (1,) + lead + (1,) + tail)
        return piece.reshape(lead + tail)

    total = take(0, 0).astype(F32)
    for k in range(size):
        for u in range(tensors):
            if k or u:
                total = total + exchange(take(k, u), k, u).astype(F32)
    for number in reversed(range(len(groups))):
        shift, size = groups[number]
        mine = (me >> shift) & (size - 1)
        low = total.astype(BF16)

        def part(k, whole=low, number=number, mine=mine):
            return lax.dynamic_index_in_dim(whole, mine ^ k, number, keepdims=False)

        total = part(0, total).astype(F32)
        for k in range(1, size):
            total = total + exchange(part(k), k << shift, 0).astype(F32)
    return total


def stack_peers(block, stage):
    return jnp.stack([block] + [exchange(block, *peer) for peer in stage]), [(0, 0)] + stage


def chunks_of(block, masks, stage):
    pieces = [((0, 0), block)] + [(peer, exchange(block, *peer)) for peer in stage]
    return [
        (piece, [((j,), (m ^ peer[0], u ^ peer[1])) for j, (m, u) in enumerate(masks)]) for peer, piece in pieces
    ]


def gathered(shards, on_query, me, tensors, width, units):
    qkv, out_t, up, down_t, gains, biases = shards
    shard = up.shape[0]
    small = jnp.concatenate([gains, biases], axis=0).astype(BF16)
    vec_rows = put(jnp.zeros((8, width), BF16), small, (0, me * shard))
    half_0 = jnp.concatenate([qkv[0], qkv[1]], axis=1).astype(BF16)
    half_1 = jnp.concatenate([qkv[2], out_t], axis=1).astype(BF16)
    half_0, half_1 = (jnp.concatenate([half, vec_rows], axis=0) for half in (half_0, half_1))
    mlp_0, mlp_1 = up.astype(BF16), down_t.astype(BF16)

    def finish(first, second):
        keep, got = jnp.where(on_query, first, second), swap_cores(jnp.where(on_query, second, first))
        both = []
        for block in (jnp.where(on_query, keep, got), jnp.where(on_query, got, keep)):
            own = gather(block)
            other = swap_cores(own)
            both.append(jnp.stack([jnp.where(on_query, own, other), jnp.where(on_query, other, own)]))
        return both

    def parts_of(whole):
        vec = jnp.sum(whole[0, 0, :, shard:].astype(F32), axis=0)
        return whole[:, :, :, :shard].reshape(2, tensors, width, width), vec

    (wq_1, vec_q), (wm_1, vec_m) = (parts_of(whole) for whole in finish(half_0, half_1))
    wq_2, wm_2 = (whole.reshape(2, tensors, width, units) for whole in finish(mlp_0, mlp_1))
    return [wq_1, vec_q, wm_1, vec_m], [wq_2], [wm_2]


def on_device(
    crops, segment_ids, cotangent, qkv_weight, out_weight, up_weight, down_weight, gain_rows, biases
):
    branch, me, t = lax.axis_index("branch"), lax.axis_index("dp"), lax.axis_index("tensor")
    dp, tensors = lax.axis_size("dp"), lax.axis_size("tensor")
    on_query = branch == 0
    _, sequences, slots, width = crops.shape
    nseq = sequences // (2 * tensors)
    rows = nseq * slots
    shard = qkv_weight.shape[1]
    group = out_weight.shape[1]
    units = up_weight.shape[2]
    heads = tensors * group // HD
    heads_g = group // HD
    share = width // (2 * dp)
    fine = tensors == 2 and dp == 8 and shard % 16 == 0
    near = [(k << 1, 0) for k in range(1, 4)]
    both_ways = [(1, 0), (0, 1), (1, 1)]

    w1_shape, w2_shape = (2, tensors, width, width), (2, tensors, width, units)
    head_block = ((heads, HD, rows), BF16)
    v_block = ((heads, HD + 16, rows), BF16)
    ctx_block = ((tensors, 2 * heads_g, HD, rows), BF16)
    bias_block = ((nseq, slots, slots), F32)
    score_block, pb_block = ((slots, slots), F32), ((heads, slots, slots), BF16)
    col_block, vec_block = ((width, 128), F32), ((128, width), F32)
    crop_block = ((nseq, slots, width), BF16)
    wide_f, wide_b = ((width, rows), F32), ((width, rows), BF16)
    kept = [(w1_shape, BF16), wide_f, ((8, rows), F32), wide_b, head_block, head_block, v_block]
    kept = kept + [((heads, 8, rows), F32), ctx_block] + [pb_block] * nseq
    grads_1, grads_2 = (tensors, width // 2, 4 * group + 128), (tensors, width // 2, 2 * units)
    scatter = None
    if fine:
        grads_1, grads_2 = (4, dp // 2, share, grads_1[2]), (4, dp // 2, share, grads_2[2])
        scatter = (dp, 1)

    def attention(plan, weights, got_crops):
        return call(
            functools.partial(attention_kernel, plan, shard),
            [wide_f, wide_f, col_block] + kept,
            [score_block] * nseq
            + [pb_block] * nseq
            + [head_block, head_block, v_block, ctx_block, bias_block, crop_block]
            + [(w1_shape, BF16) if plan else vec_block],
            (got_crops, segment_ids, *weights, crops[0]),
            hbm=1,
            copies=1,
        )

    def query_mlp(plan, weights, res, cols):
        return call(
            functools.partial(query_mlp_kernel, scatter, plan, shard),
            [((rows, width), BF16), (grads_2, BF16), (grads_2, BF16), wide_f, col_block],
            [wide_f, wide_f, wide_b, wide_b] + ([(w2_shape, BF16)] if plan else []) + [crop_block],
            (res, cols, *weights, cotangent),
            hbm=1,
            copies=1,
        )

    def query_back(d_res, vgrad, cols, saved):
        return call(
            functools.partial(query_back_kernel, scatter, nseq),
            [((nseq, width // 2, slots), F32), ((nseq, width // 2, slots), BF16), (grads_1, BF16), (grads_1, BF16)],
            [head_block, ((tensors, 4 * heads_g, HD, rows), BF16), wide_b, col_block, wide_f]
            + [score_block] * nseq
            + [((slots, slots), BF16)] * nseq
            + [((8, slots), F32)] * nseq,
            (d_res, vgrad, cols, *saved),
        )

    def momentum_mlp(plan, weights, res_m, cols, out_q):
        return call(
            functools.partial(momentum_mlp_kernel, plan, shard),
            [((rows, width), BF16)] * 3,
            [wide_f] + ([(w2_shape, BF16)] if plan else []),
            (res_m, cols, out_q, *weights),
        )

    shards = (
        qkv_weight[0].transpose(1, 0, 2),
        out_weight[0].T,
        up_weight[0],
        down_weight[0].T,
        gain_rows[0],
        biases[0],
    )
    def send_crops(*deps):
        other = nseq * (2 * t + 1 - branch)
        return lax.dynamic_slice(after(crops, *deps)[0], (other, 0, 0), (nseq, slots, width)).reshape(rows, width)

    if fine:
        block = ((shard, width + 128 + units), BF16)
        keep, send = call(
            pack_kernel, [block] * 2, [(x.shape, F32) for x in shards], shards, hbm=6, copies=6, limit=56
        )
        block_1, block_2 = call(
            functools.partial(split_kernel, width),
            [((2 * (width // 128) * shard + 16, 128), BF16), ((shard, 2 * units), BF16)],
            [block],
            (swap_cores(send), keep),
            hbm=1,
            copies=1,
        )
        masks = [(0, 0)] + near
        plan = [[((j,), (m ^ n, u)) for j, (m, _) in enumerate(masks)] for n, u in [(0, 0)] + both_ways]
        far_1 = [exchange(block_1, *peer) for peer in near]
        got_crops = swap_cores(send_crops(far_1[0]))
        stack_1 = jnp.stack([block_1, *far_1])
        own_1 = [stack_1] + [exchange(stack_1, *peer) for peer in both_ways]
        got_1 = [swap_cores(x) for x in own_1]
        parts = after([block_2] + [exchange(block_2, *peer) for peer in near], own_1[2], own_1[3])
        stack_q, stack_a, stack_b = (
            jnp.stack([x[..., start : start + wide] for x in parts])
            for start, wide in ((0, units), (units, units // 2), (units + units // 2, units // 2))
        )
        by_y = [[((v, j), (m ^ n, v)) for v in range(2) for j, (m, _) in enumerate(masks)] for n in range(2)]
        by_x = [[((n, j), (m ^ n, v)) for n in range(2) for j, (m, _) in enumerate(masks)] for v in range(2)]
        own_q = [stack_q] + [exchange(stack_q, *peer) for peer in both_ways]
        got_a, got_b = exchange(stack_a, 0, 1), exchange(stack_b, 1, 0)
        res, res_m, cols, *saved = attention(plan, own_1 + got_1, after(got_crops, stack_q, stack_a, stack_b))
        own_q, got_a, got_b, res, res_m = after((own_q, got_a, got_b, res, res_m))
        got_q = [swap_cores(x) for x in own_q]
        stack_a, stack_b = jnp.stack([stack_a, got_a]), jnp.stack([stack_b, got_b])
        own_m = [stack_a, exchange(stack_a, 1, 0), stack_b, exchange(stack_b, 0, 1)]
        out_q, keep_g2, send_g2, d_res, vgrad = query_mlp(plan, own_q + got_q, res, cols)
        own_m, out_q, keep_g2, send_g2, d_res, vgrad = after((own_m, out_q, keep_g2, send_g2, d_res, vgrad))
        got_m = [swap_cores(x) for x in own_m]

        part = (2, dp // 2, share, 2 * units)
        mlp_own, mlp_send = call(half_sum_kernel, [(part, F32), (part, BF16)], [], (keep_g2, swap_cores(send_g2)))
        mlp_got = exchange(mlp_send, 1, 0)
        far_q = exchange(out_q, 0, 1)
        res_m = after(res_m, mlp_own)
        out_m, out_own, out_send = momentum_mlp((by_y, by_x), own_m + got_m, res_m, cols, out_q)
        far_q, out_m, out_send = after((far_q, out_m, out_send))
        far_m = exchange(out_m, 0, 1)
        crop_keep, crop_send, keep_g1, send_g1 = query_back(after(d_res, out_m), vgrad, cols, saved)
        mlp_got, far_m, crop_send, send_g1 = after((mlp_got, far_m, crop_send, send_g1))
        part = (dp // 2, share, 2 * units)
        mlp_own, mlp_send = call(x_sum_kernel, [(part, F32), (part, BF16)], [], (mlp_own, mlp_got))
        mlp_got = exchange(mlp_send, 0, 1)
        part = (dp // 2, share, grads_1[3])
        attn_own, *attn_sends = call(
            chip_sum_kernel, [(part, F32)] + [(part, BF16)] * 3, [], (keep_g1, swap_cores(send_g1))
        )
        attn_got = [exchange(x, *peer) for x, peer in zip(attn_sends, [(0, 1), (1, 0), (1, 1)])]
        half = (nseq, width // 2, slots)
        crop_got = swap_cores(crop_send)
        (pair,) = call(crop_pair_kernel, [((2, *half), BF16)], [], (crop_keep, crop_got))
        attn_got, mlp_got, pair = after((attn_got, mlp_got, pair))
        crop_far = exchange(pair, 0, 1)
        wide = 2 * units + grads_1[3]
        own, *sends = call(
            near_sum_kernel,
            [((share, wide), F32)] + [((share, wide), BF16)] * 3,
            [],
            (mlp_own, mlp_got, attn_own, *attn_got),
        )
        got = [exchange(x, *peer) for x, peer in zip(sends, near)]
        (crop_grad,) = call(
            crop_kernel, [((tensors, 2, *half), F32)], [], (crop_keep, crop_got, crop_far)
        )
        got, crop_grad = after((got, crop_grad))
        qkv_grad, out_grad, up_grad, down_grad, gain_grad, bias_grad = call(
            functools.partial(shares_kernel, units, group),
            [
                ((3, share, group), F32),
                ((share, group), F32),
                ((share, units), F32),
                ((share, units), F32),
                ((2, share), F32),
                ((4, share), F32),
            ],
            [],
            (own, *got),
        )
        qkv_grad, out_grad, down_grad = qkv_grad.transpose(1, 0, 2), out_grad.T, down_grad.T
        crop_grad = crop_grad.reshape(sequences, width // 2, slots).transpose(0, 2, 1)
        far_own, far_send = call(pick_kernel, [((rows, width), BF16)] * 2, [], (far_q, far_m))
        (encoded,) = call(
            encoded_kernel,
            [((tensors, 2, rows, width), BF16)],
            [],
            (out_own, far_own, swap_cores(out_send), swap_cores(far_send)),
            hbm=4,
            hbm_outs=1,
            copies=4,
        )
        encoded = encoded.reshape(1, sequences, slots, width)
        return (encoded, crop_grad, qkv_grad, out_grad, up_grad, down_grad, gain_grad, bias_grad)

    weights_1, weights_2, weights_4 = gathered(shards, on_query, me, tensors, width, units)
    got_crops = swap_cores(send_crops())
    res, res_m, cols, *saved = attention(None, weights_1, got_crops)
    out_q, keep_g2, send_g2, d_res, vgrad = query_mlp(None, weights_2, res, cols)
    crop_keep, crop_send, keep_g1, send_g1 = query_back(d_res, vgrad, cols, saved)
    _, out_own, out_send = momentum_mlp(None, weights_4, res_m, cols, out_q)

    def shares(keep, send):
        both = (keep.astype(F32) + swap_cores(send).astype(F32)).astype(BF16)
        return scatter_sum(both.reshape(tensors, dp, share, both.shape[-1]))

    mlp_share, attn_share = shares(keep_g2, send_g2), shares(keep_g1, send_g1)
    qkv_grad = attn_share[:, : 3 * group].reshape(share, 3, group)
    vec_grad = attn_share[:, 3 * group : 3 * group + 6].T
    out_grad = attn_share[:, 3 * group + 64 : 4 * group + 64].T
    up_grad, down_grad = mlp_share[:, :units], mlp_share[:, units:].T

    mine = (2, nseq, width // 2, slots)
    pair = jnp.zeros(mine, F32)
    pair = put(pair, crop_keep[None], (branch, 0, 0, 0))
    pair = put(pair, swap_cores(crop_send).astype(F32)[None], (1 - branch, 0, 0, 0))
    far = exchange(pair.astype(BF16), 0, 1)
    crop_grad = jnp.zeros((tensors,) + mine, F32)
    crop_grad = put(crop_grad, pair[None], (t, 0, 0, 0, 0))
    crop_grad = put(crop_grad, far.astype(F32)[None], (1 - t, 0, 0, 0, 0))
    crop_grad = crop_grad.reshape(sequences, width // 2, slots).transpose(0, 2, 1)

    pair = jnp.zeros((2, rows, width), BF16)
    pair = put(put(pair, out_own[None], (branch, 0, 0)), swap_cores(out_send)[None], (1 - branch, 0, 0))
    encoded = jnp.zeros((tensors, 2, rows, width), BF16)
    encoded = put(encoded, pair[None], (t, 0, 0, 0))
    encoded = put(encoded, exchange(pair, 0, 1)[None], (1 - t, 0, 0, 0))
    encoded = encoded.reshape(1, sequences, slots, width)

    return (encoded, crop_grad, qkv_grad, out_grad, up_grad, down_grad, vec_grad[:2], vec_grad[2:])


def solution(mesh):
    placed = (
        P("branch", "dp", None, None),
        P(None, "dp", None),
        P("dp", None, None),
        P("branch", "dp", None, "tensor"),
        P("branch", "tensor", "dp"),
        P("branch", "dp", "tensor"),
        P("branch", "tensor", "dp"),
        P("branch", None, "dp"),
        P("branch", None, "dp"),
    )
    return jax.shard_map(
        on_device,
        mesh=mesh,
        in_specs=placed,
        out_specs=(
            P("branch", "dp", None, None),
            P("dp", None, "branch"),
            P(("branch", "dp"), None, "tensor"),
            P("tensor", ("branch", "dp")),
            P(("branch", "dp"), "tensor"),
            P("tensor", ("branch", "dp")),
            P(None, ("branch", "dp")),
            P(None, ("branch", "dp")),
        ),
        check_vma=False,
    )
```
